32 devices in a mesh: gx: 4 (over y, core), gy: 8 (over z, x).
Axes of the slice: x: 2, y: 2, z: 4, core: 2. Of those that a mesh axis runs over, the one named last changes fastest.
Arguments:
- tracers: float32 [2016, 2, 20, 1024], P(('gx', 'gy')), may hold values from -6 to 6
- diffusion: float32 [20], replicated, may hold values from 0.03 to 0.24
- layer_weight: float32 [2, 20], replicated, may hold values from -2 to 2
- surface_term: float32 [1280, 1792], P('gy', 'gx'), may hold values from 0.05 to 2
- clinic_blocks: int32 [2016], P(('gx', 'gy')), may hold values from 0 to 2239, as said below
- halo_source: int32 [2016, 4], P(('gx', 'gy')), may hold values from 0 to 8064, as said below
Outputs:
- tracers_next: float32 [2016, 2, 20, 1024], P(('gx', 'gy'))
- pressure: float32 [2016, 1024], P(('gx', 'gy'))
The draws below stay inside these ranges and needn't reach their ends.
Inputs may be any that keep to these rules, and one draw needn't show every extreme that they name: `clinic_blocks`: each entry is a grid block, each block at most once; blocks that no entry names are land. Region (a, b) holds blocks bx in [a 14, (a + 1) * 14) and by in [b * 5, (b + 1) * 5). The slots of the device at mesh index (i, j), d = i * 8 + j, are slots d * 63 to (d + 1) * 63 - 1, and their blocks lie in region (i, j) or region (i, (j + 1) mod 8); those in region (i, (j + 1) mod 8) are the device's last slots, at most 22 of them, and some device has exactly 22. halo_source[s, t] is 4 s' + t' for the ocean block beside side t of slot s's block (t' the side facing it; periodic along the columns), or 8064 where that block is land or beyond the first or last row. Slot s' lies on the device of slot s or on one of the eight devices around it in the mesh (periodic along gx and gy); where its gx index differs, t' is 0 or 1.
All inputs are finite; a program needn't handle non-finite values.
Results may differ from the reference program's by a relative error of at most 0.0001.
Values sent between devices are 32-bit elements; how exact they have to be, the bound alone decides.
No kernel may reach another device: no remote copies, remote signals or barrier semaphores. Data moves between devices by JAX's collectives and lax.ppermute only.
A program may use at most 320 MiB of HBM per device.

```python
import math
import jax
import jax.numpy as jnp
from jax import lax

BLOCK = 32
LEVELS = 20
TRACER = 2
REG_X = 14
REG_Y = 5
ITERS = 3
LAND = 7
HEAD = 15
BLK_DEV = 63
NBLK = 2016
NBX = 56
NBY = 40
NX = 1792
NY = 1280
STRIP = 1280
N_GX = 4
N_GY = 8


def geometry(key):
    region_size = REG_X * REG_Y
    excess = jax.random.randint(jax.random.fold_in(key, 1), (N_GX, N_GY), 0, LAND + 1)
    excess = excess.at[0, 0].set(LAND)
    land_count = LAND + jnp.roll(excess, -1, axis=1) - excess
    score_ints = jax.random.randint(jax.random.fold_in(key, 2), (N_GX, N_GY, REG_X), 0, 1 << 20) * REG_X + jnp.arange(REG_X)
    order_cols = jnp.argsort(score_ints, axis=-1, stable=True)
    col_ranks = jnp.argsort(order_cols, axis=-1, stable=True)
    land_cols = col_ranks < land_count[:, :, None]
    row_ids = jnp.arange(REG_Y)
    is_land = (row_ids[None, None, :, None] == 2) & land_cols[:, :, None, :]
    ocean = jnp.where(is_land, 0, 1).reshape(N_GX, N_GY, region_size).astype(jnp.int32)
    rank_in = jnp.cumsum(ocean, axis=-1) - 1
    positions = jnp.arange(region_size, dtype=jnp.int32)
    matches = (rank_in[..., None, :] == positions[:, None]) & (ocean[..., None, :] == 1)
    by_rank = jnp.sum(jnp.where(matches, positions, 0), axis=-1)
    head_count = HEAD + excess
    tail_count = BLK_DEV - HEAD - jnp.roll(excess, -1, axis=1)
    slot_ids = jnp.arange(BLK_DEV, dtype=jnp.int32)
    in_tail = slot_ids[None, None, :] < tail_count[:, :, None]
    rank_tail = jnp.clip(head_count[:, :, None] + slot_ids, 0, region_size - 1)
    rank_head = jnp.clip(slot_ids - tail_count[:, :, None], 0, region_size - 1)
    pos_tail = jnp.take_along_axis(by_rank, rank_tail, axis=-1)
    pos_head = jnp.take_along_axis(jnp.roll(by_rank, -1, axis=1), rank_head, axis=-1)
    place_pos = jnp.where(in_tail, pos_tail, pos_head)
    column_ids = jnp.arange(N_GX, dtype=jnp.int32)[:, None, None]
    row_reg = jnp.arange(N_GY, dtype=jnp.int32)[None, :, None]
    region_row = jnp.where(in_tail, row_reg, (row_reg + 1) % N_GY)
    block_col = column_ids * REG_X + place_pos % REG_X
    block_row = region_row * REG_Y + place_pos // REG_X
    blocks = (block_row * NBX + block_col).reshape(NBLK).astype(jnp.int32)
    inverse = jnp.full((NBX * NBY,), -1, jnp.int32).at[blocks].set(jnp.arange(NBLK, dtype=jnp.int32))
    col_of = blocks % NBX
    row_of = blocks // NBX
    west_id = row_of * NBX + (col_of - 1) % NBX
    east_id = row_of * NBX + (col_of + 1) % NBX
    south_id = jnp.clip(row_of - 1, 0, NBY - 1) * NBX + col_of
    north_id = jnp.clip(row_of + 1, 0, NBY - 1) * NBX + col_of
    neighbours = jnp.stack([west_id, east_id, south_id, north_id], axis=1)
    inside_grid = jnp.stack([row_of >= 0, row_of >= 0, row_of > 0, row_of < NBY - 1], axis=1)
    source = inverse[neighbours]
    facing = jnp.array([1, 0, 3, 2], dtype=jnp.int32)
    halo = jnp.where(inside_grid & (source >= 0), source * 4 + facing[None, :], 4 * NBLK)
    return (blocks, halo.astype(jnp.int32))


def draw_clinic_blocks(key, part):
    return geometry(key)[0]


def draw_halo_source(key, part):
    return geometry(key)[1]


def draw_tracers(key, part):
    shape = (NBLK, TRACER, LEVELS, BLOCK * BLOCK)
    slot_scale = 0.5 + jnp.arange(NBLK, dtype=jnp.float32) / NBLK
    key = jax.random.fold_in(key, 11)
    values = jnp.clip(jax.random.normal(key, shape, jnp.float32), -4.0, 4.0)
    return (values * slot_scale[:, None, None, None]).astype(jnp.float32)


def steps_of(own_key, extent, split, smallest, top_value):
    gain, own = 1.0, jax.random.fold_in(own_key, 6)
    for axis_at, parts in split:
        steps = jnp.exp(jax.random.uniform(jax.random.fold_in(own, axis_at), (parts,), jnp.float32, smallest / len(split), top_value / len(split)))
        gain = gain * jnp.repeat(steps, extent[axis_at] // parts).reshape([-1 if axis == axis_at else 1 for axis in range(len(extent))])
    return gain


def noise(own_key, extent, spread, most, kind=jnp.bfloat16):
    values = spread * jax.random.normal(own_key, extent, jnp.float32)
    return jnp.clip(values, min=-most, max=most).astype(kind)


def setup_inputs(seed: int = 0) -> dict:
    key_list = jax.random.split(jax.random.key(seed), 7)
    tracers = draw_tracers(jax.random.fold_in(key_list[6], 71), 0)
    diffusion = jnp.clip(jnp.exp(jax.random.uniform(key_list[1], (LEVELS,), jnp.float32, math.log(0.03), math.log(0.24))), 0.03, 0.24)
    layer_weight = noise(key_list[2], (TRACER, LEVELS), 0.5, 2.0, jnp.float32)
    surface_term = jnp.clip(jnp.exp(math.log(2.0) - 3.6888794 * jax.random.uniform(key_list[3], (NY, NX), jnp.float32) ** steps_of(key_list[3], (NY, NX), ((0, 8), (1, 4)), -0.2, 0.2)), 0.05, 2.0)
    clinic_blocks = draw_clinic_blocks(jax.random.fold_in(key_list[6], 71), 0)
    halo_source = draw_halo_source(jax.random.fold_in(key_list[6], 71), 0)
    return {"tracers": tracers, "diffusion": diffusion, "layer_weight": layer_weight, "surface_term": surface_term, "clinic_blocks": clinic_blocks, "halo_source": halo_source}


def edge_strips(tracer_grid):
    west_edge = tracer_grid[..., :, 0]
    east_edge = tracer_grid[..., :, -1]
    south_edge = tracer_grid[..., 0, :]
    north_edge = tracer_grid[..., -1, :]
    stacked = jnp.stack([west_edge, east_edge, south_edge, north_edge], axis=1)
    return stacked.reshape(tracer_grid.shape[0] * 4, -1)


def diffuse(tracer_grid, halo_rows, opened, diffusion):
    slot_count = tracer_grid.shape[0]
    halo_grid = halo_rows.reshape(slot_count, 4, TRACER, LEVELS, BLOCK)
    open_gate = opened.reshape(slot_count, 4, 1, 1, 1)
    inner_x = tracer_grid[..., :, :-1] - tracer_grid[..., :, 1:]
    inner_y = tracer_grid[..., :-1, :] - tracer_grid[..., 1:, :]
    west_term = (halo_grid[:, 0] - tracer_grid[..., :, 0]) * open_gate[:, 0]
    east_term = (halo_grid[:, 1] - tracer_grid[..., :, -1]) * open_gate[:, 1]
    south_term = (halo_grid[:, 2] - tracer_grid[..., 0, :]) * open_gate[:, 2]
    north_term = (halo_grid[:, 3] - tracer_grid[..., -1, :]) * open_gate[:, 3]
    from_west = jnp.concatenate([west_term[..., None], inner_x], axis=-1)
    from_east = jnp.concatenate([-inner_x, east_term[..., None]], axis=-1)
    from_south = jnp.concatenate([south_term[..., None, :], inner_y], axis=-2)
    from_north = jnp.concatenate([-inner_y, north_term[..., None, :]], axis=-2)
    laplace = from_west + from_east + from_south + from_north
    return tracer_grid + diffusion[None, None, :, None, None] * laplace


def to_blocks(values):
    return values.reshape(NBY, BLOCK, NBX, BLOCK).transpose(0, 2, 1, 3).reshape(NBY * NBX, BLOCK * BLOCK)


def from_blocks(blocks):
    return blocks.reshape(NBY, NBX, BLOCK, BLOCK).transpose(0, 2, 1, 3).reshape(NY, NX)


def operate(values, mask_field, diagonal):
    padded = jnp.pad(values, ((1, 1), (0, 0)))
    padded = jnp.concatenate([padded[:, -1:], padded, padded[:, :1]], axis=1)
    edge_sum = padded[2:, 1:-1] + padded[:-2, 1:-1] + padded[1:-1, 2:] + padded[1:-1, :-2]
    corners = padded[2:, 2:] + padded[2:, :-2] + padded[:-2, 2:] + padded[:-2, :-2]
    return mask_field * (diagonal * values - edge_sum - 0.5 * corners)


def reference(tracers, diffusion, layer_weight, surface_term, clinic_blocks, halo_source):
    slot_count = tracers.shape[0]
    groups = N_GX * N_GY
    tracer_grid = tracers.reshape(slot_count, TRACER, LEVELS, BLOCK, BLOCK)
    strips = edge_strips(tracer_grid)
    padded_strips = jnp.concatenate([strips, jnp.zeros((1, strips.shape[1]), jnp.float32)], axis=0)
    source = halo_source.reshape(-1).astype(jnp.int32)
    halo_rows = jnp.take(padded_strips, source, axis=0)
    opened = jnp.where(source < 4 * slot_count, 1.0, 0.0).astype(jnp.float32)

    def one_group(pieces):
        group_grid, group_halo, group_open = pieces
        updated = diffuse(group_grid, group_halo, group_open, diffusion)
        summed = jnp.sum(updated * layer_weight[None, :, :, None, None], axis=(1, 2))
        return updated, summed

    grouped = (tracer_grid.reshape(groups, BLK_DEV, TRACER, LEVELS, BLOCK, BLOCK),
               halo_rows.reshape(groups, BLK_DEV * 4, STRIP),
               opened.reshape(groups, BLK_DEV * 4))
    updated, summed = lax.map(one_group, grouped)
    tracers_next = updated.reshape(tracers.shape)
    forcing = summed.reshape(slot_count, BLOCK * BLOCK)
    forcing_blocks = jnp.zeros((NBY * NBX, BLOCK * BLOCK), jnp.float32).at[clinic_blocks].set(forcing)
    ocean_blocks = jnp.zeros((NBY * NBX, BLOCK * BLOCK), jnp.float32).at[clinic_blocks].set(1.0)
    rhs_field = from_blocks(forcing_blocks)
    mask_field = from_blocks(ocean_blocks)
    diagonal = 6.0 + surface_term
    solution = jnp.zeros_like(rhs_field)
    residual = rhs_field
    precond = residual / diagonal
    direction = precond
    norm_now = jnp.sum(residual * precond)
    for iteration in range(ITERS):
        applied = operate(direction, mask_field, diagonal)
        step_length = norm_now / jnp.sum(direction * applied)
        solution = solution + step_length * direction
        if iteration + 1 < ITERS:
            residual = residual - step_length * applied
            precond = residual / diagonal
            norm_next = jnp.sum(residual * precond)
            direction = precond + (norm_next / norm_now) * direction
            norm_now = norm_next
    pressure = jnp.take(to_blocks(solution), clinic_blocks, axis=0)
    return tracers_next, pressure
```

```python
import jax
import jax.numpy as jnp
from jax import lax
from jax.experimental import pallas as pl
from jax.experimental.pallas import tpu as pltpu
from jax.sharding import PartitionSpec as P

BLOCK = 32
LEVELS = 20
TRACER = 2
REG_X = 14
REG_Y = 5
REGION = REG_X * REG_Y
MOVED = 22
LANES = 128
TILE = 8
ROWS = 16
HALF = LEVELS // 2
STEP_SLOTS = 7
FIELD_ROWS = 176
FIELD_TILES = 4
CAP_WE = 6
CAP_NS = 16
RELAY = 10
RIM_S = 2 * MOVED * TILE
RIM_Q = RIM_S + 16
RIM_M = RIM_Q + 16
SURF = RIM_M + 16
MESSAGE = SURF + FIELD_TILES * TILE
F32 = jnp.float32
SMEM = pl.BlockSpec(memory_space=pltpu.SMEM)
VMEM = pl.BlockSpec(memory_space=pltpu.VMEM)
ANY = pl.BlockSpec(memory_space=pl.ANY)


def lane_id(shape):
    return lax.broadcasted_iota(jnp.int32, shape, len(shape) - 1)


def turn(x, by, axis):
    size = x.shape[axis]
    if isinstance(by, int):
        by = by % size
        if by == 0:
            return x
    return pltpu.roll(x, by, axis)


def swap(to_next, to_last, axis, count):
    first = [(i, i ^ 1) for i in range(count)]
    second = [(i, (i + 1) % count if i % 2 else (i - 1) % count) for i in range(count)]
    return lax.ppermute(to_next, axis, first), lax.ppermute(to_last, axis, second)


def shifted(x, axis, by):
    length = lax.axis_size(axis)
    return lax.ppermute(x, axis, [(i, (i + by) % length) for i in range(length)])


def fill_places(code_ref, inv, slots):
    def clear(r, carry):
        inv[r] = -1
        return carry

    def place(s, carry):
        inv[code_ref[s]] = s
        return carry

    lax.fori_loop(0, 2 * REGION, clear, 0)
    lax.fori_loop(0, slots, place, 0)


def sums_kernel(meta, code, weight, diffusion, t_ref, low_ref, high_ref, s_ref, q_ref, a_ref, b_ref, far_ref, inv, part):
    step = pl.program_id(0)
    slots = s_ref.shape[0] // TILE
    tracer = lax.broadcasted_iota(jnp.int32, (TILE, LANES), 0) % 2
    pairs = [(n, h) for n in range(STEP_SLOTS) for h in range(2)]
    acc_s = {p: jnp.zeros((TILE, LANES), F32) for p in pairs}
    acc_q = {p: jnp.zeros((TILE, LANES), F32) for p in pairs}
    for level in range(LEVELS):
        w = jnp.where(tracer == 0, weight[0, level], weight[1, level])
        wd = w * diffusion[level]
        for n, h in pairs:
            x = t_ref[n, level, pl.ds(h * TILE, TILE), :]
            acc_s[n, h] = acc_s[n, h] + w * x
            acc_q[n, h] = acc_q[n, h] + wd * x
    for n, h in pairs:
        part[0, pl.ds(n * ROWS + h * TILE, TILE), :] = acc_s[n, h]
        part[1, pl.ds(n * ROWS + h * TILE, TILE), :] = acc_q[n, h]
    for n in range(STEP_SLOTS):
        row = pl.multiple_of((step * STEP_SLOTS + n) * TILE, TILE)
        for kind, out in ((0, s_ref), (1, q_ref)):
            even = part[kind, pl.ds(n * ROWS, TILE, stride=2), :]
            odd = part[kind, pl.ds(n * ROWS + 1, TILE, stride=2), :]
            out[pl.ds(row, TILE), :] = even + odd

    @pl.when(step == 0)
    def _():
        fill_places(code, inv, slots)

    def rim(dest, base, first, chunk):
        for k in range(REG_X):
            src = inv[first + k]
            at = jnp.maximum(src, 0) * TILE + chunk
            has = jnp.where(src >= 0, 1.0, 0.0)
            dest[pl.ds(base + k, 1), :] = jnp.where(src >= 0, s_ref[pl.ds(at, 1), :], 0.0)
            dest[pl.ds(base + 16 + k, 1), :] = jnp.where(src >= 0, q_ref[pl.ds(at, 1), :], 0.0)
            dest[pl.ds(base + 32 + k, 1), :] = jnp.full((1, LANES), has, F32)
        for k in range(REG_X, 16):
            for kind in range(3):
                dest[pl.ds(base + 16 * kind + k, 1), :] = jnp.zeros((1, LANES), F32)

    def surface(dest, edge):
        for b in range(FIELD_TILES):
            if b < 3:
                dest[pl.ds(SURF + b * TILE, TILE), :] = edge[:, pl.ds(b * LANES, LANES)]
            else:
                width = edge.shape[1] - b * LANES
                dest[pl.ds(SURF + b * TILE, TILE), :] = jnp.zeros((TILE, LANES), F32)
                dest[pl.ds(SURF + b * TILE, TILE), pl.ds(0, width)] = edge[:, pl.ds(b * LANES, width)]

    def messages(up, down):
        height = MOVED * TILE
        first = (slots - MOVED) * TILE
        up[pl.ds(0, height), :] = s_ref[pl.ds(first, height), :]
        up[pl.ds(height, height), :] = q_ref[pl.ds(first, height), :]
        rim(up, RIM_S, REGION - REG_X, TILE - 1)
        surface(up, high_ref)
        down[pl.ds(0, 2 * height), :] = jnp.zeros((2 * height, LANES), F32)
        rim(down, RIM_S, 0, 0)
        surface(down, low_ref)

    @pl.when(step == pl.num_programs(0) - 1)
    def _():
        rim(far_ref, 0, 2 * REGION - REG_X, TILE - 1)

        @pl.when(meta[1] % 2 == 0)
        def _():
            messages(a_ref, b_ref)

        @pl.when(meta[1] % 2 == 1)
        def _():
            messages(b_ref, a_ref)


def depth_sums(view, meta, code, weight, diffusion, surface):
    slots = view.shape[0]
    steps = slots // STEP_SLOTS
    rows, width = surface.shape
    whole = lambda *shape: pl.BlockSpec(shape, lambda s: (0,) * len(shape))
    return pl.pallas_call(
        sums_kernel,
        grid=(steps,),
        in_specs=[
            SMEM,
            SMEM,
            SMEM,
            SMEM,
            pl.BlockSpec((STEP_SLOTS, LEVELS, ROWS, LANES), lambda s: (s, 0, 0, 0)),
            pl.BlockSpec((TILE, width), lambda s: (0, 0)),
            pl.BlockSpec((TILE, width), lambda s: (rows // TILE - 1, 0)),
        ],
        out_specs=[
            whole(slots * TILE, LANES),
            whole(slots * TILE, LANES),
            whole(MESSAGE, LANES),
            whole(MESSAGE, LANES),
            whole(48, LANES),
        ],
        out_shape=[
            jax.ShapeDtypeStruct((slots * TILE, LANES), F32),
            jax.ShapeDtypeStruct((slots * TILE, LANES), F32),
            jax.ShapeDtypeStruct((MESSAGE, LANES), F32),
            jax.ShapeDtypeStruct((MESSAGE, LANES), F32),
            jax.ShapeDtypeStruct((48, LANES), F32),
        ],
        scratch_shapes=[
            pltpu.SMEM((2 * REGION,), jnp.int32),
            pltpu.VMEM((2, STEP_SLOTS * ROWS, LANES), F32),
        ],
        compiler_params=pltpu.CompilerParams(vmem_limit_bytes=12 << 20),
        name="depth_sums",
    )(meta, code, weight, diffusion, view, surface, surface)


def field_kernel(meta, code, came, s_ref, q_ref, a_ref, b_ref, far_ref, surf_ref, f_ref, ca_ref, cb_ref, inv):
    slots = s_ref.shape[0] // TILE
    even = meta[1] % 2 == 0
    group = lane_id((TILE, LANES)) // BLOCK
    fill_places(code, inv, slots)

    def place_came(k, carry):
        r = came[slots - MOVED + k] - REGION

        @pl.when(r >= 0)
        def _():
            inv[r] = slots + k

        return carry

    lax.fori_loop(0, MOVED, place_came, 0)

    def below(start, size):
        return jnp.where(even, b_ref[pl.ds(start, size), :], a_ref[pl.ds(start, size), :])

    def above(start, size):
        return jnp.where(even, a_ref[pl.ds(start, size), :], b_ref[pl.ds(start, size), :])

    f_ref[...] = jnp.zeros(f_ref.shape, F32)
    for by in range(REG_Y):
        for b in range(FIELD_TILES):
            held = [g for g in range(4) if 4 * b + g < REG_X]
            mask = jnp.zeros((TILE, LANES), F32)
            tiles = {}
            for g in held:
                src = inv[by * REG_X + 4 * b + g]
                own_at = pl.multiple_of(jnp.clip(src, 0, slots - 1) * TILE, TILE)
                came_at = pl.multiple_of(jnp.clip(src - slots, 0, MOVED - 1) * TILE, TILE)
                for kind, ref in ((0, s_ref), (1, q_ref)):
                    own = ref[pl.ds(own_at, TILE), :]
                    other = below(pl.multiple_of(kind * MOVED * TILE + came_at, TILE), TILE)
                    tiles[kind, g] = jnp.where(src >= slots, other, jnp.where(src >= 0, own, 0.0))
                mask = jnp.where(group == g, jnp.where(src >= 0, 1.0, 0.0), mask)
            for kind in range(2):
                for q in range(4):
                    value = jnp.zeros((TILE, LANES), F32)
                    for g in held:
                        value = jnp.where(group == g, turn(tiles[kind, g], BLOCK * (g - q), 1), value)
                    f_ref[kind, b, pl.ds(TILE + BLOCK * by + q, TILE, stride=4), :] = value
            for q in range(4):
                f_ref[2, b, pl.ds(TILE + BLOCK * by + TILE * q, TILE), :] = mask

    row16 = lax.broadcasted_iota(jnp.int32, (16, LANES), 0)
    group16 = lane_id((16, LANES)) // BLOCK

    def rim_rows(kind, rim, first):
        rolled = [turn(rim, BLOCK * d, 1) for d in range(4)]
        for q in range(4):
            value = jnp.zeros((16, LANES), F32)
            for g in range(4):
                value = jnp.where((row16 % 4 == g) & (group16 == g), rolled[(g - q) % 4], value)
            value = value + turn(value, -1, 0)
            value = value + turn(value, -2, 0)
            for b in range(FIELD_TILES):
                f_ref[kind, b, pl.ds(first + q, 1), :] = value[4 * b : 4 * b + 1, :]

    @pl.when(meta[1] > 0)
    def _():
        for kind, base in ((0, RIM_S), (1, RIM_Q), (2, RIM_M)):
            rim_rows(kind, below(base, 16) + far_ref[pl.ds(base - RIM_S, 16), :], 4)

    @pl.when(meta[1] < meta[2] - 1)
    def _():
        def own_rim(ref):
            rows = []
            for k in range(16):
                if k < REG_X:
                    src = inv[REGION + k]
                    at = jnp.maximum(src, 0) * TILE
                    line = jnp.ones((1, LANES), F32) if ref is None else ref[pl.ds(at, 1), :]
                    rows.append(jnp.where(src >= 0, line, 0.0))
                else:
                    rows.append(jnp.zeros((1, LANES), F32))
            return jnp.concatenate(rows, axis=0)

        for kind, base, ref in ((0, RIM_S, s_ref), (1, RIM_Q, q_ref), (2, RIM_M, None)):
            rim_rows(kind, above(base, 16) + own_rim(ref), FIELD_ROWS - TILE)

    height, width = surf_ref.shape
    for b in range(FIELD_TILES):
        lanes = min(LANES, width - b * LANES)
        f_ref[3, b, pl.ds(TILE, height), pl.ds(0, lanes)] = surf_ref[:, pl.ds(b * LANES, lanes)]
        f_ref[3, b, pl.ds(4, 4), :] = below(SURF + b * TILE, TILE)[4:]
        f_ref[3, b, pl.ds(FIELD_ROWS - TILE, 4), :] = above(SURF + b * TILE, TILE)[:4]

    lane = lane_id((TILE, LANES))
    last = width - (FIELD_TILES - 1) * LANES - 4
    east_even = meta[0] % 2 == 0
    for h in range(3):
        west_out = jnp.zeros((TILE, LANES), F32)
        east_out = jnp.zeros((TILE, LANES), F32)
        for g in range(8):
            v = 3 * g + h
            if v * TILE >= FIELD_ROWS:
                continue
            for kind in range(4):
                at = 16 * g + 4 * kind
                inside = (lane >= at) & (lane < at + 4)
                west = f_ref[kind, 0, pl.ds(v * TILE, TILE), :]
                east = f_ref[kind, FIELD_TILES - 1, pl.ds(v * TILE, TILE), :]
                west_out = jnp.where(inside, turn(west, at, 1), west_out)
                east_out = jnp.where(inside, turn(east, at - last, 1), east_out)
        ca_ref[pl.ds(h * TILE, TILE), :] = jnp.where(east_even, east_out, west_out)
        cb_ref[pl.ds(h * TILE, TILE), :] = jnp.where(east_even, west_out, east_out)


def region_fields(meta, code, came, s, q, a, b, far, surface):
    return pl.pallas_call(
        field_kernel,
        in_specs=[SMEM, SMEM, SMEM] + [VMEM] * 6,
        out_specs=[VMEM] * 3,
        out_shape=[
            jax.ShapeDtypeStruct((4, FIELD_TILES, FIELD_ROWS, LANES), F32),
            jax.ShapeDtypeStruct((24, LANES), F32),
            jax.ShapeDtypeStruct((24, LANES), F32),
        ],
        scratch_shapes=[pltpu.SMEM((2 * REGION,), jnp.int32)],
        compiler_params=pltpu.CompilerParams(vmem_limit_bytes=12 << 20),
        name="region_fields",
    )(meta, code, came, s, q, a, b, far, surface)


def basis_kernel(meta, f_ref, ca_ref, cb_ref, u_ref, g_ref):
    even = meta[0] % 2 == 0
    lane = lane_id((TILE, LANES))
    tiles = range(FIELD_TILES)
    fields = []
    for kind in range(4):
        parts = [f_ref[kind, b] for b in tiles]
        strip = []
        for v in range(FIELD_ROWS // TILE):
            g, h = v // 3, v % 3
            ca = ca_ref[pl.ds(h * TILE, TILE), :]
            cb = cb_ref[pl.ds(h * TILE, TILE), :]
            at = 16 * g + 4 * kind
            west = turn(jnp.where(even, cb, ca), 124 - at, 1)
            east = turn(jnp.where(even, ca, cb), 64 - at, 1)
            tile = f_ref[kind, FIELD_TILES - 1, pl.ds(v * TILE, TILE), :]
            tile = jnp.where((lane >= 64) & (lane < 68), east, tile)
            strip.append(jnp.where(lane >= 124, west, tile))
        parts[-1] = jnp.concatenate(strip, axis=0)
        fields.append(parts)
    depth, inner, mask, surf = fields
    wide = lane_id((FIELD_ROWS, LANES))

    def sides(v):
        fwd = [turn(x, 1, 1) for x in v]
        bwd = [turn(x, -1, 1) for x in v]
        out = []
        for b in tiles:
            left = jnp.where(wide == 0, fwd[b - 1], fwd[b])
            right = jnp.where(wide == LANES - 1, bwd[(b + 1) % FIELD_TILES], bwd[b])
            out.append(left + right)
        return out

    def rows(v):
        return [turn(x, 1, 0) + turn(x, -1, 0) for x in v]

    def spread(v):
        side = sides(v)
        both = rows([v[b] + 0.5 * side[b] for b in tiles])
        return [mask[b] * (side[b] + both[b]) for b in tiles]

    def edges(v):
        side, both = sides(v), rows(v)
        return [side[b] + both[b] for b in tiles]

    near, count = edges(inner), edges(mask)
    rhs = [mask[b] * (depth[b] + near[b] - count[b] * inner[b]) for b in tiles]
    scale = [1.0 / (6.0 + surf[b]) for b in tiles]
    u0 = [rhs[b] * scale[b] for b in tiles]
    z1 = spread(u0)
    u1 = [z1[b] * scale[b] for b in tiles]
    z2 = spread(u1)
    u2 = [z2[b] * scale[b] for b in tiles]
    z3 = spread(u2)
    rows_in = slice(TILE, FIELD_ROWS - TILE)

    def dot(x, y):
        total = jnp.zeros((TILE, LANES), F32)
        for b in tiles:
            p = x[b][rows_in] * y[b][rows_in]
            p = jnp.sum(p.reshape(-1, TILE, LANES), axis=0)
            if b == FIELD_TILES - 1:
                p = jnp.where(lane < 64, p, 0.0)
            total = total + p
        return jnp.sum(jnp.sum(total, axis=1, keepdims=True), axis=0, keepdims=True)

    row = jnp.zeros((1, LANES), F32)
    pairs = ((u0, rhs), (u0, z1), (u1, z1), (u1, z2), (u2, z2), (u2, z3))
    for k, (x, y) in enumerate(pairs):
        row = jnp.where(lane[:1] == k, dot(x, y), row)
    row = jnp.where(lane[:1] == 6, meta[3].astype(F32), row)
    g_ref[...] = jnp.broadcast_to(row, g_ref.shape)
    for k, u in enumerate((u0, u1, u2)):
        for b in tiles:
            u_ref[k, b] = u[b][rows_in]


def solve_basis(meta, fields, ca, cb, devices):
    return pl.pallas_call(
        basis_kernel,
        in_specs=[SMEM, VMEM, VMEM, VMEM],
        out_specs=[VMEM, VMEM],
        out_shape=[
            jax.ShapeDtypeStruct((3, FIELD_TILES, FIELD_ROWS - 2 * TILE, LANES), F32),
            jax.ShapeDtypeStruct((devices, LANES), F32),
        ],
        compiler_params=pltpu.CompilerParams(vmem_limit_bytes=24 << 20),
        name="solve_basis",
    )(meta, fields, ca, cb)


def solution_kernel(came, u_ref, g_ref, blocks_ref, back_ref, over_ref):
    total = jnp.sum(g_ref[...].reshape(-1, TILE, LANES), axis=0)
    total = jnp.broadcast_to(jnp.sum(total, axis=0, keepdims=True), (TILE, LANES))
    lane = lane_id((TILE, LANES))
    pick = lambda k: jnp.sum(jnp.where(lane == k, total, 0.0), axis=1, keepdims=True)
    over_ref[...] = jnp.broadcast_to(pick(6), (TILE, LANES))
    g = [pick(k) for k in range(6)]
    g = [x / g[0] for x in g]
    a = [g[k] - g[k + 1] for k in range(5)]
    zero = jnp.zeros_like(g[0])
    one = zero + 1.0

    def form(v, m):
        out = zero
        for i in range(3):
            for k in range(3):
                out = out + v[i] * v[k] * m[i + k]
        return out

    coef = [zero, zero, zero]
    rho = [one, zero, zero]
    way = [one, zero, zero]
    norm = g[0]
    for iteration in range(3):
        length = norm / form(way, a)
        coef = [coef[k] + length * way[k] for k in range(3)]
        if iteration < 2:
            moved = [way[0], way[1] - way[0], way[2] - way[1]]
            rho = [rho[k] - length * moved[k] for k in range(3)]
            norm_next = form(rho, g)
            way = [rho[k] + (norm_next / norm) * way[k] for k in range(3)]
            norm = norm_next
    coef = [jnp.broadcast_to(c, (TILE, LANES)) for c in coef]
    group = lane // BLOCK
    for by in range(REG_Y):
        for b in range(FIELD_TILES):
            value = []
            for q in range(4):
                at = pl.ds(BLOCK * by + q, TILE, stride=4)
                value.append(coef[0] * u_ref[0, b, at, :] + coef[1] * u_ref[1, b, at, :] + coef[2] * u_ref[2, b, at, :])
            for g4 in range(4):
                if 4 * b + g4 >= REG_X:
                    continue
                tile = jnp.zeros((TILE, LANES), F32)
                for q in range(4):
                    tile = jnp.where(group == q, turn(value[q], BLOCK * (q - g4), 1), tile)
                blocks_ref[pl.ds((by * REG_X + 4 * b + g4) * TILE, TILE), :] = tile
    first = came.shape[0] - MOVED
    for k in range(MOVED):
        at = pl.multiple_of(jnp.maximum(came[first + k] - REGION, 0) * TILE, TILE)
        back_ref[pl.ds(k * TILE, TILE), :] = blocks_ref[pl.ds(at, TILE), :]


def region_solution(came, u, g):
    return pl.pallas_call(
        solution_kernel,
        in_specs=[SMEM, VMEM, VMEM],
        out_specs=[VMEM] * 3,
        out_shape=[
            jax.ShapeDtypeStruct((REGION * TILE, LANES), F32),
            jax.ShapeDtypeStruct((MOVED * TILE, LANES), F32),
            jax.ShapeDtypeStruct((TILE, LANES), F32),
        ],
        compiler_params=pltpu.CompilerParams(vmem_limit_bytes=12 << 20),
        name="region_solution",
    )(came, u, g)


def pressure_kernel(code, blocks_ref, back_ref, out_ref, work):
    slots = out_ref.shape[0]
    for s in range(slots):
        c = code[s]
        at = pl.multiple_of(jnp.where(c < REGION, c, 0) * TILE, TILE)
        tile = blocks_ref[pl.ds(at, TILE), :]
        k = s - (slots - MOVED)
        if k >= 0:
            tile = jnp.where(c < REGION, tile, back_ref[pl.ds(k * TILE, TILE), :])
        work[pl.ds(s * TILE, TILE), :] = tile
    for first in range(0, slots, TILE):
        size = min(TILE, slots - first)
        for c in range(TILE):
            lines = work[pl.ds(first * TILE + c, size, stride=TILE), :]
            out_ref[pl.ds(first, size), pl.ds(c * LANES, LANES)] = lines


def slot_pressure(code, blocks, back):
    slots = code.shape[0]
    return pl.pallas_call(
        pressure_kernel,
        in_specs=[SMEM, VMEM, VMEM],
        out_specs=VMEM,
        out_shape=jax.ShapeDtypeStruct((slots, TILE * LANES), F32),
        scratch_shapes=[pltpu.VMEM((slots * TILE, LANES), F32)],
        compiler_params=pltpu.CompilerParams(vmem_limit_bytes=12 << 20),
        name="slot_pressure",
    )(code, blocks, back)


def columns_kernel(meta, code, t_ref, a_ref, b_ref, inv, west, east, sems):
    fill_places(code, inv, code.shape[0])
    even = meta[0] % 2 == 0
    count = 2 * REG_Y

    def copies(k):
        w, e = inv[REG_X * k], inv[REG_X * k + REG_X - 1]
        cw = pltpu.make_async_copy(t_ref.at[jnp.maximum(w, 0)], west.at[k], sems.at[0, k])
        ce = pltpu.make_async_copy(t_ref.at[jnp.maximum(e, 0)], east.at[k], sems.at[1, k])
        return cw, ce

    for k in range(count):
        for c in copies(k):
            c.start()
    for k in range(count):
        for c in copies(k):
            c.wait()
    column = lane_id((ROWS, LANES)) % BLOCK
    for level in range(HALF):
        out_w = jnp.zeros((ROWS, LANES), F32)
        out_e = jnp.zeros((ROWS, LANES), F32)
        for k in range(count):
            has_w, has_e = inv[REG_X * k] >= 0, inv[REG_X * k + REG_X - 1] >= 0
            for part in range(2):
                lane = k + 16 * part
                here = column == lane
                at = level + HALF * part
                out_w = jnp.where(here & has_w, turn(west[k, at], lane, 1), out_w)
                out_e = jnp.where(here & has_e, turn(east[k, at], lane - (BLOCK - 1), 1), out_e)
        a_ref[pl.ds(level * ROWS, ROWS), :] = jnp.where(even, out_e, out_w)
        b_ref[pl.ds(level * ROWS, ROWS), :] = jnp.where(even, out_w, out_e)


def column_strips(meta, code, view):
    count = 2 * REG_Y
    return pl.pallas_call(
        columns_kernel,
        in_specs=[SMEM, SMEM, ANY],
        out_specs=[VMEM] * 2,
        out_shape=[jax.ShapeDtypeStruct((HALF * ROWS, LANES), F32)] * 2,
        scratch_shapes=[
            pltpu.SMEM((2 * REGION,), jnp.int32),
            pltpu.VMEM((count, LEVELS, ROWS, LANES), F32),
            pltpu.VMEM((count, LEVELS, ROWS, LANES), F32),
            pltpu.SemaphoreType.DMA((2, count)),
        ],
        compiler_params=pltpu.CompilerParams(vmem_limit_bytes=12 << 20),
        name="column_strips",
    )(meta, code, view)


def links_kernel(meta, table, t_ref, ga_ref, gb_ref, a_ref, b_ref, whole, half, sem_we, sem_ns):
    even_x = meta[0] % 2 == 0
    even_y = meta[1] % 2 == 0

    def we_copy(way, k):
        link = jnp.maximum(table[way * (CAP_WE + CAP_NS) + k], 0)
        return pltpu.make_async_copy(t_ref.at[link // 4], whole.at[way, k], sem_we.at[way, k])

    def ns_copy(way, k):
        link = jnp.maximum(table[way * (CAP_WE + CAP_NS) + CAP_WE + k], 2)
        rows = pl.ds(pl.multiple_of((link % 4 - 2) * TILE, TILE), TILE)
        return pltpu.make_async_copy(t_ref.at[link // 4, :, rows, :], half.at[way, k], sem_ns.at[way, k])

    for way in range(2):
        for k in range(CAP_WE):
            @pl.when(table[way * (CAP_WE + CAP_NS) + k] >= 0)
            def _():
                we_copy(way, k).start()

        for k in range(CAP_NS):
            @pl.when(table[way * (CAP_WE + CAP_NS) + CAP_WE + k] >= 0)
            def _():
                ns_copy(way, k).start()

    column = lane_id((HALF * ROWS, LANES)) % 16
    from_west = jnp.where(even_x, gb_ref[...], ga_ref[...])
    from_east = jnp.where(even_x, ga_ref[...], gb_ref[...])
    ways = ((turn(from_west, -5, 1), from_east), (from_west, turn(from_east, 5, 1)))
    relays = [jnp.where(column < 5, w, jnp.where(column < RELAY, e, 0.0)) for w, e in ways]

    def message(way, out):
        out[pl.ds(0, HALF * ROWS), :] = relays[way]
        out[pl.ds(HALF * ROWS, LEVELS * TILE), :] = jnp.zeros((LEVELS * TILE, LANES), F32)
        lane32 = lane_id((ROWS, LANES)) % BLOCK
        for k in range(CAP_WE):
            link = table[way * (CAP_WE + CAP_NS) + k]

            @pl.when(link >= 0)
            def _():
                we_copy(way, k).wait()
                start = (link % 4) * (BLOCK - 1)
                for level in range(HALF):
                    at = pl.ds(level * ROWS, ROWS)
                    value = out[at, :]
                    for part in range(2):
                        lane = RELAY + k + 16 * part
                        x = turn(whole[way, k, level + HALF * part], lane, 1)
                        x = jnp.where(start > 0, turn(x, 1 - BLOCK, 1), x)
                        value = jnp.where(lane32 == lane, x, value)
                    out[at, :] = value

        row = lax.broadcasted_iota(jnp.int32, (LEVELS, TILE, LANES), 1)
        group = lane_id((LEVELS, TILE, LANES)) // BLOCK
        base = HALF * ROWS
        for k in range(CAP_NS):
            link = table[way * (CAP_WE + CAP_NS) + CAP_WE + k]

            @pl.when(link >= 0)
            def _():
                ns_copy(way, k).wait()
                x = half[way, k]

                def put(x):
                    keep = (row // 2 == k // 4) & (group == k % 4)
                    old = out[pl.ds(base, LEVELS * TILE), :].reshape(LEVELS, TILE, LANES)
                    new = jnp.where(keep, x, old)
                    out[pl.ds(base, LEVELS * TILE), :] = new.reshape(LEVELS * TILE, LANES)

                @pl.when(link % 4 == 2)
                def _():
                    put(turn(turn(x, 2 * (k // 4), 1), BLOCK * (k % 4), 2))

                @pl.when(link % 4 == 3)
                def _():
                    put(turn(turn(x, 2 * (k // 4) + 2, 1), BLOCK * (k % 4) + BLOCK, 2))

    @pl.when(even_y)
    def _():
        message(0, a_ref)
        message(1, b_ref)

    @pl.when(jnp.logical_not(even_y))
    def _():
        message(0, b_ref)
        message(1, a_ref)


def link_strips(meta, table, view, ga, gb):
    rows = HALF * ROWS + LEVELS * TILE
    return pl.pallas_call(
        links_kernel,
        in_specs=[SMEM, SMEM, ANY, VMEM, VMEM],
        out_specs=[VMEM] * 2,
        out_shape=[jax.ShapeDtypeStruct((rows, LANES), F32)] * 2,
        scratch_shapes=[
            pltpu.VMEM((2, CAP_WE, LEVELS, ROWS, LANES), F32),
            pltpu.VMEM((2, CAP_NS, LEVELS, TILE, LANES), F32),
            pltpu.SemaphoreType.DMA((2, CAP_WE)),
            pltpu.SemaphoreType.DMA((2, CAP_NS)),
        ],
        compiler_params=pltpu.CompilerParams(vmem_limit_bytes=12 << 20),
        name="link_strips",
    )(meta, table, view, ga, gb)


EXTRA = 7
TALL = 32
CHUNK = 4


def tracer_kernel(meta, table, need, diffusion, t_ref, ga_ref, gb_ref, ha_ref, hb_ref, out_ref, buf, seen, sems):
    step = pl.program_id(0)
    steps = pl.num_programs(0)
    slots = buf.shape[0] - EXTRA

    def fetch(c):
        src = t_ref.at[pl.ds(c * STEP_SLOTS, STEP_SLOTS)]
        dst = buf.at[pl.ds(c * STEP_SLOTS, STEP_SLOTS), :, pl.ds(TILE, ROWS), :]
        return pltpu.make_async_copy(src, dst, sems.at[c])

    @pl.when(step == 0)
    def _():
        for c in range(slots // STEP_SLOTS):
            fetch(c).start()
        seen[0] = 0
        even_x = meta[0] % 2 == 0
        even_y = meta[1] % 2 == 0

        def unfold(image, value):
            for level in range(HALF):
                x = value[level * ROWS : (level + 1) * ROWS]
                buf[image, level, pl.ds(TILE, ROWS), :] = x
                buf[image, level + HALF, pl.ds(TILE, ROWS), :] = turn(x, -16, 1)

        for level in range(LEVELS):
            buf[slots, level, pl.ds(TILE, ROWS), :] = jnp.zeros((ROWS, LANES), F32)
        unfold(slots + 1, jnp.where(even_x, gb_ref[...], ga_ref[...]))
        unfold(slots + 2, jnp.where(even_x, ga_ref[...], gb_ref[...]))
        folded = pl.ds(0, HALF * ROWS)
        unfold(slots + 3, jnp.where(even_y, hb_ref[folded, :], ha_ref[folded, :]))
        unfold(slots + 4, jnp.where(even_y, ha_ref[folded, :], hb_ref[folded, :]))
        for level in range(LEVELS):
            rows = pl.ds(HALF * ROWS + level * TILE, TILE)
            first, second = ha_ref[rows, :], hb_ref[rows, :]
            buf[slots + 5, level, pl.ds(TILE, TILE), :] = jnp.where(even_y, second, first)
            buf[slots + 6, level, pl.ds(TILE, TILE), :] = jnp.where(even_y, first, second)

    def arrive(c, carry):
        fetch(c).wait()
        return carry

    upto = jnp.maximum(seen[0], need[step] + 1)
    lax.fori_loop(seen[0], upto, arrive, 0)
    seen[0] = upto

    cells = (ROWS, LANES)
    lane = lane_id(cells)
    column = lane % BLOCK
    row = lax.broadcasted_iota(jnp.int32, cells, 0)
    edge = (
        jnp.where(column == 0, 1.0, 0.0),
        jnp.where(column == BLOCK - 1, 1.0, 0.0),
        jnp.where((row < 2) & (lane < BLOCK), 1.0, 0.0),
        jnp.where((row >= ROWS - 2) & (lane >= LANES - BLOCK), 1.0, 0.0),
    )

    def one_slot(n, carry):
        s = step * STEP_SLOTS + n
        entry = [[table[s * 16 + 4 * t + f] for f in range(4)] for t in range(4)]
        count = jnp.full(cells, 4.0, F32)
        for t in range(4):
            count = count - edge[t] * entry[t][3].astype(F32)
        for t, dest in ((2, TILE - 2), (3, TILE + ROWS)):
            image, at, by, _ = entry[t]
            line = buf[image, :, pl.ds(TILE + at, 2), :]
            buf[s, :, pl.ds(dest, 2), :] = pltpu.roll(line, by, 2)
        (west, _, by_west, _), (east, _, by_east, _) = entry[0], entry[1]
        shape = (CHUNK, ROWS, LANES)
        lane3 = lane_id(shape)
        column3 = lane3 % BLOCK
        for first in range(0, LEVELS, CHUNK):
            some = pl.ds(first, CHUNK)
            x = buf[s, some, pl.ds(TILE, ROWS), :]
            under = buf[s, some, pl.ds(TILE - 2, ROWS), :]
            over = buf[s, some, pl.ds(TILE + 2, ROWS), :]
            w = buf[west, some, pl.ds(TILE, ROWS), :]
            e = buf[east, some, pl.ds(TILE, ROWS), :]
            total = pltpu.roll(jnp.where(lane3 >= LANES - BLOCK, under, x), BLOCK, 2)
            total = total + pltpu.roll(jnp.where(lane3 < BLOCK, over, x), LANES - BLOCK, 2)
            total = total + jnp.where(column3 == 0, pltpu.roll(w, by_west, 2), pltpu.roll(x, 1, 2))
            total = total + jnp.where(column3 == BLOCK - 1, pltpu.roll(e, by_east, 2), pltpu.roll(x, LANES - 1, 2))
            for i in range(CHUNK):
                out_ref[n, first + i] = x[i] + diffusion[first + i] * (total[i] - count * x[i])
        return carry

    lax.fori_loop(0, STEP_SLOTS, one_slot, 0)

    @pl.when(step == steps - 1)
    def _():
        lax.fori_loop(seen[0], slots // STEP_SLOTS, arrive, 0)


def step_tracers(meta, table, need, diffusion, view, ga, gb, ha, hb):
    slots = view.shape[0]
    steps = slots // STEP_SLOTS
    shape = (STEP_SLOTS, LEVELS, ROWS, LANES)
    return pl.pallas_call(
        tracer_kernel,
        grid=(steps,),
        in_specs=[SMEM] * 4 + [ANY] + [VMEM] * 4,
        out_specs=pl.BlockSpec(shape, lambda s: (s, 0, 0, 0)),
        out_shape=jax.ShapeDtypeStruct(view.shape, F32),
        scratch_shapes=[
            pltpu.VMEM((slots + EXTRA, LEVELS, TALL, LANES), F32),
            pltpu.SMEM((1,), jnp.int32),
            pltpu.SemaphoreType.DMA((steps,)),
        ],
        compiler_params=pltpu.CompilerParams(vmem_limit_bytes=40 << 20),
        name="step_tracers",
    )(meta, table, need, diffusion, view, ga, gb, ha, hb)


def with_halo(block, sides, width):
    for axis, dim in sides:
        low = shifted(lax.slice_in_dim(block, block.shape[dim] - width, None, axis=dim), axis, 1)
        high = shifted(lax.slice_in_dim(block, 0, width, axis=dim), axis, -1)
        block = jnp.concatenate([low, block, high], axis=dim)
    return block


def edge_strips(grid):
    sides = [grid[..., :, 0], grid[..., :, -1], grid[..., 0, :], grid[..., -1, :]]
    return jnp.stack(sides, axis=1).reshape(grid.shape[0] * 4, -1)


def general_step(tracers, diffusion, halo_source):
    slots = tracers.shape[0]
    grid = tracers.reshape(slots, TRACER, LEVELS, BLOCK, BLOCK)
    strips = edge_strips(grid)
    width = strips.shape[1]
    count_gx, count_gy = lax.axis_size("gx"), lax.axis_size("gy")
    source = halo_source.reshape(-1)
    missing = source >= 4 * slots * count_gx * count_gy
    slot = jnp.where(missing, 0, source) // 4
    owner = slot // slots
    step_gx = (owner // count_gy - lax.axis_index("gx") + count_gx + 1) % count_gx
    step_gy = (owner % count_gy - lax.axis_index("gy") + count_gy + 1) % count_gy
    every = slots * 4
    table = with_halo(strips.reshape(1, 1, every, width), (("gx", 0), ("gy", 1)), 1).reshape(9 * every, width)
    index = (step_gx * 3 + step_gy) * every + slot % slots * 4 + source % 4
    halo = jnp.take(table, jnp.where(missing, 0, index), axis=0, mode="clip")
    halo = halo.reshape(slots, 4, TRACER, LEVELS, BLOCK)
    gate = jnp.where(missing, 0.0, 1.0).astype(F32).reshape(slots, 4, 1, 1, 1)
    inner_x = grid[..., :, :-1] - grid[..., :, 1:]
    inner_y = grid[..., :-1, :] - grid[..., 1:, :]
    west = (halo[:, 0] - grid[..., :, 0]) * gate[:, 0]
    east = (halo[:, 1] - grid[..., :, -1]) * gate[:, 1]
    south = (halo[:, 2] - grid[..., 0, :]) * gate[:, 2]
    north = (halo[:, 3] - grid[..., -1, :]) * gate[:, 3]
    laplace = (
        jnp.concatenate([west[..., None], inner_x], axis=-1)
        + jnp.concatenate([-inner_x, east[..., None]], axis=-1)
        + jnp.concatenate([south[..., None, :], inner_y], axis=-2)
        + jnp.concatenate([-inner_y, north[..., None, :]], axis=-2)
    )
    return (grid + diffusion[None, None, :, None, None] * laplace).reshape(tracers.shape)


def strip_tables(halo_source, code, at_x, at_y, count_x, count_y):
    slots = halo_source.shape[0]
    source = halo_source
    missing = source >= 4 * slots * count_x * count_y
    source = jnp.where(missing, 0, source)
    owner = source // (4 * slots)
    local_slot = source // 4 - owner * slots
    same_x = owner // count_y == at_x
    owner_y = owner % count_y
    up = owner_y == (at_y + 1) % count_y
    down = owner_y == (at_y + count_y - 1) % count_y
    here = owner_y == at_y
    side = lax.broadcasted_iota(jnp.int32, (slots, 4), 1)
    index = lax.broadcasted_iota(jnp.int32, (slots, 4), 0) * 4 + side
    kind = jnp.where(side >= 2, 1, 0)
    linked = ~missing & same_x & ~here
    group = jnp.where(linked, jnp.where(up, kind, 2 + kind), -1)

    def rank(key):
        flat_key, flat_group = key.reshape(-1), group.reshape(-1)
        before = (flat_key[None, :] < flat_key[:, None]) & (flat_group[None, :] == flat_group[:, None])
        return jnp.sum(before.astype(jnp.int32), axis=1).reshape(slots, 4)

    take = rank(index)
    give = rank(source)
    entries = []
    for way in range(2):
        entries += [(way * 2, k) for k in range(CAP_WE)] + [(way * 2 + 1, k) for k in range(CAP_NS)]
    want = jnp.asarray([g * 1024 + k for g, k in entries], jnp.int32)
    has = jnp.where(group >= 0, group * 1024 + give, -1).reshape(-1)
    hit = want[:, None] == has[None, :]
    send = jnp.sum(jnp.where(hit, index.reshape(-1)[None, :] + 1, 0), axis=1) - 1
    over = jnp.any(linked & (take >= jnp.where(kind == 1, CAP_NS, CAP_WE)))
    row = (code // REG_X)[:, None]
    land, west, east, we_low, we_high, ns_low, ns_high = [slots + k for k in range(EXTRA)]
    local = same_x & here
    beside = jnp.where(here, jnp.where(side == 0, west, east), jnp.where(up, we_high, we_low))
    beside_lane = jnp.where(here, row, row % REG_Y + jnp.where(side == 0, 0, REG_Y))
    lane = jnp.where(same_x, RELAY + take, beside_lane)
    image_we = jnp.where(local, local_slot, jnp.where(same_x, jnp.where(up, we_high, we_low), beside))
    by_we = jnp.where(side == 0, -jnp.where(local, BLOCK - 1, lane), BLOCK - 1 - jnp.where(local, 0, lane))
    image_ns = jnp.where(local, local_slot, jnp.where(up, ns_high, ns_low))
    row_ns = jnp.where(local, jnp.where(side == 2, ROWS - 2, 0), 2 * (take // 4))
    by_ns = jnp.where(local, 0, jnp.where(side == 2, LANES - BLOCK, 0) - BLOCK * (take % 4))
    north = kind == 1
    image = jnp.where(missing, land, jnp.where(north, image_ns, image_we))
    at = jnp.where(missing | ~north, 0, jnp.minimum(row_ns, ROWS - 2))
    by = jnp.where(missing, 0, jnp.where(north, by_ns, by_we)) % LANES
    table = jnp.stack([image, at, by, missing.astype(jnp.int32)], axis=-1).reshape(-1)
    last = jnp.where(local & ~missing, local_slot, 0)
    last = jnp.maximum(jnp.max(last, axis=1), jnp.arange(slots))
    need = jnp.max(last.reshape(-1, STEP_SLOTS), axis=1) // STEP_SLOTS
    return table, need, send, over.astype(jnp.int32)


def on_device(tracers, diffusion, layer_weight, surface_term, clinic_blocks, halo_source):
    slots = tracers.shape[0]
    count_x, count_y = lax.axis_size("gx"), lax.axis_size("gy")
    at_x, at_y = lax.axis_index("gx"), lax.axis_index("gy")
    grid_columns = REG_X * count_x
    grid_rows = REG_Y * count_y
    own_row = (clinic_blocks // grid_columns - REG_Y * at_y) % grid_rows
    code = own_row * REG_X + clinic_blocks % grid_columns % REG_X
    came = shifted(code, "gy", 1)
    zero = jnp.zeros((), jnp.int32)
    meta = jnp.stack([at_x, at_y, zero + count_y, zero]).astype(jnp.int32)

    view = tracers.reshape(slots, TRACER, LEVELS, TILE, LANES).transpose(0, 2, 3, 1, 4)
    view = view.reshape(slots, LEVELS, ROWS, LANES)
    s, q, a, b, far = depth_sums(view, meta, code, layer_weight, diffusion, surface_term)
    ra, rb = swap(a, b, "gy", count_y)
    rfar = shifted(far, "gy", 2)

    table, need, send, over = strip_tables(halo_source, code, at_x, at_y, count_x, count_y)
    ga, gb = swap(*column_strips(meta, code, view), "gx", count_x)

    fields, ca, cb = region_fields(meta, code, came, s, q, ra, rb, rfar, surface_term)
    ca, cb = swap(ca, cb, "gx", count_x)
    ha, hb = swap(*link_strips(meta, send, view, ga, gb), "gy", count_y)

    meta_over = jnp.stack([at_x, at_y, zero + count_y, over]).astype(jnp.int32)
    u, sums = solve_basis(meta_over, fields, ca, cb, count_x * count_y)
    sums = lax.all_to_all(sums, ("gx", "gy"), 0, 0, tiled=True)
    blocks, back, total_over = region_solution(came, u, sums)
    back = shifted(back, "gy", -1)

    updated = step_tracers(meta, table, need, diffusion, view, ga, gb, ha, hb)
    updated = updated.reshape(slots, LEVELS, TILE, TRACER, LANES).transpose(0, 3, 1, 2, 4)
    updated = updated.reshape(tracers.shape)
    pressure = slot_pressure(code, blocks, back)
    updated = lax.cond(
        total_over[0, 0] > 0,
        lambda fast: general_step(tracers, diffusion, halo_source),
        lambda fast: fast,
        updated,
    )
    return (updated, pressure)


def solution(mesh):
    placed = (
        P(("gx", "gy"), None, None, None),
        P(),
        P(),
        P("gy", "gx"),
        P(("gx", "gy")),
        P(("gx", "gy"), None),
    )
    return jax.shard_map(
        on_device,
        mesh=mesh,
        in_specs=placed,
        out_specs=(P(("gx", "gy"), None, None, None), P(("gx", "gy"), None)),
        check_vma=False,
    )
```

```python
import jax
import jax.numpy as jnp
from jax import lax
from jax.experimental import pallas as pl
from jax.experimental.layout import Layout, with_layout_constraint
from jax.experimental.pallas import tpu as pltpu
from jax.sharding import PartitionSpec as P

BLOCK = 32
LEVELS = 20
TRACER = 2
REG_X = 14
REG_Y = 5
ITERS = 3
REGION = REG_X * REG_Y
MOVED = 22
LANES = 128
TILE = 8
ROWS = 16
HALF = LEVELS // 2
STEP_SLOTS = 7
FIELD_ROWS = 176
FIELD_TILES = 4
CAP_WE = 6
CAP_NS = 16
RELAY = 10
LINK_ROWS = HALF * ROWS + (LEVELS + 1) * TILE
RIM_S = 2 * MOVED * TILE
RIM_Q = RIM_S + 16
RIM_M = RIM_Q + 16
SURF = RIM_M + 16
MESSAGE = SURF + FIELD_TILES * TILE
F32 = jnp.float32
SMEM = pl.BlockSpec(memory_space=pltpu.SMEM)
VMEM = pl.BlockSpec(memory_space=pltpu.VMEM)
ANY = pl.BlockSpec(memory_space=pl.ANY)


def lane_id(shape):
    return lax.broadcasted_iota(jnp.int32, shape, len(shape) - 1)


def turn(x, by, axis):
    size = x.shape[axis]
    if isinstance(by, int):
        by = by % size
        if by == 0:
            return x
    return pltpu.roll(x, by, axis)


def swap(to_next, to_last, axis, count):
    first = [(i, i ^ 1) for i in range(count)]
    second = [(i, (i + 1) % count if i % 2 else (i - 1) % count) for i in range(count)]
    return lax.ppermute(to_next, axis, first), lax.ppermute(to_last, axis, second)


def plain(x):
    return with_layout_constraint(x, Layout(major_to_minor=tuple(range(x.ndim))))


def seen_by_rows(tracers):
    slots = tracers.shape[0]
    view = tracers.reshape(slots, TRACER, LEVELS, TILE, LANES).transpose(0, 2, 3, 1, 4)
    return view.reshape(slots, LEVELS, ROWS, LANES)


def shifted(x, axis, by):
    length = lax.axis_size(axis)
    return lax.ppermute(x, axis, [(i, (i + by) % length) for i in range(length)])


def sums_kernel(meta, inv, weight, diffusion, t_ref, low_ref, high_ref, s_ref, q_ref, a_ref, b_ref, far_ref, part):
    step = pl.program_id(0)
    slots = s_ref.shape[0] // TILE
    tracer = lax.broadcasted_iota(jnp.int32, (TILE, LANES), 0) % 2
    pairs = [(n, h) for n in range(STEP_SLOTS) for h in range(2)]
    acc_s = {p: jnp.zeros((TILE, LANES), F32) for p in pairs}
    acc_q = {p: jnp.zeros((TILE, LANES), F32) for p in pairs}
    for level in range(LEVELS):
        w = jnp.where(tracer == 0, weight[0, level], weight[1, level])
        wd = w * diffusion[level]
        for n, h in pairs:
            x = t_ref[n, level, pl.ds(h * TILE, TILE), :]
            acc_s[n, h] = acc_s[n, h] + w * x
            acc_q[n, h] = acc_q[n, h] + wd * x
    for n, h in pairs:
        part[0, pl.ds(n * ROWS + h * TILE, TILE), :] = acc_s[n, h]
        part[1, pl.ds(n * ROWS + h * TILE, TILE), :] = acc_q[n, h]
    for n in range(STEP_SLOTS):
        row = pl.multiple_of((step * STEP_SLOTS + n) * TILE, TILE)
        for kind, out in ((0, s_ref), (1, q_ref)):
            even = part[kind, pl.ds(n * ROWS, TILE, stride=2), :]
            odd = part[kind, pl.ds(n * ROWS + 1, TILE, stride=2), :]
            out[pl.ds(row, TILE), :] = even + odd

    def rim(dest, base, first, chunk):
        for k in range(REG_X):
            src = inv[first + k]
            at = jnp.maximum(src, 0) * TILE + chunk
            has = jnp.where(src >= 0, 1.0, 0.0)
            dest[pl.ds(base + k, 1), :] = jnp.where(src >= 0, s_ref[pl.ds(at, 1), :], 0.0)
            dest[pl.ds(base + 16 + k, 1), :] = jnp.where(src >= 0, q_ref[pl.ds(at, 1), :], 0.0)
            dest[pl.ds(base + 32 + k, 1), :] = jnp.full((1, LANES), has, F32)
        for k in range(REG_X, 16):
            for kind in range(3):
                dest[pl.ds(base + 16 * kind + k, 1), :] = jnp.zeros((1, LANES), F32)

    def surface(dest, edge):
        for b in range(FIELD_TILES):
            if b < 3:
                dest[pl.ds(SURF + b * TILE, TILE), :] = edge[:, pl.ds(b * LANES, LANES)]
            else:
                width = edge.shape[1] - b * LANES
                dest[pl.ds(SURF + b * TILE, TILE), :] = jnp.zeros((TILE, LANES), F32)
                dest[pl.ds(SURF + b * TILE, TILE), pl.ds(0, width)] = edge[:, pl.ds(b * LANES, width)]

    def messages(up, down):
        height = MOVED * TILE
        first = (slots - MOVED) * TILE
        up[pl.ds(0, height), :] = s_ref[pl.ds(first, height), :]
        up[pl.ds(height, height), :] = q_ref[pl.ds(first, height), :]
        rim(up, RIM_S, REGION - REG_X, TILE - 1)
        surface(up, high_ref)
        down[pl.ds(0, 2 * height), :] = jnp.zeros((2 * height, LANES), F32)
        rim(down, RIM_S, 0, 0)
        surface(down, low_ref)

    @pl.when(step == pl.num_programs(0) - 1)
    def _():
        rim(far_ref, 0, 2 * REGION - REG_X, TILE - 1)

        @pl.when(meta[1] % 2 == 0)
        def _():
            messages(a_ref, b_ref)

        @pl.when(meta[1] % 2 == 1)
        def _():
            messages(b_ref, a_ref)


def depth_sums(view, meta, places, weight, diffusion, surface):
    slots = view.shape[0]
    steps = slots // STEP_SLOTS
    rows, width = surface.shape
    whole = lambda *shape: pl.BlockSpec(shape, lambda s: (0,) * len(shape))
    return pl.pallas_call(
        sums_kernel,
        grid=(steps,),
        in_specs=[
            SMEM,
            SMEM,
            SMEM,
            SMEM,
            pl.BlockSpec((STEP_SLOTS, LEVELS, ROWS, LANES), lambda s: (s, 0, 0, 0)),
            pl.BlockSpec((TILE, width), lambda s: (0, 0)),
            pl.BlockSpec((TILE, width), lambda s: (rows // TILE - 1, 0)),
        ],
        out_specs=[
            whole(slots * TILE, LANES),
            whole(slots * TILE, LANES),
            whole(MESSAGE, LANES),
            whole(MESSAGE, LANES),
            whole(48, LANES),
        ],
        out_shape=[
            jax.ShapeDtypeStruct((slots * TILE, LANES), F32),
            jax.ShapeDtypeStruct((slots * TILE, LANES), F32),
            jax.ShapeDtypeStruct((MESSAGE, LANES), F32),
            jax.ShapeDtypeStruct((MESSAGE, LANES), F32),
            jax.ShapeDtypeStruct((48, LANES), F32),
        ],
        scratch_shapes=[pltpu.VMEM((2, STEP_SLOTS * ROWS, LANES), F32)],
        compiler_params=pltpu.CompilerParams(vmem_limit_bytes=12 << 20),
        name="depth_sums",
    )(meta, places, weight, diffusion, view, surface, surface)


def field_kernel(meta, inv, s_ref, q_ref, a_ref, b_ref, far_ref, surf_ref, f_ref, ca_ref, cb_ref):
    slots = s_ref.shape[0] // TILE
    even = meta[1] % 2 == 0
    group = lane_id((TILE, LANES)) // BLOCK

    def below(start, size):
        return jnp.where(even, b_ref[pl.ds(start, size), :], a_ref[pl.ds(start, size), :])

    def above(start, size):
        return jnp.where(even, a_ref[pl.ds(start, size), :], b_ref[pl.ds(start, size), :])

    f_ref[...] = jnp.zeros(f_ref.shape, F32)
    for by in range(REG_Y):
        for b in range(FIELD_TILES):
            held = [g for g in range(4) if 4 * b + g < REG_X]
            mask = jnp.zeros((TILE, LANES), F32)
            tiles = {}
            for g in held:
                src = inv[by * REG_X + 4 * b + g]
                own_at = pl.multiple_of(jnp.clip(src, 0, slots - 1) * TILE, TILE)
                came_at = pl.multiple_of(jnp.clip(src - slots, 0, MOVED - 1) * TILE, TILE)
                for kind, ref in ((0, s_ref), (1, q_ref)):
                    own = ref[pl.ds(own_at, TILE), :]
                    other = below(pl.multiple_of(kind * MOVED * TILE + came_at, TILE), TILE)
                    tiles[kind, g] = jnp.where(src >= slots, other, jnp.where(src >= 0, own, 0.0))
                mask = jnp.where(group == g, jnp.where(src >= 0, 1.0, 0.0), mask)
            for kind in range(2):
                for q in range(4):
                    value = jnp.zeros((TILE, LANES), F32)
                    for g in held:
                        value = jnp.where(group == g, turn(tiles[kind, g], BLOCK * (g - q), 1), value)
                    f_ref[kind, b, pl.ds(TILE + BLOCK * by + q, TILE, stride=4), :] = value
            for q in range(4):
                f_ref[2, b, pl.ds(TILE + BLOCK * by + TILE * q, TILE), :] = mask

    row16 = lax.broadcasted_iota(jnp.int32, (16, LANES), 0)
    group16 = lane_id((16, LANES)) // BLOCK

    def rim_rows(kind, rim, first):
        rolled = [turn(rim, BLOCK * d, 1) for d in range(4)]
        for q in range(4):
            value = jnp.zeros((16, LANES), F32)
            for g in range(4):
                value = jnp.where((row16 % 4 == g) & (group16 == g), rolled[(g - q) % 4], value)
            value = value + turn(value, -1, 0)
            value = value + turn(value, -2, 0)
            for b in range(FIELD_TILES):
                f_ref[kind, b, pl.ds(first + q, 1), :] = value[4 * b : 4 * b + 1, :]

    @pl.when(meta[1] > 0)
    def _():
        for kind, base in ((0, RIM_S), (1, RIM_Q), (2, RIM_M)):
            rim_rows(kind, below(base, 16) + far_ref[pl.ds(base - RIM_S, 16), :], 4)

    @pl.when(meta[1] < meta[2] - 1)
    def _():
        def own_rim(ref):
            rows = []
            for k in range(16):
                if k < REG_X:
                    src = inv[REGION + k]
                    at = jnp.maximum(src, 0) * TILE
                    line = jnp.ones((1, LANES), F32) if ref is None else ref[pl.ds(at, 1), :]
                    rows.append(jnp.where(src >= 0, line, 0.0))
                else:
                    rows.append(jnp.zeros((1, LANES), F32))
            return jnp.concatenate(rows, axis=0)

        for kind, base, ref in ((0, RIM_S, s_ref), (1, RIM_Q, q_ref), (2, RIM_M, None)):
            rim_rows(kind, above(base, 16) + own_rim(ref), FIELD_ROWS - TILE)

    height, width = surf_ref.shape
    for b in range(FIELD_TILES):
        lanes = min(LANES, width - b * LANES)
        f_ref[3, b, pl.ds(TILE, height), pl.ds(0, lanes)] = surf_ref[:, pl.ds(b * LANES, lanes)]
        f_ref[3, b, pl.ds(4, 4), :] = below(SURF + b * TILE, TILE)[4:]
        f_ref[3, b, pl.ds(FIELD_ROWS - TILE, 4), :] = above(SURF + b * TILE, TILE)[:4]

    lane = lane_id((TILE, LANES))
    last = width - (FIELD_TILES - 1) * LANES - 4
    east_even = meta[0] % 2 == 0
    for h in range(3):
        west_out = jnp.zeros((TILE, LANES), F32)
        east_out = jnp.zeros((TILE, LANES), F32)
        for g in range(8):
            v = 3 * g + h
            if v * TILE >= FIELD_ROWS:
                continue
            for kind in range(4):
                at = 16 * g + 4 * kind
                inside = (lane >= at) & (lane < at + 4)
                west = f_ref[kind, 0, pl.ds(v * TILE, TILE), :]
                east = f_ref[kind, FIELD_TILES - 1, pl.ds(v * TILE, TILE), :]
                west_out = jnp.where(inside, turn(west, at, 1), west_out)
                east_out = jnp.where(inside, turn(east, at - last, 1), east_out)
        ca_ref[pl.ds(h * TILE, TILE), :] = jnp.where(east_even, east_out, west_out)
        cb_ref[pl.ds(h * TILE, TILE), :] = jnp.where(east_even, west_out, east_out)


def region_fields(meta, places, s, q, a, b, far, surface):
    return pl.pallas_call(
        field_kernel,
        in_specs=[SMEM, SMEM] + [VMEM] * 6,
        out_specs=[VMEM] * 3,
        out_shape=[
            jax.ShapeDtypeStruct((4, FIELD_TILES, FIELD_ROWS, LANES), F32),
            jax.ShapeDtypeStruct((24, LANES), F32),
            jax.ShapeDtypeStruct((24, LANES), F32),
        ],
        compiler_params=pltpu.CompilerParams(vmem_limit_bytes=12 << 20),
        name="region_fields",
    )(meta, places, s, q, a, b, far, surface)


def basis_kernel(meta, came, f_ref, ca_ref, cb_ref, g_ref, blocks_ref, back_ref, u_ref):
    even = meta[0] % 2 == 0
    lane = lane_id((TILE, LANES))
    tiles = range(FIELD_TILES)
    fields = []
    for kind in range(4):
        parts = [f_ref[kind, b] for b in tiles]
        strip = []
        for v in range(FIELD_ROWS // TILE):
            g, h = v // 3, v % 3
            ca = ca_ref[pl.ds(h * TILE, TILE), :]
            cb = cb_ref[pl.ds(h * TILE, TILE), :]
            at = 16 * g + 4 * kind
            west = turn(jnp.where(even, cb, ca), 124 - at, 1)
            east = turn(jnp.where(even, ca, cb), 64 - at, 1)
            tile = f_ref[kind, FIELD_TILES - 1, pl.ds(v * TILE, TILE), :]
            tile = jnp.where((lane >= 64) & (lane < 68), east, tile)
            strip.append(jnp.where(lane >= 124, west, tile))
        parts[-1] = jnp.concatenate(strip, axis=0)
        fields.append(parts)
    depth, inner, mask, surf = fields
    wide = lane_id((FIELD_ROWS, LANES))

    def sides(v):
        fwd = [turn(x, 1, 1) for x in v]
        bwd = [turn(x, -1, 1) for x in v]
        out = []
        for b in tiles:
            left = jnp.where(wide == 0, fwd[b - 1], fwd[b])
            right = jnp.where(wide == LANES - 1, bwd[(b + 1) % FIELD_TILES], bwd[b])
            out.append(left + right)
        return out

    def rows(v):
        return [turn(x, 1, 0) + turn(x, -1, 0) for x in v]

    def spread(v):
        side = sides(v)
        both = rows([v[b] + 0.5 * side[b] for b in tiles])
        return [mask[b] * (side[b] + both[b]) for b in tiles]

    def edges(v):
        side, both = sides(v), rows(v)
        return [side[b] + both[b] for b in tiles]

    near, count = edges(inner), edges(mask)
    rhs = [mask[b] * (depth[b] + near[b] - count[b] * inner[b]) for b in tiles]
    scale = [1.0 / (6.0 + surf[b]) for b in tiles]
    u0 = [rhs[b] * scale[b] for b in tiles]
    z1 = spread(u0)
    u1 = [z1[b] * scale[b] for b in tiles]
    z2 = spread(u1)
    u2 = [z2[b] * scale[b] for b in tiles]
    z3 = spread(u2)
    rows_in = slice(TILE, FIELD_ROWS - TILE)

    def dot(x, y):
        total = jnp.zeros((TILE, LANES), F32)
        for b in tiles:
            p = x[b][rows_in] * y[b][rows_in]
            p = jnp.sum(p.reshape(-1, TILE, LANES), axis=0)
            if b == FIELD_TILES - 1:
                p = jnp.where(lane < 64, p, 0.0)
            total = total + p
        return jnp.sum(jnp.sum(total, axis=1, keepdims=True), axis=0, keepdims=True)

    row = jnp.zeros((1, LANES), F32)
    pairs = ((u0, rhs), (u0, z1), (u1, z1), (u1, z2), (u2, z2), (u2, z3))
    for k, (x, y) in enumerate(pairs):
        row = jnp.where(lane[:1] == k, dot(x, y), row)
    row = jnp.where(lane[:1] == 6, meta[3].astype(F32), row)
    g_ref[...] = jnp.broadcast_to(row, g_ref.shape)
    for k, u in enumerate((u0, u1, u2)):
        for b in tiles:
            u_ref[k, b] = u[b][rows_in]
    group = lane // BLOCK
    for k in range(3):
        for by in range(REG_Y):
            for b in tiles:
                value = [u_ref[k, b, pl.ds(BLOCK * by + q, TILE, stride=4), :] for q in range(4)]
                for g in range(4):
                    if 4 * b + g >= REG_X:
                        continue
                    tile = value[0]
                    for q in range(4):
                        part = turn(value[q], BLOCK * (q - g), 1)
                        tile = part if q == 0 else jnp.where(group == q, part, tile)
                    blocks_ref[pl.ds((k * REGION + by * REG_X + 4 * b + g) * TILE, TILE), :] = tile
    first = came.shape[0] - MOVED
    for m in range(MOVED):
        at = pl.multiple_of(jnp.maximum(came[first + m] - REGION, 0) * TILE, TILE)
        for k in range(3):
            tile = blocks_ref[pl.ds(k * REGION * TILE + at, TILE), :]
            back_ref[pl.ds((k * MOVED + m) * TILE, TILE), :] = tile


def solve_basis(meta, came, fields, ca, cb, devices):
    return pl.pallas_call(
        basis_kernel,
        in_specs=[SMEM, SMEM, VMEM, VMEM, VMEM],
        out_specs=[VMEM] * 3,
        out_shape=[
            jax.ShapeDtypeStruct((devices, LANES), F32),
            jax.ShapeDtypeStruct((3 * REGION * TILE, LANES), F32),
            jax.ShapeDtypeStruct((3 * MOVED * TILE, LANES), F32),
        ],
        scratch_shapes=[pltpu.VMEM((3, FIELD_TILES, FIELD_ROWS - 2 * TILE, LANES), F32)],
        compiler_params=pltpu.CompilerParams(vmem_limit_bytes=24 << 20),
        name="solve_basis",
    )(meta, came, fields, ca, cb)


def pressure_kernel(code, g_ref, blocks_ref, back_ref, held_ref, out_ref, same_ref, work):
    del held_ref, same_ref
    slots = out_ref.shape[0]
    total = jnp.sum(g_ref[...].reshape(-1, TILE, LANES), axis=0)
    total = jnp.broadcast_to(jnp.sum(total, axis=0, keepdims=True), (TILE, LANES))
    lane = lane_id((TILE, LANES))
    pick = lambda k: jnp.sum(jnp.where(lane == k, total, 0.0), axis=1, keepdims=True)
    g = [pick(k) for k in range(6)]
    g = [x / g[0] for x in g]
    a = [g[k] - g[k + 1] for k in range(5)]
    zero = jnp.zeros_like(g[0])
    one = zero + 1.0

    def form(v, m):
        out = zero
        for i in range(3):
            for k in range(3):
                out = out + v[i] * v[k] * m[i + k]
        return out

    coef = [zero, zero, zero]
    rho = [one, zero, zero]
    way = [one, zero, zero]
    norm = g[0]
    for iteration in range(ITERS):
        length = norm / form(way, a)
        coef = [coef[k] + length * way[k] for k in range(3)]
        if iteration + 1 < ITERS:
            moved = [way[0], way[1] - way[0], way[2] - way[1]]
            rho = [rho[k] - length * moved[k] for k in range(3)]
            norm_next = form(rho, g)
            way = [rho[k] + (norm_next / norm) * way[k] for k in range(3)]
            norm = norm_next
    coef = [jnp.broadcast_to(c, (TILE, LANES)) for c in coef]
    for s in range(slots):
        c = code[s]
        at = pl.multiple_of(jnp.where(c < REGION, c, 0) * TILE, TILE)
        tiles = [blocks_ref[pl.ds(k * REGION * TILE + at, TILE), :] for k in range(3)]
        m = s - (slots - MOVED)
        if m >= 0:
            for k in range(3):
                other = back_ref[pl.ds((k * MOVED + m) * TILE, TILE), :]
                tiles[k] = jnp.where(c < REGION, tiles[k], other)
        work[pl.ds(s * TILE, TILE), :] = coef[0] * tiles[0] + coef[1] * tiles[1] + coef[2] * tiles[2]
    for first in range(0, slots, TILE):
        size = min(TILE, slots - first)
        for c in range(TILE):
            lines = work[pl.ds(first * TILE + c, size, stride=TILE), :]
            out_ref[pl.ds(first, size), pl.ds(c * LANES, LANES)] = lines


def slot_pressure(code, sums, blocks, back, held):
    slots = code.shape[0]
    return pl.pallas_call(
        pressure_kernel,
        in_specs=[SMEM, VMEM, VMEM, VMEM, ANY],
        out_specs=[VMEM, ANY],
        out_shape=[
            jax.ShapeDtypeStruct((slots, TILE * LANES), F32),
            jax.ShapeDtypeStruct(held.shape, F32),
        ],
        scratch_shapes=[pltpu.VMEM((slots * TILE, LANES), F32)],
        input_output_aliases={4: 1},
        compiler_params=pltpu.CompilerParams(vmem_limit_bytes=12 << 20),
        name="slot_pressure",
    )(code, sums, blocks, back, held)


def columns_kernel(meta, inv, t_ref, after_ref, a_ref, b_ref, west, east, sems):
    del after_ref
    even = meta[0] % 2 == 0
    count = 2 * REG_Y

    def copies(k):
        w, e = inv[REG_X * k], inv[REG_X * k + REG_X - 1]
        cw = pltpu.make_async_copy(t_ref.at[jnp.maximum(w, 0)], west.at[k], sems.at[0, k])
        ce = pltpu.make_async_copy(t_ref.at[jnp.maximum(e, 0)], east.at[k], sems.at[1, k])
        return cw, ce

    for k in range(count):
        for c in copies(k):
            c.start()
    for k in range(count):
        for c in copies(k):
            c.wait()
    column = lane_id((ROWS, LANES)) % BLOCK
    for level in range(HALF):
        out_w = jnp.zeros((ROWS, LANES), F32)
        out_e = jnp.zeros((ROWS, LANES), F32)
        for k in range(count):
            has_w, has_e = inv[REG_X * k] >= 0, inv[REG_X * k + REG_X - 1] >= 0
            for part in range(2):
                lane = k + 16 * part
                here = column == lane
                at = level + HALF * part
                out_w = jnp.where(here & has_w, turn(west[k, at], lane, 1), out_w)
                out_e = jnp.where(here & has_e, turn(east[k, at], lane - (BLOCK - 1), 1), out_e)
        a_ref[pl.ds(level * ROWS, ROWS), :] = jnp.where(even, out_e, out_w)
        b_ref[pl.ds(level * ROWS, ROWS), :] = jnp.where(even, out_w, out_e)


def column_strips(meta, places, view, after):
    count = 2 * REG_Y
    return pl.pallas_call(
        columns_kernel,
        in_specs=[SMEM, SMEM, ANY, ANY],
        out_specs=[VMEM] * 2,
        out_shape=[jax.ShapeDtypeStruct((HALF * ROWS, LANES), F32)] * 2,
        scratch_shapes=[
            pltpu.VMEM((count, LEVELS, ROWS, LANES), F32),
            pltpu.VMEM((count, LEVELS, ROWS, LANES), F32),
            pltpu.SemaphoreType.DMA((2, count)),
        ],
        compiler_params=pltpu.CompilerParams(vmem_limit_bytes=12 << 20),
        name="column_strips",
    )(meta, places, view, after)


def links_kernel(meta, table, t_ref, ga_ref, gb_ref, a_ref, b_ref, whole, half, sem_we, sem_ns):
    even_x = meta[0] % 2 == 0
    even_y = meta[1] % 2 == 0

    def we_copy(way, k):
        link = jnp.maximum(table[way * (CAP_WE + CAP_NS) + k], 0)
        return pltpu.make_async_copy(t_ref.at[link // 4], whole.at[way, k], sem_we.at[way, k])

    def ns_copy(way, k):
        link = jnp.maximum(table[way * (CAP_WE + CAP_NS) + CAP_WE + k], 2)
        rows = pl.ds(pl.multiple_of((link % 4 - 2) * TILE, TILE), TILE)
        return pltpu.make_async_copy(t_ref.at[link // 4, :, rows, :], half.at[way, k], sem_ns.at[way, k])

    for way in range(2):
        for k in range(CAP_WE):
            @pl.when(table[way * (CAP_WE + CAP_NS) + k] >= 0)
            def _():
                we_copy(way, k).start()

        for k in range(CAP_NS):
            @pl.when(table[way * (CAP_WE + CAP_NS) + CAP_WE + k] >= 0)
            def _():
                ns_copy(way, k).start()

    column = lane_id((HALF * ROWS, LANES)) % 16
    from_west = jnp.where(even_x, gb_ref[...], ga_ref[...])
    from_east = jnp.where(even_x, ga_ref[...], gb_ref[...])
    ways = ((turn(from_west, -5, 1), from_east), (from_west, turn(from_east, 5, 1)))
    relays = [jnp.where(column < 5, w, jnp.where(column < RELAY, e, 0.0)) for w, e in ways]

    def message(way, out):
        out[pl.ds(0, HALF * ROWS), :] = relays[way]
        out[pl.ds(HALF * ROWS, (LEVELS + 1) * TILE), :] = jnp.zeros(((LEVELS + 1) * TILE, LANES), F32)
        lane32 = lane_id((ROWS, LANES)) % BLOCK
        for k in range(CAP_WE):
            link = table[way * (CAP_WE + CAP_NS) + k]

            @pl.when(link >= 0)
            def _():
                we_copy(way, k).wait()
                start = (link % 4) * (BLOCK - 1)
                for level in range(HALF):
                    at = pl.ds(level * ROWS, ROWS)
                    value = out[at, :]
                    for part in range(2):
                        lane = RELAY + k + 16 * part
                        x = turn(whole[way, k, level + HALF * part], lane, 1)
                        x = jnp.where(start > 0, turn(x, 1 - BLOCK, 1), x)
                        value = jnp.where(lane32 == lane, x, value)
                    out[at, :] = value

        row = lax.broadcasted_iota(jnp.int32, (LEVELS, TILE, LANES), 1)
        group = lane_id((LEVELS, TILE, LANES)) // BLOCK
        base = HALF * ROWS
        for k in range(CAP_NS):
            link = table[way * (CAP_WE + CAP_NS) + CAP_WE + k]

            @pl.when(link >= 0)
            def _():
                ns_copy(way, k).wait()
                x = half[way, k]

                def put(x):
                    keep = (row // 2 == k // 4) & (group == k % 4)
                    old = out[pl.ds(base, LEVELS * TILE), :].reshape(LEVELS, TILE, LANES)
                    new = jnp.where(keep, x, old)
                    out[pl.ds(base, LEVELS * TILE), :] = new.reshape(LEVELS * TILE, LANES)

                @pl.when(link % 4 == 2)
                def _():
                    put(turn(turn(x, 2 * (k // 4), 1), BLOCK * (k % 4), 2))

                @pl.when(link % 4 == 3)
                def _():
                    put(turn(turn(x, 2 * (k // 4) + 2, 1), BLOCK * (k % 4) + BLOCK, 2))

    @pl.when(even_y)
    def _():
        message(0, a_ref)
        message(1, b_ref)

    @pl.when(jnp.logical_not(even_y))
    def _():
        message(0, b_ref)
        message(1, a_ref)


def link_strips(meta, table, view, ga, gb):
    rows = LINK_ROWS
    return pl.pallas_call(
        links_kernel,
        in_specs=[SMEM, SMEM, ANY, VMEM, VMEM],
        out_specs=[VMEM] * 2,
        out_shape=[jax.ShapeDtypeStruct((rows, LANES), F32)] * 2,
        scratch_shapes=[
            pltpu.VMEM((2, CAP_WE, LEVELS, ROWS, LANES), F32),
            pltpu.VMEM((2, CAP_NS, LEVELS, TILE, LANES), F32),
            pltpu.SemaphoreType.DMA((2, CAP_WE)),
            pltpu.SemaphoreType.DMA((2, CAP_NS)),
        ],
        compiler_params=pltpu.CompilerParams(vmem_limit_bytes=12 << 20),
        name="link_strips",
    )(meta, table, view, ga, gb)


IMAGE = LEVELS * ROWS
FIELDS = 5
BOX_LOW = 2 * HALF * ROWS
BOX_HIGH = BOX_LOW + LINK_ROWS
BOX = BOX_HIGH + LINK_ROWS


def tracer_kernel(meta, table, need, diffusion, t_ref, ga_ref, gb_ref, ha_ref, hb_ref, out_ref, own, up, down, box, seen, sems):
    step = pl.program_id(0)
    slots = own.shape[0] // IMAGE
    chunk = STEP_SLOTS * IMAGE
    chunks = slots // STEP_SLOTS

    def fetch(c):
        rows = pl.ds(pl.multiple_of(c * chunk, TILE), chunk)
        return pltpu.make_async_copy(t_ref.at[rows], own.at[rows], sems.at[c])

    @pl.when(step == 0)
    def _():
        for c in range(chunks):
            fetch(c).start()
        seen[0] = 0
        even_x = meta[0] % 2 == 0
        even_y = meta[1] % 2 == 0
        land = pl.ds(TILE + slots * IMAGE - TILE, IMAGE + 2 * TILE)
        up[land, :] = jnp.zeros((IMAGE + 2 * TILE, LANES), F32)
        down[land, :] = jnp.zeros((IMAGE + 2 * TILE, LANES), F32)
        for first, second, size, low, high in (
            (ga_ref, gb_ref, HALF * ROWS, 0, HALF * ROWS),
            (ha_ref, hb_ref, LINK_ROWS, BOX_LOW, BOX_HIGH),
        ):
            even = even_x if low == 0 else even_y
            box[pl.ds(low, size), :] = jnp.where(even, second[...], first[...])
            box[pl.ds(high, size), :] = jnp.where(even, first[...], second[...])

    def arrive(c, carry):
        fetch(c).wait()

        def roll_slot(n, carry):
            base = pl.multiple_of((c * STEP_SLOTS + n) * IMAGE, TILE)
            for level in range(LEVELS):
                x = own[pl.ds(base + level * ROWS, ROWS), :]
                up[pl.ds(base + TILE + level * ROWS, ROWS), :] = pltpu.roll(x, BLOCK, 1)
                down[pl.ds(base + TILE + level * ROWS, ROWS), :] = pltpu.roll(x, LANES - BLOCK, 1)
            return carry

        return lax.fori_loop(0, STEP_SLOTS, roll_slot, carry)

    upto = jnp.maximum(seen[0], need[step] + 1)
    lax.fori_loop(seen[0], upto, arrive, 0)
    seen[0] = upto

    cells = (ROWS, LANES)
    lane = lane_id(cells)
    column = lane % BLOCK
    row = lax.broadcasted_iota(jnp.int32, cells, 0)
    row8 = row[:TILE]
    edge = (
        jnp.where(column == 0, 1.0, 0.0),
        jnp.where(column == BLOCK - 1, 1.0, 0.0),
        jnp.where((row < 2) & (lane < BLOCK), 1.0, 0.0),
        jnp.where((row >= ROWS - 2) & (lane >= LANES - BLOCK), 1.0, 0.0),
    )

    def one_slot(n, carry):
        s = step * STEP_SLOTS + n
        entry = [[table[(s * 4 + t) * FIELDS + f] for f in range(FIELDS)] for t in range(4)]
        count = jnp.full(cells, 4.0, F32)
        for t in range(4):
            count = count - edge[t] * entry[t][4].astype(F32)
        base = pl.multiple_of(s * IMAGE, TILE)
        west, east, south, north = [pl.multiple_of(entry[t][0] * IMAGE, TILE) + TILE for t in range(4)]

        for t, dest in ((0, down), (1, up)):
            @pl.when(entry[t][1] == 1)
            def _():
                first, by = pl.multiple_of(entry[t][2], TILE), entry[t][3]
                for level in range(LEVELS):
                    part = level // HALF
                    x = box[pl.ds(first + (level % HALF) * ROWS, ROWS), :]
                    x = pltpu.roll(x, (by + LANES - 16 * part) % LANES, 1)
                    dest[pl.ds(TILE + (slots + 1) * IMAGE + level * ROWS, ROWS), :] = x

        for t, dest, offset in ((2, up, ROWS - 2), (3, down, -6)):
            @pl.when(entry[t][1] == 1)
            def _():
                first, by = entry[t][2], entry[t][3]
                for level in range(LEVELS):
                    x = pltpu.roll(box[pl.ds(first + level * TILE, TILE), :], by, 1)
                    dest[pl.ds(TILE + (slots + 3) * IMAGE + level * ROWS + offset, TILE), :] = x

        for level in range(LEVELS):
            at = level * ROWS
            x = own[pl.ds(base + at, ROWS), :]
            under = up[pl.ds(base + TILE + at - 2, ROWS), :]
            over = down[pl.ds(base + TILE + at + 2, ROWS), :]
            low = up[pl.ds(south + at + ROWS - 2, TILE), :]
            high = down[pl.ds(north + at - 6, TILE), :]
            under = jnp.concatenate([jnp.where(row8 < 2, low, under[:TILE]), under[TILE:]], axis=0)
            over = jnp.concatenate([over[:TILE], jnp.where(row8 >= TILE - 2, high, over[TILE:])], axis=0)
            total = jnp.where(lane < BLOCK, under, up[pl.ds(base + TILE + at, ROWS), :])
            total = total + jnp.where(lane >= LANES - BLOCK, over, down[pl.ds(base + TILE + at, ROWS), :])
            w = down[pl.ds(west + at, ROWS), :]
            e = up[pl.ds(east + at, ROWS), :]
            total = total + pltpu.roll(jnp.where(column == BLOCK - 1, w, x), 1, 1)
            total = total + pltpu.roll(jnp.where(column == 0, e, x), LANES - 1, 1)
            out_ref[pl.ds(pl.multiple_of(n * IMAGE, TILE) + at, ROWS), :] = x + diffusion[level] * (total - count * x)
        return carry

    lax.fori_loop(0, STEP_SLOTS, one_slot, 0)

    @pl.when(step == pl.num_programs(0) - 1)
    def _():
        lax.fori_loop(seen[0], chunks, arrive, 0)


def step_tracers(meta, table, need, diffusion, view, ga, gb, ha, hb):
    slots = view.shape[0]
    steps = slots // STEP_SLOTS
    rows = slots * IMAGE
    out = pl.pallas_call(
        tracer_kernel,
        grid=(steps,),
        in_specs=[SMEM] * 4 + [ANY] + [VMEM] * 4,
        out_specs=pl.BlockSpec((STEP_SLOTS * IMAGE, LANES), lambda s: (s, 0)),
        out_shape=jax.ShapeDtypeStruct((rows, LANES), F32),
        scratch_shapes=[
            pltpu.VMEM((rows, LANES), F32),
            pltpu.VMEM((rows + 4 * IMAGE + 2 * TILE, LANES), F32),
            pltpu.VMEM((rows + 4 * IMAGE + 2 * TILE, LANES), F32),
            pltpu.VMEM((BOX, LANES), F32),
            pltpu.SMEM((1,), jnp.int32),
            pltpu.SemaphoreType.DMA((steps,)),
        ],
        compiler_params=pltpu.CompilerParams(vmem_limit_bytes=44 << 20),
        cost_estimate=pl.CostEstimate(flops=14 * rows * LANES, bytes_accessed=8 * rows * LANES, transcendentals=0),
        name="step_tracers",
    )(meta, table, need, diffusion, view.reshape(rows, LANES), ga, gb, ha, hb)
    return out.reshape(view.shape)


def with_halo(block, sides, width):
    for axis, dim in sides:
        low = shifted(lax.slice_in_dim(block, block.shape[dim] - width, None, axis=dim), axis, 1)
        high = shifted(lax.slice_in_dim(block, 0, width, axis=dim), axis, -1)
        block = jnp.concatenate([low, block, high], axis=dim)
    return block


def edge_strips(grid):
    sides = [grid[..., :, 0], grid[..., :, -1], grid[..., 0, :], grid[..., -1, :]]
    return jnp.stack(sides, axis=1).reshape(grid.shape[0] * 4, -1)


def general_step(tracers, diffusion, halo_source):
    slots = tracers.shape[0]
    grid = tracers.reshape(slots, TRACER, LEVELS, BLOCK, BLOCK)
    strips = edge_strips(grid)
    width = strips.shape[1]
    count_gx, count_gy = lax.axis_size("gx"), lax.axis_size("gy")
    source = halo_source.reshape(-1)
    missing = source >= 4 * slots * count_gx * count_gy
    slot = jnp.where(missing, 0, source) // 4
    owner = slot // slots
    step_gx = (owner // count_gy - lax.axis_index("gx") + count_gx + 1) % count_gx
    step_gy = (owner % count_gy - lax.axis_index("gy") + count_gy + 1) % count_gy
    every = slots * 4
    table = with_halo(strips.reshape(1, 1, every, width), (("gx", 0), ("gy", 1)), 1).reshape(9 * every, width)
    index = (step_gx * 3 + step_gy) * every + slot % slots * 4 + source % 4
    halo = jnp.take(table, jnp.where(missing, 0, index), axis=0, mode="clip")
    halo = halo.reshape(slots, 4, TRACER, LEVELS, BLOCK)
    gate = jnp.where(missing, 0.0, 1.0).astype(F32).reshape(slots, 4, 1, 1, 1)
    inner_x = grid[..., :, :-1] - grid[..., :, 1:]
    inner_y = grid[..., :-1, :] - grid[..., 1:, :]
    west = (halo[:, 0] - grid[..., :, 0]) * gate[:, 0]
    east = (halo[:, 1] - grid[..., :, -1]) * gate[:, 1]
    south = (halo[:, 2] - grid[..., 0, :]) * gate[:, 2]
    north = (halo[:, 3] - grid[..., -1, :]) * gate[:, 3]
    laplace = (
        jnp.concatenate([west[..., None], inner_x], axis=-1)
        + jnp.concatenate([-inner_x, east[..., None]], axis=-1)
        + jnp.concatenate([south[..., None, :], inner_y], axis=-2)
        + jnp.concatenate([-inner_y, north[..., None, :]], axis=-2)
    )
    updated = grid + diffusion[None, None, :, None, None] * laplace
    return plain(seen_by_rows(updated.reshape(tracers.shape)))


def strip_tables(halo_source, code, at_x, at_y, count_x, count_y):
    slots = halo_source.shape[0]
    source = halo_source
    missing = source >= 4 * slots * count_x * count_y
    source = jnp.where(missing, 0, source)
    owner = source // (4 * slots)
    local_slot = source // 4 - owner * slots
    same_x = owner // count_y == at_x
    owner_y = owner % count_y
    up = owner_y == (at_y + 1) % count_y
    down = owner_y == (at_y + count_y - 1) % count_y
    here = owner_y == at_y
    side = lax.broadcasted_iota(jnp.int32, (slots, 4), 1)
    index = lax.broadcasted_iota(jnp.int32, (slots, 4), 0) * 4 + side
    kind = jnp.where(side >= 2, 1, 0)
    linked = ~missing & same_x & ~here
    group = jnp.where(linked, jnp.where(up, kind, 2 + kind), -1)

    def rank(key):
        flat_key, flat_group = key.reshape(-1), group.reshape(-1)
        before = (flat_key[None, :] < flat_key[:, None]) & (flat_group[None, :] == flat_group[:, None])
        return jnp.sum(before.astype(jnp.int32), axis=1).reshape(slots, 4)

    take = rank(index)
    give = rank(source)
    entries = []
    for way in range(2):
        entries += [(way * 2, k) for k in range(CAP_WE)] + [(way * 2 + 1, k) for k in range(CAP_NS)]
    want = jnp.asarray([g * 1024 + k for g, k in entries], jnp.int32)
    has = jnp.where(group >= 0, group * 1024 + give, -1).reshape(-1)
    hit = want[:, None] == has[None, :]
    send = jnp.sum(jnp.where(hit, index.reshape(-1)[None, :] + 1, 0), axis=1) - 1
    over = jnp.any(linked & (take >= jnp.where(kind == 1, CAP_NS, CAP_WE)))
    row = (code // REG_X)[:, None]
    local = same_x & here
    north = kind == 1
    lane = jnp.where(same_x, RELAY + take, jnp.where(here, row, row % REG_Y + jnp.where(side == 0, 0, REG_Y)))
    beside = jnp.where(side == 0, 0, HALF * ROWS)
    along = jnp.where(up, BOX_HIGH, BOX_LOW)
    box_we = jnp.where(same_x | ~here, along, beside)
    by_we = jnp.where(side == 0, -1, BLOCK) - lane
    box_ns = along + HALF * ROWS + 2 * jnp.minimum(take // 4, TILE // 2 - 1) - jnp.where(side == 3, TILE - 2, 0)
    by_ns = jnp.where(side == 3, LANES - BLOCK, 0) - BLOCK * (take % 4)
    remote = ~missing & ~local
    image = jnp.where(missing, slots, jnp.where(local, local_slot, slots + 1 + 2 * kind))
    at = jnp.where(remote, jnp.where(north, box_ns, box_we), 0)
    by = jnp.where(remote, jnp.where(north, by_ns, by_we), 0) % LANES
    fields = [image, remote.astype(jnp.int32), at, by, missing.astype(jnp.int32)]
    table = jnp.stack(fields, axis=-1).reshape(-1)
    last = jnp.where(local & ~missing, local_slot, 0)
    last = jnp.maximum(jnp.max(last, axis=1), jnp.arange(slots))
    need = jnp.max(last.reshape(-1, STEP_SLOTS), axis=1) // STEP_SLOTS
    return table, need, send, over.astype(jnp.int32)


def on_device(tracers, diffusion, layer_weight, surface_term, clinic_blocks, halo_source):
    slots = tracers.shape[0]
    count_x, count_y = lax.axis_size("gx"), lax.axis_size("gy")
    at_x, at_y = lax.axis_index("gx"), lax.axis_index("gy")
    grid_columns = REG_X * count_x
    grid_rows = REG_Y * count_y
    own_row = (clinic_blocks // grid_columns - REG_Y * at_y) % grid_rows
    code = own_row * REG_X + clinic_blocks % grid_columns % REG_X
    came = shifted(code, "gy", 1)
    zero = jnp.zeros((), jnp.int32)
    meta = jnp.stack([at_x, at_y, zero + count_y, zero]).astype(jnp.int32)
    spot = jnp.arange(2 * REGION, dtype=jnp.int32)[:, None]
    index = jnp.arange(slots, dtype=jnp.int32)[None, :]
    places = jnp.sum(jnp.where(code[None, :] == spot, index + 1, 0), axis=1) - 1

    view = seen_by_rows(tracers)
    s, q, a, b, far = depth_sums(view, meta, places, layer_weight, diffusion, surface_term)
    ra, rb = swap(a, b, "gy", count_y)
    rfar = shifted(far, "gy", 2)

    table, need, send, over = strip_tables(halo_source, code, at_x, at_y, count_x, count_y)
    ga, gb = swap(*column_strips(meta, places, view, far), "gx", count_x)

    moved = (came[None, :] - REGION == spot) & (came[None, :] >= REGION)
    both = places + jnp.sum(jnp.where(moved, index + 1 + MOVED, 0), axis=1)
    fields, ca, cb = region_fields(meta, both, s, q, ra, rb, rfar, surface_term)
    ca, cb = swap(ca, cb, "gx", count_x)
    ha, hb = swap(*link_strips(meta, send, view, ga, gb), "gy", count_y)

    meta_over = jnp.stack([at_x, at_y, zero + count_y, over]).astype(jnp.int32)
    sums, blocks, back = solve_basis(meta_over, came, fields, ca, cb, count_x * count_y)
    back = shifted(back, "gy", -1)
    sums = lax.all_to_all(sums[:, None], ("gx", "gy"), 0, 0, tiled=True)
    updated = step_tracers(meta, table, need, diffusion, view, ga, gb, ha, hb)
    updated = lax.cond(
        jnp.max(sums[:, 0, 6]) > 0.0,
        lambda fast: general_step(tracers, diffusion, halo_source),
        lambda fast: fast,
        updated,
    )
    pressure, updated = slot_pressure(code, sums.reshape(-1, LANES), blocks, back, updated)
    updated = updated.reshape(slots, LEVELS, TILE, TRACER, LANES).transpose(0, 3, 1, 2, 4)
    return (updated.reshape(tracers.shape), pressure)


def solution(mesh):
    placed = (
        P(("gx", "gy"), None, None, None),
        P(),
        P(),
        P("gy", "gx"),
        P(("gx", "gy")),
        P(("gx", "gy"), None),
    )
    return jax.shard_map(
        on_device,
        mesh=mesh,
        in_specs=placed,
        out_specs=(P(("gx", "gy"), None, None, None), P(("gx", "gy"), None)),
        check_vma=False,
    )
```

```python
import jax
import jax.numpy as jnp
from jax import lax
from jax.experimental import pallas as pl
from jax.experimental.layout import Layout, with_layout_constraint
from jax.experimental.pallas import tpu as pltpu
from jax.sharding import PartitionSpec as P

BLOCK = 32
LEVELS = 20
TRACER = 2
REG_X = 14
REG_Y = 5
ITERS = 3
REGION = REG_X * REG_Y
MOVED = 22
LANES = 128
TILE = 8
ROWS = 16
HALF = LEVELS // 2
STEP_SLOTS = 7
IMAGE = LEVELS * ROWS
FIELD_ROWS = 176
FIELD_TILES = 4
CAP_WE = 6
CAP_NS = 16
RELAY = 10
LINK_ROWS = HALF * ROWS + (LEVELS + 1) * TILE
RIM_S = 2 * MOVED * TILE
RIM_Q = RIM_S + 16
RIM_M = RIM_Q + 16
SURF = RIM_M + 16
IDS = SURF + FIELD_TILES * TILE
MESSAGE = IDS + TILE
F32 = jnp.float32
SMEM = pl.BlockSpec(memory_space=pltpu.SMEM)
VMEM = pl.BlockSpec(memory_space=pltpu.VMEM)
ANY = pl.BlockSpec(memory_space=pl.ANY)
HBM = pl.BlockSpec(memory_space=pltpu.HBM)


def lane_id(shape):
    return lax.broadcasted_iota(jnp.int32, shape, len(shape) - 1)


def turn(x, by, axis):
    size = x.shape[axis]
    if isinstance(by, int):
        by = by % size
        if by == 0:
            return x
    return pltpu.roll(x, by, axis)


def swap(to_next, to_last, axis, count):
    first = [(i, i ^ 1) for i in range(count)]
    second = [(i, (i + 1) % count if i % 2 else (i - 1) % count) for i in range(count)]
    return lax.ppermute(to_next, axis, first), lax.ppermute(to_last, axis, second)


def plain(x):
    return with_layout_constraint(x, Layout(major_to_minor=tuple(range(x.ndim))))


def seen_by_rows(tracers):
    slots = tracers.shape[0]
    view = tracers.reshape(slots, TRACER, LEVELS, TILE, LANES).transpose(0, 2, 3, 1, 4)
    return view.reshape(slots, LEVELS, ROWS, LANES)


def shifted(x, axis, by):
    length = lax.axis_size(axis)
    return lax.ppermute(x, axis, [(i, (i + by) % length) for i in range(length)])


def sums_kernel(meta, code, weight, diffusion, t_ref, surf_ref, s_ref, q_ref, a_ref, b_ref, far_ref, inv, own, part, edges, sems, sem_low, sem_high):
    slots = own.shape[0]
    chunks = slots // STEP_SLOTS
    height = surf_ref.shape[0]

    def fetch(c):
        part = pl.ds(c * STEP_SLOTS, STEP_SLOTS)
        return pltpu.make_async_copy(t_ref.at[part], own.at[part], sems.at[c])

    def fetch_low():
        return pltpu.make_async_copy(surf_ref.at[pl.ds(0, TILE), :], edges.at[0], sem_low)

    def fetch_high():
        return pltpu.make_async_copy(surf_ref.at[pl.ds(height - TILE, TILE), :], edges.at[1], sem_high)

    for c in range(chunks):
        fetch(c).start()
    fetch_low().start()
    fetch_high().start()
    for r in range(2 * REGION):
        inv[r] = -1
    for s in range(slots):
        inv[code[s]] = s
    tracer = lax.broadcasted_iota(jnp.int32, (TILE, LANES), 0) % 2
    pairs = [(n, h) for n in range(STEP_SLOTS) for h in range(2)]

    def sum_chunk(c, carry):
        fetch(c).wait()
        acc_s = {p: jnp.zeros((TILE, LANES), F32) for p in pairs}
        acc_q = {p: jnp.zeros((TILE, LANES), F32) for p in pairs}
        for level in range(LEVELS):
            w = jnp.where(tracer == 0, weight[0, level], weight[1, level])
            wd = w * diffusion[level]
            for n, h in pairs:
                x = own[c * STEP_SLOTS + n, pl.ds(level * ROWS + h * TILE, TILE), :]
                acc_s[n, h] = acc_s[n, h] + w * x
                acc_q[n, h] = acc_q[n, h] + wd * x
        for n, h in pairs:
            part[0, pl.ds(n * ROWS + h * TILE, TILE), :] = acc_s[n, h]
            part[1, pl.ds(n * ROWS + h * TILE, TILE), :] = acc_q[n, h]
        for n in range(STEP_SLOTS):
            row = pl.multiple_of((c * STEP_SLOTS + n) * TILE, TILE)
            for kind, out in ((0, s_ref), (1, q_ref)):
                even = part[kind, pl.ds(n * ROWS, TILE, stride=2), :]
                odd = part[kind, pl.ds(n * ROWS + 1, TILE, stride=2), :]
                out[pl.ds(row, TILE), :] = even + odd
        return carry

    lax.fori_loop(0, chunks, sum_chunk, 0)
    fetch_low().wait()
    fetch_high().wait()

    def rim(dest, base, first, chunk):
        for k in range(REG_X):
            src = inv[first + k]
            at = jnp.maximum(src, 0) * TILE + chunk
            has = jnp.where(src >= 0, 1.0, 0.0)
            dest[pl.ds(base + k, 1), :] = jnp.where(src >= 0, s_ref[pl.ds(at, 1), :], 0.0)
            dest[pl.ds(base + 16 + k, 1), :] = jnp.where(src >= 0, q_ref[pl.ds(at, 1), :], 0.0)
            dest[pl.ds(base + 32 + k, 1), :] = jnp.full((1, LANES), has, F32)
        for k in range(REG_X, 16):
            for kind in range(3):
                dest[pl.ds(base + 16 * kind + k, 1), :] = jnp.zeros((1, LANES), F32)

    def surface(dest, edge):
        for b in range(FIELD_TILES):
            if b < 3:
                dest[pl.ds(SURF + b * TILE, TILE), :] = edges[edge, :, pl.ds(b * LANES, LANES)]
            else:
                width = edges.shape[2] - b * LANES
                dest[pl.ds(SURF + b * TILE, TILE), :] = jnp.zeros((TILE, LANES), F32)
                dest[pl.ds(SURF + b * TILE, TILE), pl.ds(0, width)] = edges[edge, :, pl.ds(b * LANES, width)]

    lane = lane_id((TILE, LANES))
    ids = jnp.full((TILE, LANES), -1.0, F32)
    for k in range(MOVED):
        ids = jnp.where(lane == k, (code[slots - MOVED + k] - REGION).astype(F32), ids)

    def messages(up, down):
        height = MOVED * TILE
        first = (slots - MOVED) * TILE
        up[pl.ds(0, height), :] = s_ref[pl.ds(first, height), :]
        up[pl.ds(height, height), :] = q_ref[pl.ds(first, height), :]
        rim(up, RIM_S, REGION - REG_X, TILE - 1)
        surface(up, 1)
        up[pl.ds(IDS, TILE), :] = ids
        down[pl.ds(0, 2 * height), :] = jnp.zeros((2 * height, LANES), F32)
        rim(down, RIM_S, 0, 0)
        surface(down, 0)
        down[pl.ds(IDS, TILE), :] = ids

    rim(far_ref, 0, 2 * REGION - REG_X, TILE - 1)

    @pl.when(meta[1] % 2 == 0)
    def _():
        messages(a_ref, b_ref)

    @pl.when(meta[1] % 2 == 1)
    def _():
        messages(b_ref, a_ref)


def depth_sums(view, meta, code, weight, diffusion, surface):
    slots = view.shape[0]
    shapes = [(slots * TILE, LANES), (slots * TILE, LANES), (MESSAGE, LANES), (MESSAGE, LANES), (48, LANES)]
    return pl.pallas_call(
        sums_kernel,
        in_specs=[SMEM] * 4 + [HBM, HBM],
        out_specs=[VMEM] * 5 + [SMEM],
        out_shape=[jax.ShapeDtypeStruct(x, F32) for x in shapes] + [jax.ShapeDtypeStruct((2 * REGION,), jnp.int32)],
        scratch_shapes=[
            pltpu.VMEM((slots, IMAGE, LANES), F32),
            pltpu.VMEM((2, STEP_SLOTS * ROWS, LANES), F32),
            pltpu.VMEM((2, TILE, surface.shape[1]), F32),
            pltpu.SemaphoreType.DMA((slots // STEP_SLOTS,)),
            pltpu.SemaphoreType.DMA,
            pltpu.SemaphoreType.DMA,
        ],
        compiler_params=pltpu.CompilerParams(vmem_limit_bytes=52 << 20),
        name="depth_sums",
    )(meta, code, weight, diffusion, view.reshape(slots, IMAGE, LANES), surface)


def field_kernel(meta, inv, s_ref, q_ref, a_ref, b_ref, far_ref, surf_ref, f_ref, ca_ref, cb_ref):
    slots = s_ref.shape[0] // TILE
    even = meta[1] % 2 == 0
    group = lane_id((TILE, LANES)) // BLOCK

    def below(start, size):
        return jnp.where(even, b_ref[pl.ds(start, size), :], a_ref[pl.ds(start, size), :])

    def above(start, size):
        return jnp.where(even, a_ref[pl.ds(start, size), :], b_ref[pl.ds(start, size), :])

    f_ref[...] = jnp.zeros(f_ref.shape, F32)
    for by in range(REG_Y):
        for b in range(FIELD_TILES):
            held = [g for g in range(4) if 4 * b + g < REG_X]
            mask = jnp.zeros((TILE, LANES), F32)
            tiles = {}
            for g in held:
                src = inv[by * REG_X + 4 * b + g]
                own_at = pl.multiple_of(jnp.clip(src, 0, slots - 1) * TILE, TILE)
                came_at = pl.multiple_of(jnp.clip(src - slots, 0, MOVED - 1) * TILE, TILE)
                for kind, ref in ((0, s_ref), (1, q_ref)):
                    own = ref[pl.ds(own_at, TILE), :]
                    other = below(pl.multiple_of(kind * MOVED * TILE + came_at, TILE), TILE)
                    tiles[kind, g] = jnp.where(src >= slots, other, jnp.where(src >= 0, own, 0.0))
                mask = jnp.where(group == g, jnp.where(src >= 0, 1.0, 0.0), mask)
            for kind in range(2):
                for q in range(4):
                    value = jnp.zeros((TILE, LANES), F32)
                    for g in held:
                        value = jnp.where(group == g, turn(tiles[kind, g], BLOCK * (g - q), 1), value)
                    f_ref[kind, b, pl.ds(TILE + BLOCK * by + q, TILE, stride=4), :] = value
            for q in range(4):
                f_ref[2, b, pl.ds(TILE + BLOCK * by + TILE * q, TILE), :] = mask

    row16 = lax.broadcasted_iota(jnp.int32, (16, LANES), 0)
    group16 = lane_id((16, LANES)) // BLOCK

    def rim_rows(kind, rim, first):
        rolled = [turn(rim, BLOCK * d, 1) for d in range(4)]
        for q in range(4):
            value = jnp.zeros((16, LANES), F32)
            for g in range(4):
                value = jnp.where((row16 % 4 == g) & (group16 == g), rolled[(g - q) % 4], value)
            value = value + turn(value, -1, 0)
            value = value + turn(value, -2, 0)
            for b in range(FIELD_TILES):
                f_ref[kind, b, pl.ds(first + q, 1), :] = value[4 * b : 4 * b + 1, :]

    @pl.when(meta[1] > 0)
    def _():
        for kind, base in ((0, RIM_S), (1, RIM_Q), (2, RIM_M)):
            rim_rows(kind, below(base, 16) + far_ref[pl.ds(base - RIM_S, 16), :], 4)

    @pl.when(meta[1] < meta[2] - 1)
    def _():
        def own_rim(ref):
            rows = []
            for k in range(16):
                if k < REG_X:
                    src = inv[REGION + k]
                    at = jnp.maximum(src, 0) * TILE
                    line = jnp.ones((1, LANES), F32) if ref is None else ref[pl.ds(at, 1), :]
                    rows.append(jnp.where(src >= 0, line, 0.0))
                else:
                    rows.append(jnp.zeros((1, LANES), F32))
            return jnp.concatenate(rows, axis=0)

        for kind, base, ref in ((0, RIM_S, s_ref), (1, RIM_Q, q_ref), (2, RIM_M, None)):
            rim_rows(kind, above(base, 16) + own_rim(ref), FIELD_ROWS - TILE)

    height, width = surf_ref.shape
    for b in range(FIELD_TILES):
        lanes = min(LANES, width - b * LANES)
        f_ref[3, b, pl.ds(TILE, height), pl.ds(0, lanes)] = surf_ref[:, pl.ds(b * LANES, lanes)]
        f_ref[3, b, pl.ds(4, 4), :] = below(SURF + b * TILE, TILE)[4:]
        f_ref[3, b, pl.ds(FIELD_ROWS - TILE, 4), :] = above(SURF + b * TILE, TILE)[:4]

    lane = lane_id((TILE, LANES))
    last = width - (FIELD_TILES - 1) * LANES - 4
    east_even = meta[0] % 2 == 0
    for h in range(3):
        west_out = jnp.zeros((TILE, LANES), F32)
        east_out = jnp.zeros((TILE, LANES), F32)
        for g in range(8):
            v = 3 * g + h
            if v * TILE >= FIELD_ROWS:
                continue
            for kind in range(4):
                at = 16 * g + 4 * kind
                inside = (lane >= at) & (lane < at + 4)
                west = f_ref[kind, 0, pl.ds(v * TILE, TILE), :]
                east = f_ref[kind, FIELD_TILES - 1, pl.ds(v * TILE, TILE), :]
                west_out = jnp.where(inside, turn(west, at, 1), west_out)
                east_out = jnp.where(inside, turn(east, at - last, 1), east_out)
        ca_ref[pl.ds(h * TILE, TILE), :] = jnp.where(east_even, east_out, west_out)
        cb_ref[pl.ds(h * TILE, TILE), :] = jnp.where(east_even, west_out, east_out)


def region_fields(meta, places, s, q, a, b, far, surface):
    return pl.pallas_call(
        field_kernel,
        in_specs=[SMEM, SMEM] + [VMEM] * 6,
        out_specs=[VMEM] * 3,
        out_shape=[
            jax.ShapeDtypeStruct((4, FIELD_TILES, FIELD_ROWS, LANES), F32),
            jax.ShapeDtypeStruct((24, LANES), F32),
            jax.ShapeDtypeStruct((24, LANES), F32),
        ],
        compiler_params=pltpu.CompilerParams(vmem_limit_bytes=12 << 20),
        name="region_fields",
    )(meta, places, s, q, a, b, far, surface)


def basis_kernel(meta, moved, f_ref, ca_ref, cb_ref, g_ref, blocks_ref, back_ref, u_ref):
    even = meta[0] % 2 == 0
    lane = lane_id((TILE, LANES))
    tiles = range(FIELD_TILES)
    fields = []
    for kind in range(4):
        parts = [f_ref[kind, b] for b in tiles]
        strip = []
        for v in range(FIELD_ROWS // TILE):
            g, h = v // 3, v % 3
            ca = ca_ref[pl.ds(h * TILE, TILE), :]
            cb = cb_ref[pl.ds(h * TILE, TILE), :]
            at = 16 * g + 4 * kind
            west = turn(jnp.where(even, cb, ca), 124 - at, 1)
            east = turn(jnp.where(even, ca, cb), 64 - at, 1)
            tile = f_ref[kind, FIELD_TILES - 1, pl.ds(v * TILE, TILE), :]
            tile = jnp.where((lane >= 64) & (lane < 68), east, tile)
            strip.append(jnp.where(lane >= 124, west, tile))
        parts[-1] = jnp.concatenate(strip, axis=0)
        fields.append(parts)
    depth, inner, mask, surf = fields
    wide = lane_id((FIELD_ROWS, LANES))

    def sides(v):
        fwd = [turn(x, 1, 1) for x in v]
        bwd = [turn(x, -1, 1) for x in v]
        out = []
        for b in tiles:
            left = jnp.where(wide == 0, fwd[b - 1], fwd[b])
            right = jnp.where(wide == LANES - 1, bwd[(b + 1) % FIELD_TILES], bwd[b])
            out.append(left + right)
        return out

    def rows(v):
        return [turn(x, 1, 0) + turn(x, -1, 0) for x in v]

    def spread(v):
        side = sides(v)
        both = rows([v[b] + 0.5 * side[b] for b in tiles])
        return [mask[b] * (side[b] + both[b]) for b in tiles]

    def edges(v):
        side, both = sides(v), rows(v)
        return [side[b] + both[b] for b in tiles]

    near, count = edges(inner), edges(mask)
    rhs = [mask[b] * (depth[b] + near[b] - count[b] * inner[b]) for b in tiles]
    scale = [1.0 / (6.0 + surf[b]) for b in tiles]
    u0 = [rhs[b] * scale[b] for b in tiles]
    z1 = spread(u0)
    u1 = [z1[b] * scale[b] for b in tiles]
    z2 = spread(u1)
    u2 = [z2[b] * scale[b] for b in tiles]
    z3 = spread(u2)
    rows_in = slice(TILE, FIELD_ROWS - TILE)

    def dot(x, y):
        total = jnp.zeros((TILE, LANES), F32)
        for b in tiles:
            p = x[b][rows_in] * y[b][rows_in]
            p = jnp.sum(p.reshape(-1, TILE, LANES), axis=0)
            if b == FIELD_TILES - 1:
                p = jnp.where(lane < 64, p, 0.0)
            total = total + p
        return jnp.sum(jnp.sum(total, axis=1, keepdims=True), axis=0, keepdims=True)

    row = jnp.zeros((1, LANES), F32)
    pairs = ((u0, rhs), (u0, z1), (u1, z1), (u1, z2), (u2, z2), (u2, z3))
    for k, (x, y) in enumerate(pairs):
        row = jnp.where(lane[:1] == k, dot(x, y), row)
    row = jnp.where(lane[:1] == 6, meta[3].astype(F32), row)
    g_ref[...] = jnp.broadcast_to(row, g_ref.shape)
    for k, u in enumerate((u0, u1, u2)):
        for b in tiles:
            u_ref[k, b] = u[b][rows_in]
    group = lane // BLOCK
    for k in range(3):
        for by in range(REG_Y):
            for b in tiles:
                value = [u_ref[k, b, pl.ds(BLOCK * by + q, TILE, stride=4), :] for q in range(4)]
                for g in range(4):
                    if 4 * b + g >= REG_X:
                        continue
                    tile = value[0]
                    for q in range(4):
                        part = turn(value[q], BLOCK * (q - g), 1)
                        tile = part if q == 0 else jnp.where(group == q, part, tile)
                    blocks_ref[pl.ds((k * REGION + by * REG_X + 4 * b + g) * TILE, TILE), :] = tile
    for m in range(MOVED):
        at = pl.multiple_of(jnp.maximum(moved[m], 0) * TILE, TILE)
        for k in range(3):
            tile = blocks_ref[pl.ds(k * REGION * TILE + at, TILE), :]
            back_ref[pl.ds((k * MOVED + m) * TILE, TILE), :] = tile


def solve_basis(meta, moved, fields, ca, cb, devices):
    return pl.pallas_call(
        basis_kernel,
        in_specs=[SMEM, SMEM, VMEM, VMEM, VMEM],
        out_specs=[VMEM] * 3,
        out_shape=[
            jax.ShapeDtypeStruct((devices, LANES), F32),
            jax.ShapeDtypeStruct((3 * REGION * TILE, LANES), F32),
            jax.ShapeDtypeStruct((3 * MOVED * TILE, LANES), F32),
        ],
        scratch_shapes=[pltpu.VMEM((3, FIELD_TILES, FIELD_ROWS - 2 * TILE, LANES), F32)],
        compiler_params=pltpu.CompilerParams(vmem_limit_bytes=24 << 20),
        name="solve_basis",
    )(meta, moved, fields, ca, cb)


def pressure_kernel(code, g_ref, blocks_ref, back_ref, held_ref, out_ref, same_ref, work):
    del held_ref, same_ref
    slots = out_ref.shape[0]
    total = jnp.sum(g_ref[...].reshape(-1, TILE, LANES), axis=0)
    total = jnp.broadcast_to(jnp.sum(total, axis=0, keepdims=True), (TILE, LANES))
    lane = lane_id((TILE, LANES))
    pick = lambda k: jnp.sum(jnp.where(lane == k, total, 0.0), axis=1, keepdims=True)
    g = [pick(k) for k in range(6)]
    g = [x / g[0] for x in g]
    a = [g[k] - g[k + 1] for k in range(5)]
    zero = jnp.zeros_like(g[0])
    one = zero + 1.0

    def form(v, m):
        out = zero
        for i in range(3):
            for k in range(3):
                out = out + v[i] * v[k] * m[i + k]
        return out

    coef = [zero, zero, zero]
    rho = [one, zero, zero]
    way = [one, zero, zero]
    norm = g[0]
    for iteration in range(ITERS):
        length = norm / form(way, a)
        coef = [coef[k] + length * way[k] for k in range(3)]
        if iteration + 1 < ITERS:
            moved = [way[0], way[1] - way[0], way[2] - way[1]]
            rho = [rho[k] - length * moved[k] for k in range(3)]
            norm_next = form(rho, g)
            way = [rho[k] + (norm_next / norm) * way[k] for k in range(3)]
            norm = norm_next
    coef = [jnp.broadcast_to(c, (TILE, LANES)) for c in coef]
    for s in range(slots):
        c = code[s]
        at = pl.multiple_of(jnp.where(c < REGION, c, 0) * TILE, TILE)
        tiles = [blocks_ref[pl.ds(k * REGION * TILE + at, TILE), :] for k in range(3)]
        m = s - (slots - MOVED)
        if m >= 0:
            for k in range(3):
                other = back_ref[pl.ds((k * MOVED + m) * TILE, TILE), :]
                tiles[k] = jnp.where(c < REGION, tiles[k], other)
        work[pl.ds(s * TILE, TILE), :] = coef[0] * tiles[0] + coef[1] * tiles[1] + coef[2] * tiles[2]
    for first in range(0, slots, TILE):
        size = min(TILE, slots - first)
        for c in range(TILE):
            lines = work[pl.ds(first * TILE + c, size, stride=TILE), :]
            out_ref[pl.ds(first, size), pl.ds(c * LANES, LANES)] = lines


def slot_pressure(code, sums, blocks, back, held):
    slots = code.shape[0]
    return pl.pallas_call(
        pressure_kernel,
        in_specs=[SMEM, VMEM, VMEM, VMEM, ANY],
        out_specs=[VMEM, ANY],
        out_shape=[
            jax.ShapeDtypeStruct((slots, TILE * LANES), F32),
            jax.ShapeDtypeStruct(held.shape, F32),
        ],
        scratch_shapes=[pltpu.VMEM((slots * TILE, LANES), F32)],
        input_output_aliases={4: 1},
        compiler_params=pltpu.CompilerParams(vmem_limit_bytes=12 << 20),
        name="slot_pressure",
    )(code, sums, blocks, back, held)


def columns_kernel(meta, inv, t_ref, after_ref, a_ref, b_ref, west, east, sems):
    del after_ref
    even = meta[0] % 2 == 0
    count = 2 * REG_Y

    def copies(k):
        w, e = inv[REG_X * k], inv[REG_X * k + REG_X - 1]
        cw = pltpu.make_async_copy(t_ref.at[jnp.maximum(w, 0)], west.at[k], sems.at[0, k])
        ce = pltpu.make_async_copy(t_ref.at[jnp.maximum(e, 0)], east.at[k], sems.at[1, k])
        return cw, ce

    for k in range(count):
        for c in copies(k):
            c.start()
    column = lane_id((ROWS, LANES)) % BLOCK
    for first in (0, REG_Y):
        for k in range(first, first + REG_Y):
            for c in copies(k):
                c.wait()
        for level in range(HALF):
            at = pl.ds(level * ROWS, ROWS)
            if first:
                out_a, out_b = a_ref[at, :], b_ref[at, :]
                out_w, out_e = jnp.where(even, out_b, out_a), jnp.where(even, out_a, out_b)
            else:
                out_w = out_e = jnp.zeros((ROWS, LANES), F32)
            for k in range(first, first + REG_Y):
                has_w, has_e = inv[REG_X * k] >= 0, inv[REG_X * k + REG_X - 1] >= 0
                for part in range(2):
                    lane = k + 16 * part
                    here = column == lane
                    x = pl.ds((level + HALF * part) * ROWS, ROWS)
                    out_w = jnp.where(here & has_w, turn(west[k, x, :], lane, 1), out_w)
                    out_e = jnp.where(here & has_e, turn(east[k, x, :], lane - (BLOCK - 1), 1), out_e)
            a_ref[at, :] = jnp.where(even, out_e, out_w)
            b_ref[at, :] = jnp.where(even, out_w, out_e)


def column_strips(meta, places, view, after):
    count = 2 * REG_Y
    return pl.pallas_call(
        columns_kernel,
        in_specs=[SMEM, SMEM, HBM, ANY],
        out_specs=[VMEM] * 2,
        out_shape=[jax.ShapeDtypeStruct((HALF * ROWS, LANES), F32)] * 2,
        scratch_shapes=[
            pltpu.VMEM((count, IMAGE, LANES), F32),
            pltpu.VMEM((count, IMAGE, LANES), F32),
            pltpu.SemaphoreType.DMA((2, count)),
        ],
        compiler_params=pltpu.CompilerParams(vmem_limit_bytes=52 << 20),
        cost_estimate=pl.CostEstimate(flops=1, bytes_accessed=1, transcendentals=0),
        name="column_strips",
    )(meta, places, view.reshape(view.shape[0], IMAGE, LANES), after)


def links_kernel(meta, table, t_ref, ga_ref, gb_ref, a_ref, b_ref, whole, half, sem_we, sem_ns):
    even_x = meta[0] % 2 == 0
    even_y = meta[1] % 2 == 0

    def we_copy(way, k):
        link = jnp.maximum(table[way * (CAP_WE + CAP_NS) + k], 0)
        return pltpu.make_async_copy(t_ref.at[link // 4], whole.at[way, k], sem_we.at[way, k])

    def ns_copy(way, k):
        link = jnp.maximum(table[way * (CAP_WE + CAP_NS) + CAP_WE + k], 2)
        rows = pl.ds(pl.multiple_of((link % 4 - 2) * TILE, TILE), TILE)
        dest = half.at[way, k, :, pl.ds(TILE, TILE), :]
        return pltpu.make_async_copy(t_ref.at[link // 4, :, rows, :], dest, sem_ns.at[way, k])

    for way in range(2):
        for k in range(CAP_WE):
            @pl.when(table[way * (CAP_WE + CAP_NS) + k] >= 0)
            def _():
                we_copy(way, k).start()

        for k in range(CAP_NS):
            ns_copy(way, k).start()

    column = lane_id((HALF * ROWS, LANES)) % 16
    from_west = jnp.where(even_x, gb_ref[...], ga_ref[...])
    from_east = jnp.where(even_x, ga_ref[...], gb_ref[...])
    ways = ((turn(from_west, -5, 1), from_east), (from_west, turn(from_east, 5, 1)))
    relays = [jnp.where(column < 5, w, jnp.where(column < RELAY, e, 0.0)) for w, e in ways]

    def message(way, out):
        out[pl.ds(0, HALF * ROWS), :] = relays[way]
        out[pl.ds(HALF * ROWS + LEVELS * TILE, TILE), :] = jnp.zeros((TILE, LANES), F32)
        lane32 = lane_id((ROWS, LANES)) % BLOCK
        for k in range(CAP_WE):
            link = table[way * (CAP_WE + CAP_NS) + k]

            @pl.when(link >= 0)
            def _():
                we_copy(way, k).wait()
                start = (link % 4) * (BLOCK - 1)
                for level in range(HALF):
                    at = pl.ds(level * ROWS, ROWS)
                    value = out[at, :]
                    for part in range(2):
                        lane = RELAY + k + 16 * part
                        x = turn(whole[way, k, level + HALF * part], lane, 1)
                        x = jnp.where(start > 0, turn(x, 1 - BLOCK, 1), x)
                        value = jnp.where(lane32 == lane, x, value)
                    out[at, :] = value

        links = [jnp.maximum(table[way * (CAP_WE + CAP_NS) + CAP_WE + k], 2) for k in range(CAP_NS)]
        first = [TILE + 6 * (links[k] % 4 - 2) - 2 * (k // 4) for k in range(CAP_NS)]
        by = [(BLOCK * (k % 4) + BLOCK * (links[k] % 4 - 2)) % LANES for k in range(CAP_NS)]
        for k in range(CAP_NS):
            ns_copy(way, k).wait()
        row = lax.broadcasted_iota(jnp.int32, (TILE, LANES), 0) // 2
        place = row * 4 + lane_id((TILE, LANES)) // BLOCK
        for level in range(LEVELS):
            value = jnp.zeros((TILE, LANES), F32)
            for k in range(CAP_NS):
                x = pltpu.roll(half[way, k, level, pl.ds(first[k], TILE), :], by[k], 1)
                value = jnp.where(place == k, x, value)
            out[pl.ds(HALF * ROWS + level * TILE, TILE), :] = value

    @pl.when(even_y)
    def _():
        message(0, a_ref)
        message(1, b_ref)

    @pl.when(jnp.logical_not(even_y))
    def _():
        message(0, b_ref)
        message(1, a_ref)


def link_strips(meta, table, view, ga, gb):
    rows = LINK_ROWS
    return pl.pallas_call(
        links_kernel,
        in_specs=[SMEM, SMEM, HBM, VMEM, VMEM],
        out_specs=[VMEM] * 2,
        out_shape=[jax.ShapeDtypeStruct((rows, LANES), F32)] * 2,
        scratch_shapes=[
            pltpu.VMEM((2, CAP_WE, LEVELS, ROWS, LANES), F32),
            pltpu.VMEM((2, CAP_NS, LEVELS, 3 * TILE, LANES), F32),
            pltpu.SemaphoreType.DMA((2, CAP_WE)),
            pltpu.SemaphoreType.DMA((2, CAP_NS)),
        ],
        compiler_params=pltpu.CompilerParams(vmem_limit_bytes=52 << 20),
        name="link_strips",
    )(meta, table, view, ga, gb)


BOX_LOW = 2 * HALF * ROWS
BOX_HIGH = BOX_LOW + LINK_ROWS
BOX = BOX_HIGH + LINK_ROWS


def tracer_kernel(meta, table, need, diffusion, t_ref, ga_ref, gb_ref, ha_ref, hb_ref, out_ref, own, up, down, box, sems, out_sems):
    slots = own.shape[0]
    chunks = slots // STEP_SLOTS

    def fetch(c):
        part = pl.ds(c * STEP_SLOTS, STEP_SLOTS)
        return pltpu.make_async_copy(t_ref.at[part], own.at[part], sems.at[c])

    def keep(c):
        part = pl.ds(c * STEP_SLOTS, STEP_SLOTS)
        return pltpu.make_async_copy(own.at[part], out_ref.at[part], out_sems.at[c])

    for c in range(chunks):
        fetch(c).start()
    even_x = meta[0] % 2 == 0
    even_y = meta[1] % 2 == 0
    up[slots] = jnp.zeros(up.shape[1:], F32)
    down[slots] = jnp.zeros(up.shape[1:], F32)
    for first, second, size, low, high in (
        (ga_ref, gb_ref, HALF * ROWS, 0, HALF * ROWS),
        (ha_ref, hb_ref, LINK_ROWS, BOX_LOW, BOX_HIGH),
    ):
        even = even_x if low == 0 else even_y
        box[pl.ds(low, size), :] = jnp.where(even, second[...], first[...])
        box[pl.ds(high, size), :] = jnp.where(even, first[...], second[...])
    for way, low in enumerate((BOX_LOW, BOX_HIGH)):
        for level in range(LEVELS):
            x = box[pl.ds(low + HALF * ROWS + level * TILE, TILE), :]
            for d in range(4):
                y = turn(x, BLOCK * d, 1)
                up[slots + 1 + 4 * way + d, pl.ds(TILE + level * ROWS, TILE), :] = y
                down[slots + 1 + 4 * way + d, pl.ds(TILE + level * ROWS, TILE), :] = y
    for level in range(LEVELS):
        part = level // HALF
        w = box[pl.ds((level % HALF) * ROWS, ROWS), :]
        e = box[pl.ds((HALF + level % HALF) * ROWS, ROWS), :]
        for k in range(2 * REG_Y):
            down[slots + 9 + k, pl.ds(TILE + level * ROWS, ROWS), :] = turn(w, -1 - k - 16 * part, 1)
            up[slots + 9 + k, pl.ds(TILE + level * ROWS, ROWS), :] = turn(e, BLOCK - k - 16 * part, 1)

    def arrive(c, carry):
        fetch(c).wait()
        for n in range(STEP_SLOTS):
            s = c * STEP_SLOTS + n
            for level in range(LEVELS):
                x = own[s, pl.ds(level * ROWS, ROWS), :]
                up[s, pl.ds(TILE + level * ROWS, ROWS), :] = pltpu.roll(x, BLOCK, 1)
                down[s, pl.ds(TILE + level * ROWS, ROWS), :] = pltpu.roll(x, LANES - BLOCK, 1)
        return carry

    cells = (ROWS, LANES)
    lane = lane_id(cells)
    column = lane % BLOCK
    row = lax.broadcasted_iota(jnp.int32, cells, 0)
    row8 = row[:TILE]
    edge = (
        jnp.where(column == 0, 1.0, 0.0),
        jnp.where(column == BLOCK - 1, 1.0, 0.0),
        jnp.where((row < 2) & (lane < BLOCK), 1.0, 0.0),
        jnp.where((row >= ROWS - 2) & (lane >= LANES - BLOCK), 1.0, 0.0),
    )

    def unpack(n, s):
        for t, dest in ((0, down), (1, up)):
            at = s * 4 + t

            @pl.when(table[1, at] == 1)
            def _():
                first, by = pl.multiple_of(table[2, at], TILE), table[3, at]
                for level in range(LEVELS):
                    part = level // HALF
                    x = box[pl.ds(first + (level % HALF) * ROWS, ROWS), :]
                    x = pltpu.roll(x, (by + LANES - 16 * part) % LANES, 1)
                    dest[slots + 19 + n, pl.ds(TILE + level * ROWS, ROWS), :] = x

    def step(n, s):
        count = jnp.full(cells, 4.0, F32)
        for t in range(4):
            count = count - edge[t] * table[4, s * 4 + t].astype(F32)
        west, east, south, north = [table[0, s * 4 + t] for t in range(4)]
        south_at, north_at = TILE + table[2, s * 4 + 2], TILE + table[2, s * 4 + 3]
        for level in range(LEVELS):
            at = level * ROWS
            x = own[s, pl.ds(at, ROWS), :]
            under = up[s, pl.ds(TILE + at - 2, ROWS), :]
            over = down[s, pl.ds(TILE + at + 2, ROWS), :]
            low = up[south, pl.ds(south_at + at, TILE), :]
            high = down[north, pl.ds(north_at + at, TILE), :]
            under = jnp.concatenate([jnp.where(row8 < 2, low, under[:TILE]), under[TILE:]], axis=0)
            over = jnp.concatenate([over[:TILE], jnp.where(row8 >= TILE - 2, high, over[TILE:])], axis=0)
            total = jnp.where(lane < BLOCK, under, up[s, pl.ds(TILE + at, ROWS), :])
            total = total + jnp.where(lane >= LANES - BLOCK, over, down[s, pl.ds(TILE + at, ROWS), :])
            w = down[west, pl.ds(TILE + at, ROWS), :]
            e = up[east, pl.ds(TILE + at, ROWS), :]
            total = total + pltpu.roll(jnp.where(column == BLOCK - 1, w, x), 1, 1)
            total = total + pltpu.roll(jnp.where(column == 0, e, x), LANES - 1, 1)
            own[s, pl.ds(at, ROWS), :] = x + diffusion[level] * (total - count * x)

    def work(c, seen):
        upto = jnp.maximum(seen, need[c] + 1)
        lax.fori_loop(seen, upto, arrive, 0)
        for n in range(STEP_SLOTS):
            unpack(n, c * STEP_SLOTS + n)
        for n in range(STEP_SLOTS):
            step(n, c * STEP_SLOTS + n)
        keep(c).start()
        return upto

    lax.fori_loop(0, chunks, work, 0)
    for c in range(chunks):
        keep(c).wait()


def step_tracers(meta, table, need, diffusion, view, ga, gb, ha, hb):
    slots = view.shape[0]
    chunks = slots // STEP_SLOTS
    size = slots * IMAGE * LANES
    images = slots + 19 + STEP_SLOTS
    out = pl.pallas_call(
        tracer_kernel,
        in_specs=[SMEM] * 4 + [HBM] + [VMEM] * 4,
        out_specs=HBM,
        out_shape=jax.ShapeDtypeStruct((slots, IMAGE, LANES), F32),
        scratch_shapes=[
            pltpu.VMEM((slots, IMAGE, LANES), F32),
            pltpu.VMEM((images, IMAGE + 2 * TILE, LANES), F32),
            pltpu.VMEM((images, IMAGE + 2 * TILE, LANES), F32),
            pltpu.VMEM((BOX, LANES), F32),
            pltpu.SemaphoreType.DMA((chunks,)),
            pltpu.SemaphoreType.DMA((chunks,)),
        ],
        compiler_params=pltpu.CompilerParams(vmem_limit_bytes=52 << 20),
        cost_estimate=pl.CostEstimate(flops=14 * size, bytes_accessed=8 * size, transcendentals=0),
        name="step_tracers",
    )(meta, table, need, diffusion, view.reshape(slots, IMAGE, LANES), ga, gb, ha, hb)
    return out.reshape(view.shape)


def with_halo(block, sides, width):
    for axis, dim in sides:
        low = shifted(lax.slice_in_dim(block, block.shape[dim] - width, None, axis=dim), axis, 1)
        high = shifted(lax.slice_in_dim(block, 0, width, axis=dim), axis, -1)
        block = jnp.concatenate([low, block, high], axis=dim)
    return block


def edge_strips(grid):
    sides = [grid[..., :, 0], grid[..., :, -1], grid[..., 0, :], grid[..., -1, :]]
    return jnp.stack(sides, axis=1).reshape(grid.shape[0] * 4, -1)


def general_step(tracers, diffusion, halo_source):
    slots = tracers.shape[0]
    grid = tracers.reshape(slots, TRACER, LEVELS, BLOCK, BLOCK)
    strips = edge_strips(grid)
    width = strips.shape[1]
    count_gx, count_gy = lax.axis_size("gx"), lax.axis_size("gy")
    source = halo_source.reshape(-1)
    missing = source >= 4 * slots * count_gx * count_gy
    slot = jnp.where(missing, 0, source) // 4
    owner = slot // slots
    step_gx = (owner // count_gy - lax.axis_index("gx") + count_gx + 1) % count_gx
    step_gy = (owner % count_gy - lax.axis_index("gy") + count_gy + 1) % count_gy
    every = slots * 4
    table = with_halo(strips.reshape(1, 1, every, width), (("gx", 0), ("gy", 1)), 1).reshape(9 * every, width)
    index = (step_gx * 3 + step_gy) * every + slot % slots * 4 + source % 4
    halo = jnp.take(table, jnp.where(missing, 0, index), axis=0, mode="clip")
    halo = halo.reshape(slots, 4, TRACER, LEVELS, BLOCK)
    gate = jnp.where(missing, 0.0, 1.0).astype(F32).reshape(slots, 4, 1, 1, 1)
    inner_x = grid[..., :, :-1] - grid[..., :, 1:]
    inner_y = grid[..., :-1, :] - grid[..., 1:, :]
    west = (halo[:, 0] - grid[..., :, 0]) * gate[:, 0]
    east = (halo[:, 1] - grid[..., :, -1]) * gate[:, 1]
    south = (halo[:, 2] - grid[..., 0, :]) * gate[:, 2]
    north = (halo[:, 3] - grid[..., -1, :]) * gate[:, 3]
    laplace = (
        jnp.concatenate([west[..., None], inner_x], axis=-1)
        + jnp.concatenate([-inner_x, east[..., None]], axis=-1)
        + jnp.concatenate([south[..., None, :], inner_y], axis=-2)
        + jnp.concatenate([-inner_y, north[..., None, :]], axis=-2)
    )
    updated = grid + diffusion[None, None, :, None, None] * laplace
    return plain(seen_by_rows(updated.reshape(tracers.shape)))


def strip_tables(halo_source, code, at_x, at_y, count_x, count_y):
    slots = halo_source.shape[0]
    source = halo_source.reshape(-1)
    missing = source >= 4 * slots * count_x * count_y
    source = jnp.where(missing, 0, source)
    owner = source // (4 * slots)
    local_slot = source // 4 - owner * slots
    same_x = owner // count_y == at_x
    owner_y = owner % count_y
    up = owner_y == (at_y + 1) % count_y
    here = owner_y == at_y
    index = jnp.arange(4 * slots, dtype=jnp.int32)
    side = index % 4
    kind = jnp.where(side >= 2, 1, 0)
    linked = ~missing & same_x & ~here
    group = jnp.where(linked, jnp.where(up, kind, 2 + kind), -1)

    def rank(key):
        before = (key[None, :] < key[:, None]) & (group[None, :] == group[:, None])
        return jnp.sum(before.astype(jnp.int32), axis=1)

    take = rank(index)
    give = rank(source)
    entry = jnp.arange(2 * (CAP_WE + CAP_NS), dtype=jnp.int32)
    rest = entry % (CAP_WE + CAP_NS)
    of_kind = jnp.where(rest >= CAP_WE, 1, 0)
    want = (2 * (entry // (CAP_WE + CAP_NS)) + of_kind) * 1024 + rest - CAP_WE * of_kind
    has = jnp.where(group >= 0, group * 1024 + give, -1)
    send = jnp.sum(jnp.where(want[:, None] == has[None, :], index[None, :] + 1, 0), axis=1) - 1
    over = jnp.any(linked & (take >= jnp.where(kind == 1, CAP_NS, CAP_WE)))
    row = jnp.broadcast_to((code // REG_X)[:, None], (slots, 4)).reshape(-1)
    local = same_x & here
    north = kind == 1
    lane = jnp.where(same_x, RELAY + take, row % REG_Y + jnp.where(side == 0, 0, REG_Y))
    box = jnp.where(up, BOX_HIGH, BOX_LOW)
    by = (jnp.where(side == 0, -1, BLOCK) - lane) % LANES
    unpacked = slots + 19 + index // 4 % STEP_SLOTS
    image_we = jnp.where(local, local_slot, jnp.where(here, slots + 9 + row, unpacked))
    take = jnp.minimum(take, CAP_NS - 1)
    turns = jnp.where(side == 2, -take, 3 - take) % 4
    image_ns = jnp.where(local, local_slot, slots + 1 + jnp.where(up, 4, 0) + turns)
    row_ns = jnp.where(local | missing, jnp.where(side == 2, ROWS - 2, 0), 2 * (take // 4))
    row_ns = row_ns - jnp.where(side == 3, TILE - 2, 0)
    image = jnp.where(missing, slots, jnp.where(north, image_ns, image_we))
    unpack = jnp.where(missing | here | north, 0, 1)
    table = jnp.stack([image, unpack, jnp.where(north, row_ns, box), by, jnp.where(missing, 1, 0)])
    last = jnp.where(local & ~missing, local_slot, 0).reshape(-1, 4 * STEP_SLOTS)
    need = jnp.maximum(jnp.max(last, axis=1) // STEP_SLOTS, jnp.arange(slots // STEP_SLOTS))
    return table, need, send, over.astype(jnp.int32)


def on_device(tracers, diffusion, layer_weight, surface_term, clinic_blocks, halo_source):
    slots = tracers.shape[0]
    count_x, count_y = lax.axis_size("gx"), lax.axis_size("gy")
    at_x, at_y = lax.axis_index("gx"), lax.axis_index("gy")
    grid_columns = REG_X * count_x
    grid_rows = REG_Y * count_y
    own_row = (clinic_blocks // grid_columns - REG_Y * at_y) % grid_rows
    code = own_row * REG_X + clinic_blocks % grid_columns % REG_X
    zero = jnp.zeros((), jnp.int32)
    meta = jnp.stack([at_x, at_y, zero + count_y, zero]).astype(jnp.int32)

    view = seen_by_rows(tracers)
    s, q, a, b, far, places = depth_sums(view, meta, code, layer_weight, diffusion, surface_term)
    ra, rb = swap(a, b, "gy", count_y)
    rfar = shifted(far, "gy", 2)

    source, places = lax.optimization_barrier((halo_source, places))
    table, need, send, over = strip_tables(source, code, at_x, at_y, count_x, count_y)
    ga, gb = swap(*column_strips(meta, places, view, rfar), "gx", count_x)

    moved = jnp.where(at_y % 2 == 0, rb[IDS, :MOVED], ra[IDS, :MOVED]).astype(jnp.int32)
    spot = jnp.arange(2 * REGION, dtype=jnp.int32)[:, None]
    index = jnp.arange(MOVED, dtype=jnp.int32)[None, :]
    both = places + jnp.sum(jnp.where(moved[None, :] == spot, index + 1 + slots, 0), axis=1)
    fields, ca, cb = region_fields(meta, both, s, q, ra, rb, rfar, surface_term)
    ca, cb = swap(ca, cb, "gx", count_x)
    ha, hb = swap(*link_strips(meta, send, view, ga, gb), "gy", count_y)

    meta_over = jnp.stack([at_x, at_y, zero + count_y, over]).astype(jnp.int32)
    sums, blocks, back = solve_basis(meta_over, moved, fields, ca, cb, count_x * count_y)
    back = shifted(back, "gy", -1)
    sums = lax.all_to_all(sums[:, None], ("gx", "gy"), 0, 0, tiled=True)
    updated = step_tracers(meta, table, need, diffusion, view, ga, gb, ha, hb)
    sums, updated = lax.optimization_barrier((sums, updated))
    updated = lax.cond(
        jnp.max(sums[:, 0, 6]) > 0.0,
        lambda fast: general_step(tracers, diffusion, halo_source),
        lambda fast: fast,
        updated,
    )
    pressure, updated = slot_pressure(code, sums.reshape(-1, LANES), blocks, back, updated)
    updated = updated.reshape(slots, LEVELS, TILE, TRACER, LANES).transpose(0, 3, 1, 2, 4)
    return (updated.reshape(tracers.shape), pressure)


def solution(mesh):
    placed = (
        P(("gx", "gy"), None, None, None),
        P(),
        P(),
        P("gy", "gx"),
        P(("gx", "gy")),
        P(("gx", "gy"), None),
    )
    return jax.shard_map(
        on_device,
        mesh=mesh,
        in_specs=placed,
        out_specs=(P(("gx", "gy"), None, None, None), P(("gx", "gy"), None)),
        check_vma=False,
    )
```

```python
import jax
import jax.numpy as jnp
from jax import lax
from jax.experimental import pallas as pl
from jax.experimental.layout import Layout, with_layout_constraint
from jax.experimental.pallas import tpu as pltpu
from jax.sharding import PartitionSpec as P

BLOCK = 32
LEVELS = 20
TRACER = 2
REG_X = 14
REG_Y = 5
ITERS = 3
REGION = REG_X * REG_Y
MOVED = 22
LANES = 128
TILE = 8
ROWS = 16
HALF = LEVELS // 2
STEP_SLOTS = 7
IMAGE = LEVELS * ROWS
FIELD_ROWS = 176
FIELD_TILES = 4
CAP_WE = 6
CAP_NS = 16
RELAY = 10
LINK_ROWS = HALF * ROWS + (LEVELS + 1) * TILE
RIM_S = 2 * MOVED * TILE
RIM_Q = RIM_S + 16
RIM_M = RIM_Q + 16
SURF = RIM_M + 16
IDS = SURF + FIELD_TILES * TILE
MESSAGE = IDS + TILE
F32 = jnp.float32
SMEM = pl.BlockSpec(memory_space=pltpu.SMEM)
VMEM = pl.BlockSpec(memory_space=pltpu.VMEM)
ANY = pl.BlockSpec(memory_space=pl.ANY)
HBM = pl.BlockSpec(memory_space=pltpu.HBM)


def lane_id(shape):
    return lax.broadcasted_iota(jnp.int32, shape, len(shape) - 1)


def turn(x, by, axis):
    size = x.shape[axis]
    if isinstance(by, int):
        by = by % size
        if by == 0:
            return x
    return pltpu.roll(x, by, axis)


def swap(to_next, to_last, axis, count):
    first = [(i, i ^ 1) for i in range(count)]
    second = [(i, (i + 1) % count if i % 2 else (i - 1) % count) for i in range(count)]
    return lax.ppermute(to_next, axis, first), lax.ppermute(to_last, axis, second)


def plain(x):
    return with_layout_constraint(x, Layout(major_to_minor=tuple(range(x.ndim))))


def seen_by_rows(tracers):
    slots = tracers.shape[0]
    view = tracers.reshape(slots, TRACER, LEVELS, TILE, LANES).transpose(0, 2, 3, 1, 4)
    return view.reshape(slots, LEVELS, ROWS, LANES)


def shifted(x, axis, by):
    length = lax.axis_size(axis)
    return lax.ppermute(x, axis, [(i, (i + by) % length) for i in range(length)])


def sums_kernel(meta, code, weight, diffusion, t_ref, surf_ref, s_ref, q_ref, a_ref, b_ref, far_ref, inv, own, part, edges, sems, sem_low, sem_high):
    slots = own.shape[0]
    chunks = slots // STEP_SLOTS
    height = surf_ref.shape[0]

    def fetch(c):
        part = pl.ds(c * STEP_SLOTS, STEP_SLOTS)
        return pltpu.make_async_copy(t_ref.at[part], own.at[part], sems.at[c])

    def fetch_low():
        return pltpu.make_async_copy(surf_ref.at[pl.ds(0, TILE), :], edges.at[0], sem_low)

    def fetch_high():
        return pltpu.make_async_copy(surf_ref.at[pl.ds(height - TILE, TILE), :], edges.at[1], sem_high)

    for c in range(chunks):
        fetch(c).start()
    fetch_low().start()
    fetch_high().start()
    for r in range(2 * REGION):
        inv[r] = -1
    for s in range(slots):
        inv[code[s]] = s
    tracer = lax.broadcasted_iota(jnp.int32, (TILE, LANES), 0) % 2
    pairs = [(n, h) for n in range(STEP_SLOTS) for h in range(2)]

    def sum_chunk(c, carry):
        fetch(c).wait()
        acc_s = {p: jnp.zeros((TILE, LANES), F32) for p in pairs}
        acc_q = {p: jnp.zeros((TILE, LANES), F32) for p in pairs}
        for level in range(LEVELS):
            w = jnp.where(tracer == 0, weight[0, level], weight[1, level])
            wd = w * diffusion[level]
            for n, h in pairs:
                x = own[c * STEP_SLOTS + n, pl.ds(level * ROWS + h * TILE, TILE), :]
                acc_s[n, h] = acc_s[n, h] + w * x
                acc_q[n, h] = acc_q[n, h] + wd * x
        for n, h in pairs:
            part[0, pl.ds(n * ROWS + h * TILE, TILE), :] = acc_s[n, h]
            part[1, pl.ds(n * ROWS + h * TILE, TILE), :] = acc_q[n, h]
        for n in range(STEP_SLOTS):
            row = pl.multiple_of((c * STEP_SLOTS + n) * TILE, TILE)
            for kind, out in ((0, s_ref), (1, q_ref)):
                even = part[kind, pl.ds(n * ROWS, TILE, stride=2), :]
                odd = part[kind, pl.ds(n * ROWS + 1, TILE, stride=2), :]
                out[pl.ds(row, TILE), :] = even + odd
        return carry

    lax.fori_loop(0, chunks, sum_chunk, 0)
    fetch_low().wait()
    fetch_high().wait()

    def rim(dest, base, first, chunk):
        for k in range(REG_X):
            src = inv[first + k]
            at = jnp.maximum(src, 0) * TILE + chunk
            has = jnp.where(src >= 0, 1.0, 0.0)
            dest[pl.ds(base + k, 1), :] = jnp.where(src >= 0, s_ref[pl.ds(at, 1), :], 0.0)
            dest[pl.ds(base + 16 + k, 1), :] = jnp.where(src >= 0, q_ref[pl.ds(at, 1), :], 0.0)
            dest[pl.ds(base + 32 + k, 1), :] = jnp.full((1, LANES), has, F32)
        for k in range(REG_X, 16):
            for kind in range(3):
                dest[pl.ds(base + 16 * kind + k, 1), :] = jnp.zeros((1, LANES), F32)

    def surface(dest, edge):
        for b in range(FIELD_TILES):
            if b < 3:
                dest[pl.ds(SURF + b * TILE, TILE), :] = edges[edge, :, pl.ds(b * LANES, LANES)]
            else:
                width = edges.shape[2] - b * LANES
                dest[pl.ds(SURF + b * TILE, TILE), :] = jnp.zeros((TILE, LANES), F32)
                dest[pl.ds(SURF + b * TILE, TILE), pl.ds(0, width)] = edges[edge, :, pl.ds(b * LANES, width)]

    lane = lane_id((TILE, LANES))
    ids = jnp.full((TILE, LANES), -1.0, F32)
    for k in range(MOVED):
        ids = jnp.where(lane == k, (code[slots - MOVED + k] - REGION).astype(F32), ids)

    def messages(up, down):
        height = MOVED * TILE
        first = (slots - MOVED) * TILE
        up[pl.ds(0, height), :] = s_ref[pl.ds(first, height), :]
        up[pl.ds(height, height), :] = q_ref[pl.ds(first, height), :]
        rim(up, RIM_S, REGION - REG_X, TILE - 1)
        surface(up, 1)
        up[pl.ds(IDS, TILE), :] = ids
        down[pl.ds(0, 2 * height), :] = jnp.zeros((2 * height, LANES), F32)
        rim(down, RIM_S, 0, 0)
        surface(down, 0)
        down[pl.ds(IDS, TILE), :] = ids

    rim(far_ref, 0, 2 * REGION - REG_X, TILE - 1)

    @pl.when(meta[1] % 2 == 0)
    def _():
        messages(a_ref, b_ref)

    @pl.when(meta[1] % 2 == 1)
    def _():
        messages(b_ref, a_ref)


def depth_sums(view, meta, code, weight, diffusion, surface):
    slots = view.shape[0]
    shapes = [(slots * TILE, LANES), (slots * TILE, LANES), (MESSAGE, LANES), (MESSAGE, LANES), (48, LANES)]
    return pl.pallas_call(
        sums_kernel,
        in_specs=[SMEM] * 4 + [HBM, HBM],
        out_specs=[VMEM] * 5 + [SMEM],
        out_shape=[jax.ShapeDtypeStruct(x, F32) for x in shapes] + [jax.ShapeDtypeStruct((2 * REGION,), jnp.int32)],
        scratch_shapes=[
            pltpu.VMEM((slots, IMAGE, LANES), F32),
            pltpu.VMEM((2, STEP_SLOTS * ROWS, LANES), F32),
            pltpu.VMEM((2, TILE, surface.shape[1]), F32),
            pltpu.SemaphoreType.DMA((slots // STEP_SLOTS,)),
            pltpu.SemaphoreType.DMA,
            pltpu.SemaphoreType.DMA,
        ],
        compiler_params=pltpu.CompilerParams(vmem_limit_bytes=52 << 20),
        name="depth_sums",
    )(meta, code, weight, diffusion, view.reshape(slots, IMAGE, LANES), surface)


def field_kernel(meta, inv, s_ref, q_ref, a_ref, b_ref, far_ref, surf_ref, f_ref, ca_ref, cb_ref):
    slots = s_ref.shape[0] // TILE
    even = meta[1] % 2 == 0
    group = lane_id((TILE, LANES)) // BLOCK

    def below(start, size):
        return jnp.where(even, b_ref[pl.ds(start, size), :], a_ref[pl.ds(start, size), :])

    def above(start, size):
        return jnp.where(even, a_ref[pl.ds(start, size), :], b_ref[pl.ds(start, size), :])

    f_ref[...] = jnp.zeros(f_ref.shape, F32)
    for by in range(REG_Y):
        for b in range(FIELD_TILES):
            held = [g for g in range(4) if 4 * b + g < REG_X]
            mask = jnp.zeros((TILE, LANES), F32)
            tiles = {}
            for g in held:
                src = inv[by * REG_X + 4 * b + g]
                own_at = pl.multiple_of(jnp.clip(src, 0, slots - 1) * TILE, TILE)
                came_at = pl.multiple_of(jnp.clip(src - slots, 0, MOVED - 1) * TILE, TILE)
                for kind, ref in ((0, s_ref), (1, q_ref)):
                    own = ref[pl.ds(own_at, TILE), :]
                    other = below(pl.multiple_of(kind * MOVED * TILE + came_at, TILE), TILE)
                    tiles[kind, g] = jnp.where(src >= slots, other, jnp.where(src >= 0, own, 0.0))
                mask = jnp.where(group == g, jnp.where(src >= 0, 1.0, 0.0), mask)
            for kind in range(2):
                for q in range(4):
                    value = jnp.zeros((TILE, LANES), F32)
                    for g in held:
                        value = jnp.where(group == g, turn(tiles[kind, g], BLOCK * (g - q), 1), value)
                    f_ref[kind, b, pl.ds(TILE + BLOCK * by + q, TILE, stride=4), :] = value
            for q in range(4):
                f_ref[2, b, pl.ds(TILE + BLOCK * by + TILE * q, TILE), :] = mask

    row16 = lax.broadcasted_iota(jnp.int32, (16, LANES), 0)
    group16 = lane_id((16, LANES)) // BLOCK

    def rim_rows(kind, rim, first):
        rolled = [turn(rim, BLOCK * d, 1) for d in range(4)]
        for q in range(4):
            value = jnp.zeros((16, LANES), F32)
            for g in range(4):
                value = jnp.where((row16 % 4 == g) & (group16 == g), rolled[(g - q) % 4], value)
            value = value + turn(value, -1, 0)
            value = value + turn(value, -2, 0)
            for b in range(FIELD_TILES):
                f_ref[kind, b, pl.ds(first + q, 1), :] = value[4 * b : 4 * b + 1, :]

    @pl.when(meta[1] > 0)
    def _():
        for kind, base in ((0, RIM_S), (1, RIM_Q), (2, RIM_M)):
            rim_rows(kind, below(base, 16) + far_ref[pl.ds(base - RIM_S, 16), :], 4)

    @pl.when(meta[1] < meta[2] - 1)
    def _():
        def own_rim(ref):
            rows = []
            for k in range(16):
                if k < REG_X:
                    src = inv[REGION + k]
                    at = jnp.maximum(src, 0) * TILE
                    line = jnp.ones((1, LANES), F32) if ref is None else ref[pl.ds(at, 1), :]
                    rows.append(jnp.where(src >= 0, line, 0.0))
                else:
                    rows.append(jnp.zeros((1, LANES), F32))
            return jnp.concatenate(rows, axis=0)

        for kind, base, ref in ((0, RIM_S, s_ref), (1, RIM_Q, q_ref), (2, RIM_M, None)):
            rim_rows(kind, above(base, 16) + own_rim(ref), FIELD_ROWS - TILE)

    height, width = surf_ref.shape
    for b in range(FIELD_TILES):
        lanes = min(LANES, width - b * LANES)
        f_ref[3, b, pl.ds(TILE, height), pl.ds(0, lanes)] = surf_ref[:, pl.ds(b * LANES, lanes)]
        f_ref[3, b, pl.ds(4, 4), :] = below(SURF + b * TILE, TILE)[4:]
        f_ref[3, b, pl.ds(FIELD_ROWS - TILE, 4), :] = above(SURF + b * TILE, TILE)[:4]

    lane = lane_id((TILE, LANES))
    last = width - (FIELD_TILES - 1) * LANES - 4
    east_even = meta[0] % 2 == 0
    for h in range(3):
        west_out = jnp.zeros((TILE, LANES), F32)
        east_out = jnp.zeros((TILE, LANES), F32)
        for g in range(8):
            v = 3 * g + h
            if v * TILE >= FIELD_ROWS:
                continue
            for kind in range(4):
                at = 16 * g + 4 * kind
                inside = (lane >= at) & (lane < at + 4)
                west = f_ref[kind, 0, pl.ds(v * TILE, TILE), :]
                east = f_ref[kind, FIELD_TILES - 1, pl.ds(v * TILE, TILE), :]
                west_out = jnp.where(inside, turn(west, at, 1), west_out)
                east_out = jnp.where(inside, turn(east, at - last, 1), east_out)
        ca_ref[pl.ds(h * TILE, TILE), :] = jnp.where(east_even, east_out, west_out)
        cb_ref[pl.ds(h * TILE, TILE), :] = jnp.where(east_even, west_out, east_out)


def region_fields(meta, places, s, q, a, b, far, surface):
    return pl.pallas_call(
        field_kernel,
        in_specs=[SMEM, SMEM] + [VMEM] * 6,
        out_specs=[VMEM] * 3,
        out_shape=[
            jax.ShapeDtypeStruct((4, FIELD_TILES, FIELD_ROWS, LANES), F32),
            jax.ShapeDtypeStruct((24, LANES), F32),
            jax.ShapeDtypeStruct((24, LANES), F32),
        ],
        compiler_params=pltpu.CompilerParams(vmem_limit_bytes=12 << 20),
        name="region_fields",
    )(meta, places, s, q, a, b, far, surface)


def basis_kernel(meta, moved, f_ref, ca_ref, cb_ref, g_ref, blocks_ref, back_ref, u_ref):
    even = meta[0] % 2 == 0
    lane = lane_id((TILE, LANES))
    tiles = range(FIELD_TILES)
    fields = []
    for kind in range(4):
        parts = [f_ref[kind, b] for b in tiles]
        strip = []
        for v in range(FIELD_ROWS // TILE):
            g, h = v // 3, v % 3
            ca = ca_ref[pl.ds(h * TILE, TILE), :]
            cb = cb_ref[pl.ds(h * TILE, TILE), :]
            at = 16 * g + 4 * kind
            west = turn(jnp.where(even, cb, ca), 124 - at, 1)
            east = turn(jnp.where(even, ca, cb), 64 - at, 1)
            tile = f_ref[kind, FIELD_TILES - 1, pl.ds(v * TILE, TILE), :]
            tile = jnp.where((lane >= 64) & (lane < 68), east, tile)
            strip.append(jnp.where(lane >= 124, west, tile))
        parts[-1] = jnp.concatenate(strip, axis=0)
        fields.append(parts)
    depth, inner, mask, surf = fields
    wide = lane_id((FIELD_ROWS, LANES))

    def sides(v):
        fwd = [turn(x, 1, 1) for x in v]
        bwd = [turn(x, -1, 1) for x in v]
        out = []
        for b in tiles:
            left = jnp.where(wide == 0, fwd[b - 1], fwd[b])
            right = jnp.where(wide == LANES - 1, bwd[(b + 1) % FIELD_TILES], bwd[b])
            out.append(left + right)
        return out

    def rows(v):
        return [turn(x, 1, 0) + turn(x, -1, 0) for x in v]

    def spread(v):
        side = sides(v)
        both = rows([v[b] + 0.5 * side[b] for b in tiles])
        return [mask[b] * (side[b] + both[b]) for b in tiles]

    def edges(v):
        side, both = sides(v), rows(v)
        return [side[b] + both[b] for b in tiles]

    near, count = edges(inner), edges(mask)
    rhs = [mask[b] * (depth[b] + near[b] - count[b] * inner[b]) for b in tiles]
    scale = [1.0 / (6.0 + surf[b]) for b in tiles]
    u0 = [rhs[b] * scale[b] for b in tiles]
    z1 = spread(u0)
    u1 = [z1[b] * scale[b] for b in tiles]
    z2 = spread(u1)
    u2 = [z2[b] * scale[b] for b in tiles]
    z3 = spread(u2)
    rows_in = slice(TILE, FIELD_ROWS - TILE)

    def dot(x, y):
        total = jnp.zeros((TILE, LANES), F32)
        for b in tiles:
            p = x[b][rows_in] * y[b][rows_in]
            p = jnp.sum(p.reshape(-1, TILE, LANES), axis=0)
            if b == FIELD_TILES - 1:
                p = jnp.where(lane < 64, p, 0.0)
            total = total + p
        return jnp.sum(jnp.sum(total, axis=1, keepdims=True), axis=0, keepdims=True)

    row = jnp.zeros((1, LANES), F32)
    pairs = ((u0, rhs), (u0, z1), (u1, z1), (u1, z2), (u2, z2), (u2, z3))
    for k, (x, y) in enumerate(pairs):
        row = jnp.where(lane[:1] == k, dot(x, y), row)
    row = jnp.where(lane[:1] == 6, meta[3].astype(F32), row)
    g_ref[...] = jnp.broadcast_to(row, g_ref.shape)
    for k, u in enumerate((u0, u1, u2)):
        for b in tiles:
            u_ref[k, b] = u[b][rows_in]
    group = lane // BLOCK
    for k in range(3):
        for by in range(REG_Y):
            for b in tiles:
                value = [u_ref[k, b, pl.ds(BLOCK * by + q, TILE, stride=4), :] for q in range(4)]
                for g in range(4):
                    if 4 * b + g >= REG_X:
                        continue
                    tile = value[0]
                    for q in range(4):
                        part = turn(value[q], BLOCK * (q - g), 1)
                        tile = part if q == 0 else jnp.where(group == q, part, tile)
                    blocks_ref[pl.ds((k * REGION + by * REG_X + 4 * b + g) * TILE, TILE), :] = tile
    for m in range(MOVED):
        at = pl.multiple_of(jnp.maximum(moved[m], 0) * TILE, TILE)
        for k in range(3):
            tile = blocks_ref[pl.ds(k * REGION * TILE + at, TILE), :]
            back_ref[pl.ds((k * MOVED + m) * TILE, TILE), :] = tile


def solve_basis(meta, moved, fields, ca, cb, devices):
    return pl.pallas_call(
        basis_kernel,
        in_specs=[SMEM, SMEM, VMEM, VMEM, VMEM],
        out_specs=[VMEM] * 3,
        out_shape=[
            jax.ShapeDtypeStruct((devices, LANES), F32),
            jax.ShapeDtypeStruct((3 * REGION * TILE, LANES), F32),
            jax.ShapeDtypeStruct((3 * MOVED * TILE, LANES), F32),
        ],
        scratch_shapes=[pltpu.VMEM((3, FIELD_TILES, FIELD_ROWS - 2 * TILE, LANES), F32)],
        compiler_params=pltpu.CompilerParams(vmem_limit_bytes=24 << 20),
        name="solve_basis",
    )(meta, moved, fields, ca, cb)


def pressure_kernel(code, g_ref, blocks_ref, back_ref, held_ref, out_ref, same_ref, work):
    del held_ref, same_ref
    slots = out_ref.shape[0]
    total = jnp.sum(g_ref[...].reshape(-1, TILE, LANES), axis=0)
    total = jnp.broadcast_to(jnp.sum(total, axis=0, keepdims=True), (TILE, LANES))
    lane = lane_id((TILE, LANES))
    pick = lambda k: jnp.sum(jnp.where(lane == k, total, 0.0), axis=1, keepdims=True)
    g = [pick(k) for k in range(6)]
    g = [x / g[0] for x in g]
    a = [g[k] - g[k + 1] for k in range(5)]
    zero = jnp.zeros_like(g[0])
    one = zero + 1.0

    def form(v, m):
        out = zero
        for i in range(3):
            for k in range(3):
                out = out + v[i] * v[k] * m[i + k]
        return out

    coef = [zero, zero, zero]
    rho = [one, zero, zero]
    way = [one, zero, zero]
    norm = g[0]
    for iteration in range(ITERS):
        length = norm / form(way, a)
        coef = [coef[k] + length * way[k] for k in range(3)]
        if iteration + 1 < ITERS:
            moved = [way[0], way[1] - way[0], way[2] - way[1]]
            rho = [rho[k] - length * moved[k] for k in range(3)]
            norm_next = form(rho, g)
            way = [rho[k] + (norm_next / norm) * way[k] for k in range(3)]
            norm = norm_next
    coef = [jnp.broadcast_to(c, (TILE, LANES)) for c in coef]
    for s in range(slots):
        c = code[s]
        at = pl.multiple_of(jnp.where(c < REGION, c, 0) * TILE, TILE)
        tiles = [blocks_ref[pl.ds(k * REGION * TILE + at, TILE), :] for k in range(3)]
        m = s - (slots - MOVED)
        if m >= 0:
            for k in range(3):
                other = back_ref[pl.ds((k * MOVED + m) * TILE, TILE), :]
                tiles[k] = jnp.where(c < REGION, tiles[k], other)
        work[pl.ds(s * TILE, TILE), :] = coef[0] * tiles[0] + coef[1] * tiles[1] + coef[2] * tiles[2]
    for first in range(0, slots, TILE):
        size = min(TILE, slots - first)
        for c in range(TILE):
            lines = work[pl.ds(first * TILE + c, size, stride=TILE), :]
            out_ref[pl.ds(first, size), pl.ds(c * LANES, LANES)] = lines


def slot_pressure(code, sums, blocks, back, held):
    slots = code.shape[0]
    return pl.pallas_call(
        pressure_kernel,
        in_specs=[SMEM, VMEM, VMEM, VMEM, ANY],
        out_specs=[VMEM, ANY],
        out_shape=[
            jax.ShapeDtypeStruct((slots, TILE * LANES), F32),
            jax.ShapeDtypeStruct(held.shape, F32),
        ],
        scratch_shapes=[pltpu.VMEM((slots * TILE, LANES), F32)],
        input_output_aliases={4: 1},
        compiler_params=pltpu.CompilerParams(vmem_limit_bytes=12 << 20),
        name="slot_pressure",
    )(code, sums, blocks, back, held)


def columns_kernel(meta, inv, t_ref, after_ref, a_ref, b_ref, west, east, sems):
    del after_ref
    even = meta[0] % 2 == 0
    count = 2 * REG_Y

    def copies(k):
        w, e = inv[REG_X * k], inv[REG_X * k + REG_X - 1]
        cw = pltpu.make_async_copy(t_ref.at[jnp.maximum(w, 0)], west.at[k], sems.at[0, k])
        ce = pltpu.make_async_copy(t_ref.at[jnp.maximum(e, 0)], east.at[k], sems.at[1, k])
        return cw, ce

    for k in range(count):
        for c in copies(k):
            c.start()
    column = lane_id((ROWS, LANES)) % BLOCK
    for first in (0, REG_Y):
        for k in range(first, first + REG_Y):
            for c in copies(k):
                c.wait()
        for level in range(HALF):
            at = pl.ds(level * ROWS, ROWS)
            if first:
                out_a, out_b = a_ref[at, :], b_ref[at, :]
                out_w, out_e = jnp.where(even, out_b, out_a), jnp.where(even, out_a, out_b)
            else:
                out_w = out_e = jnp.zeros((ROWS, LANES), F32)
            for k in range(first, first + REG_Y):
                has_w, has_e = inv[REG_X * k] >= 0, inv[REG_X * k + REG_X - 1] >= 0
                for part in range(2):
                    lane = k + 16 * part
                    here = column == lane
                    x = pl.ds((level + HALF * part) * ROWS, ROWS)
                    out_w = jnp.where(here & has_w, turn(west[k, x, :], lane, 1), out_w)
                    out_e = jnp.where(here & has_e, turn(east[k, x, :], lane - (BLOCK - 1), 1), out_e)
            a_ref[at, :] = jnp.where(even, out_e, out_w)
            b_ref[at, :] = jnp.where(even, out_w, out_e)


def column_strips(meta, places, view, after):
    count = 2 * REG_Y
    return pl.pallas_call(
        columns_kernel,
        in_specs=[SMEM, SMEM, HBM, ANY],
        out_specs=[VMEM] * 2,
        out_shape=[jax.ShapeDtypeStruct((HALF * ROWS, LANES), F32)] * 2,
        scratch_shapes=[
            pltpu.VMEM((count, IMAGE, LANES), F32),
            pltpu.VMEM((count, IMAGE, LANES), F32),
            pltpu.SemaphoreType.DMA((2, count)),
        ],
        compiler_params=pltpu.CompilerParams(vmem_limit_bytes=52 << 20),
        cost_estimate=pl.CostEstimate(flops=1, bytes_accessed=1, transcendentals=0),
        name="column_strips",
    )(meta, places, view.reshape(view.shape[0], IMAGE, LANES), after)


def links_kernel(meta, table, t_ref, ga_ref, gb_ref, a_ref, b_ref, whole, half, sem_we, sem_ns):
    even_x = meta[0] % 2 == 0
    even_y = meta[1] % 2 == 0

    def we_copy(way, k):
        link = jnp.maximum(table[way * (CAP_WE + CAP_NS) + k], 0)
        return pltpu.make_async_copy(t_ref.at[link // 4], whole.at[way, k], sem_we.at[way, k])

    def ns_copy(way, k):
        link = jnp.maximum(table[way * (CAP_WE + CAP_NS) + CAP_WE + k], 2)
        rows = pl.ds(pl.multiple_of((link % 4 - 2) * TILE, TILE), TILE)
        dest = half.at[way, k, :, pl.ds(TILE, TILE), :]
        return pltpu.make_async_copy(t_ref.at[link // 4, :, rows, :], dest, sem_ns.at[way, k])

    for way in range(2):
        for k in range(CAP_WE):
            @pl.when(table[way * (CAP_WE + CAP_NS) + k] >= 0)
            def _():
                we_copy(way, k).start()

        for k in range(CAP_NS):
            ns_copy(way, k).start()

    column = lane_id((HALF * ROWS, LANES)) % 16
    from_west = jnp.where(even_x, gb_ref[...], ga_ref[...])
    from_east = jnp.where(even_x, ga_ref[...], gb_ref[...])
    ways = ((turn(from_west, -5, 1), from_east), (from_west, turn(from_east, 5, 1)))
    relays = [jnp.where(column < 5, w, jnp.where(column < RELAY, e, 0.0)) for w, e in ways]

    def message(way, out):
        out[pl.ds(0, HALF * ROWS), :] = relays[way]
        out[pl.ds(HALF * ROWS + LEVELS * TILE, TILE), :] = jnp.zeros((TILE, LANES), F32)
        lane32 = lane_id((ROWS, LANES)) % BLOCK
        for k in range(CAP_WE):
            link = table[way * (CAP_WE + CAP_NS) + k]

            @pl.when(link >= 0)
            def _():
                we_copy(way, k).wait()
                start = (link % 4) * (BLOCK - 1)
                for level in range(HALF):
                    at = pl.ds(level * ROWS, ROWS)
                    value = out[at, :]
                    for part in range(2):
                        lane = RELAY + k + 16 * part
                        x = turn(whole[way, k, level + HALF * part], lane, 1)
                        x = jnp.where(start > 0, turn(x, 1 - BLOCK, 1), x)
                        value = jnp.where(lane32 == lane, x, value)
                    out[at, :] = value

        links = [jnp.maximum(table[way * (CAP_WE + CAP_NS) + CAP_WE + k], 2) for k in range(CAP_NS)]
        first = [TILE + 6 * (links[k] % 4 - 2) - 2 * (k // 4) for k in range(CAP_NS)]
        by = [(BLOCK * (k % 4) + BLOCK * (links[k] % 4 - 2)) % LANES for k in range(CAP_NS)]
        for k in range(CAP_NS):
            ns_copy(way, k).wait()
        row = lax.broadcasted_iota(jnp.int32, (TILE, LANES), 0) // 2
        place = row * 4 + lane_id((TILE, LANES)) // BLOCK
        for level in range(LEVELS):
            value = jnp.zeros((TILE, LANES), F32)
            for k in range(CAP_NS):
                x = pltpu.roll(half[way, k, level, pl.ds(first[k], TILE), :], by[k], 1)
                value = jnp.where(place == k, x, value)
            out[pl.ds(HALF * ROWS + level * TILE, TILE), :] = value

    @pl.when(even_y)
    def _():
        message(0, a_ref)
        message(1, b_ref)

    @pl.when(jnp.logical_not(even_y))
    def _():
        message(0, b_ref)
        message(1, a_ref)


def link_strips(meta, table, view, ga, gb):
    rows = LINK_ROWS
    return pl.pallas_call(
        links_kernel,
        in_specs=[SMEM, SMEM, HBM, VMEM, VMEM],
        out_specs=[VMEM] * 2,
        out_shape=[jax.ShapeDtypeStruct((rows, LANES), F32)] * 2,
        scratch_shapes=[
            pltpu.VMEM((2, CAP_WE, LEVELS, ROWS, LANES), F32),
            pltpu.VMEM((2, CAP_NS, LEVELS, 3 * TILE, LANES), F32),
            pltpu.SemaphoreType.DMA((2, CAP_WE)),
            pltpu.SemaphoreType.DMA((2, CAP_NS)),
        ],
        compiler_params=pltpu.CompilerParams(vmem_limit_bytes=52 << 20),
        name="link_strips",
    )(meta, table, view, ga, gb)


BOX_LOW = 2 * HALF * ROWS
BOX_HIGH = BOX_LOW + LINK_ROWS
BOX = BOX_HIGH + LINK_ROWS


def tracer_kernel(meta, table, need, diffusion, t_ref, ga_ref, gb_ref, ha_ref, hb_ref, out_ref, own, inner, across, beside, box, perm, sems, out_sems):
    slots = own.shape[0]
    chunks = slots // STEP_SLOTS

    def fetch(c):
        part = pl.ds(c * STEP_SLOTS, STEP_SLOTS)
        return pltpu.make_async_copy(t_ref.at[part], own.at[part], sems.at[c])

    def keep(c):
        part = pl.ds(c * STEP_SLOTS, STEP_SLOTS)
        return pltpu.make_async_copy(own.at[part], out_ref.at[part], out_sems.at[c])

    for c in range(chunks):
        fetch(c).start()
    even_x = meta[0] % 2 == 0
    even_y = meta[1] % 2 == 0
    src = lax.broadcasted_iota(jnp.int32, perm.shape, 0) % LANES
    dst = lax.broadcasted_iota(jnp.int32, perm.shape, 1)
    to = dst % LANES
    gap = jnp.abs(src - to)
    linked = ((gap == 1) & (src // BLOCK == to // BLOCK)) | (gap == BLOCK)
    crossed = gap == LANES - BLOCK
    swapped = (gap == BLOCK - 1) & (src // BLOCK == to // BLOCK)
    hit = ((dst < LANES) & linked) | ((dst >= LANES) & (dst < 2 * LANES) & crossed) | ((dst >= 2 * LANES) & swapped)
    perm[...] = jnp.where(hit, 1.0, 0.0).astype(jnp.bfloat16)
    across[slots] = jnp.zeros(across.shape[1:], F32)
    beside[slots] = jnp.zeros(beside.shape[1:], F32)
    for first, second, size, low, high in (
        (ga_ref, gb_ref, HALF * ROWS, 0, HALF * ROWS),
        (ha_ref, hb_ref, LINK_ROWS, BOX_LOW, BOX_HIGH),
    ):
        even = even_x if low == 0 else even_y
        box[pl.ds(low, size), :] = jnp.where(even, second[...], first[...])
        box[pl.ds(high, size), :] = jnp.where(even, first[...], second[...])

    cells = (ROWS, LANES)
    lane = lane_id(cells)
    column = lane % BLOCK
    row = lax.broadcasted_iota(jnp.int32, cells, 0)
    row8, lane8 = row[:TILE], lane[:TILE]
    outer = (lane8 < BLOCK) | (lane8 >= LANES - BLOCK)
    for way, low in enumerate((BOX_LOW, BOX_HIGH)):
        for level in range(LEVELS):
            x = box[pl.ds(low + HALF * ROWS + level * TILE, TILE), :]
            for d in range(4):
                y = jnp.where(outer, turn(x, BLOCK * d, 1), 0.0)
                across[slots + 1 + 4 * way + d, pl.ds(TILE + level * ROWS, TILE), :] = y
    for level in range(LEVELS):
        part = level // HALF
        w = box[pl.ds((level % HALF) * ROWS, ROWS), :]
        e = box[pl.ds((HALF + level % HALF) * ROWS, ROWS), :]
        for k in range(2 * REG_Y):
            y = jnp.where(column == BLOCK - 1, turn(e, BLOCK - 1 - k - 16 * part, 1), 0.0)
            y = jnp.where(column == 0, turn(w, -k - 16 * part, 1), y)
            beside[slots + 1 + k, pl.ds(level * ROWS, ROWS), :] = y

    def arrive(c, carry):
        fetch(c).wait()
        for n in range(STEP_SLOTS):
            s = c * STEP_SLOTS + n
            x = own[s]
            high = x.astype(jnp.bfloat16)
            low = (x - high.astype(F32)).astype(jnp.bfloat16)
            pair = jnp.concatenate([high, low], axis=1)
            moved = jnp.dot(pair, perm[...], preferred_element_type=F32)
            inner[s] = moved[:, :LANES]
            across[s, pl.ds(TILE, IMAGE), :] = moved[:, LANES : 2 * LANES]
            beside[s] = moved[:, 2 * LANES :]
        return carry

    edge = (
        jnp.where(column == 0, 1.0, 0.0),
        jnp.where(column == BLOCK - 1, 1.0, 0.0),
        jnp.where((row < 2) & (lane < BLOCK), 1.0, 0.0),
        jnp.where((row >= ROWS - 2) & (lane >= LANES - BLOCK), 1.0, 0.0),
    )

    def unpack(n, s):
        for t in range(2):
            at = s * 4 + t

            @pl.when(table[1, at] == 1)
            def _():
                first, by = pl.multiple_of(table[2, at], TILE), table[3, at]
                for level in range(LEVELS):
                    part = level // HALF
                    x = box[pl.ds(first + (level % HALF) * ROWS, ROWS), :]
                    x = pltpu.roll(x, (by + LANES - 16 * part) % LANES, 1)
                    x = jnp.where(column == t * (BLOCK - 1), x, 0.0)
                    beside[slots + 11 + 2 * n + t, pl.ds(level * ROWS, ROWS), :] = x

    def step(n, s):
        count = jnp.full(cells, 4.0, F32)
        for t in range(4):
            count = count - edge[t] * table[4, s * 4 + t].astype(F32)
        west, east, south, north = [table[0, s * 4 + t] for t in range(4)]
        south_at, north_at = TILE + table[2, s * 4 + 2], TILE + table[2, s * 4 + 3]
        for level in range(LEVELS):
            for h in range(2):
                at = level * ROWS + h * TILE
                x = own[s, pl.ds(at, TILE), :]
                under = across[s, pl.ds(TILE + at - 2, TILE), :]
                over = across[s, pl.ds(TILE + at + 2, TILE), :]
                if h == 0:
                    under = jnp.where(row8 < 2, across[south, pl.ds(south_at + level * ROWS, TILE), :], under)
                else:
                    over = jnp.where(row8 >= TILE - 2, across[north, pl.ds(north_at + level * ROWS, TILE), :], over)
                total = inner[s, pl.ds(at, TILE), :] + jnp.where(lane8 < LANES // 2, under, over)
                w, e = beside[west, pl.ds(at, TILE), :], beside[east, pl.ds(at, TILE), :]
                total = total + jnp.where(lane8 % BLOCK == 0, w, jnp.where(lane8 % BLOCK == BLOCK - 1, e, 0.0))
                part = count[h * TILE : (h + 1) * TILE]
                own[s, pl.ds(at, TILE), :] = x + diffusion[level] * (total - part * x)

    def work(c, seen):
        upto = jnp.maximum(seen, need[c] + 1)
        lax.fori_loop(seen, upto, arrive, 0)
        for n in range(STEP_SLOTS):
            unpack(n, c * STEP_SLOTS + n)
        for n in range(STEP_SLOTS):
            step(n, c * STEP_SLOTS + n)
        keep(c).start()
        return upto

    lax.fori_loop(0, chunks, work, 0)
    for c in range(chunks):
        keep(c).wait()


def step_tracers(meta, table, need, diffusion, view, ga, gb, ha, hb):
    slots = view.shape[0]
    chunks = slots // STEP_SLOTS
    size = slots * IMAGE * LANES
    out = pl.pallas_call(
        tracer_kernel,
        in_specs=[SMEM] * 4 + [HBM] + [VMEM] * 4,
        out_specs=HBM,
        out_shape=jax.ShapeDtypeStruct((slots, IMAGE, LANES), F32),
        scratch_shapes=[
            pltpu.VMEM((slots, IMAGE, LANES), F32),
            pltpu.VMEM((slots, IMAGE, LANES), F32),
            pltpu.VMEM((slots + 9, IMAGE + 2 * TILE, LANES), F32),
            pltpu.VMEM((slots + 11 + 2 * STEP_SLOTS, IMAGE, LANES), F32),
            pltpu.VMEM((BOX, LANES), F32),
            pltpu.VMEM((2 * LANES, 3 * LANES), jnp.bfloat16),
            pltpu.SemaphoreType.DMA((chunks,)),
            pltpu.SemaphoreType.DMA((chunks,)),
        ],
        compiler_params=pltpu.CompilerParams(vmem_limit_bytes=52 << 20),
        cost_estimate=pl.CostEstimate(flops=14 * size, bytes_accessed=8 * size, transcendentals=0),
        name="step_tracers",
    )(meta, table, need, diffusion, view.reshape(slots, IMAGE, LANES), ga, gb, ha, hb)
    return out.reshape(view.shape)


def with_halo(block, sides, width):
    for axis, dim in sides:
        low = shifted(lax.slice_in_dim(block, block.shape[dim] - width, None, axis=dim), axis, 1)
        high = shifted(lax.slice_in_dim(block, 0, width, axis=dim), axis, -1)
        block = jnp.concatenate([low, block, high], axis=dim)
    return block


def edge_strips(grid):
    sides = [grid[..., :, 0], grid[..., :, -1], grid[..., 0, :], grid[..., -1, :]]
    return jnp.stack(sides, axis=1).reshape(grid.shape[0] * 4, -1)


def general_step(tracers, diffusion, halo_source):
    slots = tracers.shape[0]
    grid = tracers.reshape(slots, TRACER, LEVELS, BLOCK, BLOCK)
    strips = edge_strips(grid)
    width = strips.shape[1]
    count_gx, count_gy = lax.axis_size("gx"), lax.axis_size("gy")
    source = halo_source.reshape(-1)
    missing = source >= 4 * slots * count_gx * count_gy
    slot = jnp.where(missing, 0, source) // 4
    owner = slot // slots
    step_gx = (owner // count_gy - lax.axis_index("gx") + count_gx + 1) % count_gx
    step_gy = (owner % count_gy - lax.axis_index("gy") + count_gy + 1) % count_gy
    every = slots * 4
    table = with_halo(strips.reshape(1, 1, every, width), (("gx", 0), ("gy", 1)), 1).reshape(9 * every, width)
    index = (step_gx * 3 + step_gy) * every + slot % slots * 4 + source % 4
    halo = jnp.take(table, jnp.where(missing, 0, index), axis=0, mode="clip")
    halo = halo.reshape(slots, 4, TRACER, LEVELS, BLOCK)
    gate = jnp.where(missing, 0.0, 1.0).astype(F32).reshape(slots, 4, 1, 1, 1)
    inner_x = grid[..., :, :-1] - grid[..., :, 1:]
    inner_y = grid[..., :-1, :] - grid[..., 1:, :]
    west = (halo[:, 0] - grid[..., :, 0]) * gate[:, 0]
    east = (halo[:, 1] - grid[..., :, -1]) * gate[:, 1]
    south = (halo[:, 2] - grid[..., 0, :]) * gate[:, 2]
    north = (halo[:, 3] - grid[..., -1, :]) * gate[:, 3]
    laplace = (
        jnp.concatenate([west[..., None], inner_x], axis=-1)
        + jnp.concatenate([-inner_x, east[..., None]], axis=-1)
        + jnp.concatenate([south[..., None, :], inner_y], axis=-2)
        + jnp.concatenate([-inner_y, north[..., None, :]], axis=-2)
    )
    updated = grid + diffusion[None, None, :, None, None] * laplace
    return plain(seen_by_rows(updated.reshape(tracers.shape)))


def strip_tables(halo_source, code, at_x, at_y, count_x, count_y):
    slots = halo_source.shape[0]
    source = halo_source.reshape(-1)
    missing = source >= 4 * slots * count_x * count_y
    source = jnp.where(missing, 0, source)
    owner = source // (4 * slots)
    local_slot = source // 4 - owner * slots
    same_x = owner // count_y == at_x
    owner_y = owner % count_y
    up = owner_y == (at_y + 1) % count_y
    here = owner_y == at_y
    index = jnp.arange(4 * slots, dtype=jnp.int32)
    side = index % 4
    kind = jnp.where(side >= 2, 1, 0)
    linked = ~missing & same_x & ~here
    group = jnp.where(linked, jnp.where(up, kind, 2 + kind), -1)

    def rank(key):
        before = (key[None, :] < key[:, None]) & (group[None, :] == group[:, None])
        return jnp.sum(before.astype(jnp.int32), axis=1)

    take = rank(index)
    give = rank(source)
    entry = jnp.arange(2 * (CAP_WE + CAP_NS), dtype=jnp.int32)
    rest = entry % (CAP_WE + CAP_NS)
    of_kind = jnp.where(rest >= CAP_WE, 1, 0)
    want = (2 * (entry // (CAP_WE + CAP_NS)) + of_kind) * 1024 + rest - CAP_WE * of_kind
    has = jnp.where(group >= 0, group * 1024 + give, -1)
    send = jnp.sum(jnp.where(want[:, None] == has[None, :], index[None, :] + 1, 0), axis=1) - 1
    over = jnp.any(linked & (take >= jnp.where(kind == 1, CAP_NS, CAP_WE)))
    row = jnp.broadcast_to((code // REG_X)[:, None], (slots, 4)).reshape(-1)
    local = same_x & here
    north = kind == 1
    lane = jnp.where(same_x, RELAY + take, row % REG_Y + jnp.where(side == 0, 0, REG_Y))
    box = jnp.where(up, BOX_HIGH, BOX_LOW)
    by = (jnp.where(side == 0, 0, BLOCK - 1) - lane) % LANES
    unpacked = slots + 11 + 2 * (index // 4 % STEP_SLOTS) + side
    image_we = jnp.where(local, local_slot, jnp.where(here, slots + 1 + row, unpacked))
    take = jnp.minimum(take, CAP_NS - 1)
    turns = jnp.where(side == 2, -take, 3 - take) % 4
    image_ns = jnp.where(local, local_slot, slots + 1 + jnp.where(up, 4, 0) + turns)
    row_ns = jnp.where(local | missing, jnp.where(side == 2, ROWS - 2, 0), 2 * (take // 4))
    row_ns = row_ns - jnp.where(side == 3, TILE - 2, 0)
    image = jnp.where(missing, slots, jnp.where(north, image_ns, image_we))
    unpack = jnp.where(missing | here | north, 0, 1)
    table = jnp.stack([image, unpack, jnp.where(north, row_ns, box), by, jnp.where(missing, 1, 0)])
    last = jnp.where(local & ~missing, local_slot, 0).reshape(-1, 4 * STEP_SLOTS)
    need = jnp.maximum(jnp.max(last, axis=1) // STEP_SLOTS, jnp.arange(slots // STEP_SLOTS))
    return table, need, send, over.astype(jnp.int32)


def on_device(tracers, diffusion, layer_weight, surface_term, clinic_blocks, halo_source):
    slots = tracers.shape[0]
    count_x, count_y = lax.axis_size("gx"), lax.axis_size("gy")
    at_x, at_y = lax.axis_index("gx"), lax.axis_index("gy")
    grid_columns = REG_X * count_x
    grid_rows = REG_Y * count_y
    own_row = (clinic_blocks // grid_columns - REG_Y * at_y) % grid_rows
    code = own_row * REG_X + clinic_blocks % grid_columns % REG_X
    zero = jnp.zeros((), jnp.int32)
    meta = jnp.stack([at_x, at_y, zero + count_y, zero]).astype(jnp.int32)

    view = seen_by_rows(tracers)
    s, q, a, b, far, places = depth_sums(view, meta, code, layer_weight, diffusion, surface_term)
    ra, rb = swap(a, b, "gy", count_y)
    rfar = shifted(far, "gy", 2)

    source, places = lax.optimization_barrier((halo_source, places))
    table, need, send, over = strip_tables(source, code, at_x, at_y, count_x, count_y)
    ga, gb = swap(*column_strips(meta, places, view, rfar), "gx", count_x)

    moved = jnp.where(at_y % 2 == 0, rb[IDS, :MOVED], ra[IDS, :MOVED]).astype(jnp.int32)
    spot = jnp.arange(2 * REGION, dtype=jnp.int32)[:, None]
    index = jnp.arange(MOVED, dtype=jnp.int32)[None, :]
    both = places + jnp.sum(jnp.where(moved[None, :] == spot, index + 1 + slots, 0), axis=1)
    fields, ca, cb = region_fields(meta, both, s, q, ra, rb, rfar, surface_term)
    ca, cb = swap(ca, cb, "gx", count_x)
    ha, hb = swap(*link_strips(meta, send, view, ga, gb), "gy", count_y)

    meta_over = jnp.stack([at_x, at_y, zero + count_y, over]).astype(jnp.int32)
    sums, blocks, back = solve_basis(meta_over, moved, fields, ca, cb, count_x * count_y)
    back = shifted(back, "gy", -1)
    sums = lax.all_to_all(sums[:, None], ("gx", "gy"), 0, 0, tiled=True)
    updated = step_tracers(meta, table, need, diffusion, view, ga, gb, ha, hb)
    sums, updated = lax.optimization_barrier((sums, updated))
    updated = lax.cond(
        jnp.max(sums[:, 0, 6]) > 0.0,
        lambda fast: general_step(tracers, diffusion, halo_source),
        lambda fast: fast,
        updated,
    )
    pressure, updated = slot_pressure(code, sums.reshape(-1, LANES), blocks, back, updated)
    updated = updated.reshape(slots, LEVELS, TILE, TRACER, LANES).transpose(0, 3, 1, 2, 4)
    return (updated.reshape(tracers.shape), pressure)


def solution(mesh):
    placed = (
        P(("gx", "gy"), None, None, None),
        P(),
        P(),
        P("gy", "gx"),
        P(("gx", "gy")),
        P(("gx", "gy"), None),
    )
    return jax.shard_map(
        on_device,
        mesh=mesh,
        in_specs=placed,
        out_specs=(P(("gx", "gy"), None, None, None), P(("gx", "gy"), None)),
        check_vma=False,
    )
```

```python
import jax
import jax.numpy as jnp
from jax import lax
from jax.experimental import pallas as pl
from jax.experimental.layout import Layout, with_layout_constraint
from jax.experimental.pallas import tpu as pltpu
from jax.sharding import PartitionSpec as P

BLOCK = 32
LEVELS = 20
TRACER = 2
REG_X = 14
REG_Y = 5
ITERS = 3
REGION = REG_X * REG_Y
MOVED = 22
LANES = 128
TILE = 8
ROWS = 16
HALF = LEVELS // 2
STEP_SLOTS = 7
IMAGE = LEVELS * ROWS
FIELD_ROWS = 176
FIELD_TILES = 4
CAP_WE = 6
CAP_NS = 16
RELAY = 10
LINK_ROWS = HALF * ROWS + (LEVELS + 1) * TILE
RIM_S = 2 * MOVED * TILE
RIM_Q = RIM_S + 16
RIM_M = RIM_Q + 16
SURF = RIM_M + 16
IDS = SURF + FIELD_TILES * TILE
MESSAGE = IDS + TILE
F32 = jnp.float32
SMEM = pl.BlockSpec(memory_space=pltpu.SMEM)
VMEM = pl.BlockSpec(memory_space=pltpu.VMEM)
ANY = pl.BlockSpec(memory_space=pl.ANY)
HBM = pl.BlockSpec(memory_space=pltpu.HBM)


def lane_id(shape):
    return lax.broadcasted_iota(jnp.int32, shape, len(shape) - 1)


def turn(x, by, axis):
    size = x.shape[axis]
    if isinstance(by, int):
        by = by % size
        if by == 0:
            return x
    return pltpu.roll(x, by, axis)


def swap(to_next, to_last, axis, count):
    first = [(i, i ^ 1) for i in range(count)]
    second = [(i, (i + 1) % count if i % 2 else (i - 1) % count) for i in range(count)]
    return lax.ppermute(to_next, axis, first), lax.ppermute(to_last, axis, second)


def plain(x):
    return with_layout_constraint(x, Layout(major_to_minor=tuple(range(x.ndim))))


def seen_by_rows(tracers):
    slots = tracers.shape[0]
    view = tracers.reshape(slots, TRACER, LEVELS, TILE, LANES).transpose(0, 2, 3, 1, 4)
    return view.reshape(slots, LEVELS, ROWS, LANES)


def shifted(x, axis, by):
    length = lax.axis_size(axis)
    return lax.ppermute(x, axis, [(i, (i + by) % length) for i in range(length)])


def sums_kernel(meta, code, weight, diffusion, t_ref, surf_ref, s_ref, q_ref, a_ref, b_ref, far_ref, inv, own, part, edges, sems, sem_low, sem_high):
    slots = own.shape[0]
    chunks = slots // STEP_SLOTS
    height = surf_ref.shape[0]

    def fetch(c):
        part = pl.ds(c * STEP_SLOTS, STEP_SLOTS)
        return pltpu.make_async_copy(t_ref.at[part], own.at[part], sems.at[c])

    def fetch_low():
        return pltpu.make_async_copy(surf_ref.at[pl.ds(0, TILE), :], edges.at[0], sem_low)

    def fetch_high():
        return pltpu.make_async_copy(surf_ref.at[pl.ds(height - TILE, TILE), :], edges.at[1], sem_high)

    for c in range(chunks):
        fetch(c).start()
    fetch_low().start()
    fetch_high().start()
    for r in range(2 * REGION):
        inv[r] = -1
    for s in range(slots):
        inv[code[s]] = s
    tracer = lax.broadcasted_iota(jnp.int32, (TILE, LANES), 0) % 2
    pairs = [(n, h) for n in range(STEP_SLOTS) for h in range(2)]

    def sum_chunk(c, carry):
        fetch(c).wait()
        acc_s = {p: jnp.zeros((TILE, LANES), F32) for p in pairs}
        acc_q = {p: jnp.zeros((TILE, LANES), F32) for p in pairs}
        for level in range(LEVELS):
            w = jnp.where(tracer == 0, weight[0, level], weight[1, level])
            wd = w * diffusion[level]
            for n, h in pairs:
                x = own[c * STEP_SLOTS + n, pl.ds(level * ROWS + h * TILE, TILE), :]
                acc_s[n, h] = acc_s[n, h] + w * x
                acc_q[n, h] = acc_q[n, h] + wd * x
        for n, h in pairs:
            part[0, pl.ds(n * ROWS + h * TILE, TILE), :] = acc_s[n, h]
            part[1, pl.ds(n * ROWS + h * TILE, TILE), :] = acc_q[n, h]
        for n in range(STEP_SLOTS):
            row = pl.multiple_of((c * STEP_SLOTS + n) * TILE, TILE)
            for kind, out in ((0, s_ref), (1, q_ref)):
                even = part[kind, pl.ds(n * ROWS, TILE, stride=2), :]
                odd = part[kind, pl.ds(n * ROWS + 1, TILE, stride=2), :]
                out[pl.ds(row, TILE), :] = even + odd
        return carry

    lax.fori_loop(0, chunks, sum_chunk, 0)
    fetch_low().wait()
    fetch_high().wait()

    def rim(dest, base, first, chunk):
        for k in range(REG_X):
            src = inv[first + k]
            at = jnp.maximum(src, 0) * TILE + chunk
            has = jnp.where(src >= 0, 1.0, 0.0)
            dest[pl.ds(base + k, 1), :] = jnp.where(src >= 0, s_ref[pl.ds(at, 1), :], 0.0)
            dest[pl.ds(base + 16 + k, 1), :] = jnp.where(src >= 0, q_ref[pl.ds(at, 1), :], 0.0)
            dest[pl.ds(base + 32 + k, 1), :] = jnp.full((1, LANES), has, F32)
        for k in range(REG_X, 16):
            for kind in range(3):
                dest[pl.ds(base + 16 * kind + k, 1), :] = jnp.zeros((1, LANES), F32)

    def surface(dest, edge):
        for b in range(FIELD_TILES):
            if b < 3:
                dest[pl.ds(SURF + b * TILE, TILE), :] = edges[edge, :, pl.ds(b * LANES, LANES)]
            else:
                width = edges.shape[2] - b * LANES
                dest[pl.ds(SURF + b * TILE, TILE), :] = jnp.zeros((TILE, LANES), F32)
                dest[pl.ds(SURF + b * TILE, TILE), pl.ds(0, width)] = edges[edge, :, pl.ds(b * LANES, width)]

    lane = lane_id((TILE, LANES))
    ids = jnp.full((TILE, LANES), -1.0, F32)
    for k in range(MOVED):
        ids = jnp.where(lane == k, (code[slots - MOVED + k] - REGION).astype(F32), ids)

    def messages(up, down):
        height = MOVED * TILE
        first = (slots - MOVED) * TILE
        up[pl.ds(0, height), :] = s_ref[pl.ds(first, height), :]
        up[pl.ds(height, height), :] = q_ref[pl.ds(first, height), :]
        rim(up, RIM_S, REGION - REG_X, TILE - 1)
        surface(up, 1)
        up[pl.ds(IDS, TILE), :] = ids
        down[pl.ds(0, 2 * height), :] = jnp.zeros((2 * height, LANES), F32)
        rim(down, RIM_S, 0, 0)
        surface(down, 0)
        down[pl.ds(IDS, TILE), :] = ids

    rim(far_ref, 0, 2 * REGION - REG_X, TILE - 1)

    @pl.when(meta[1] % 2 == 0)
    def _():
        messages(a_ref, b_ref)

    @pl.when(meta[1] % 2 == 1)
    def _():
        messages(b_ref, a_ref)


def depth_sums(view, meta, code, weight, diffusion, surface):
    slots = view.shape[0]
    shapes = [(slots * TILE, LANES), (slots * TILE, LANES), (MESSAGE, LANES), (MESSAGE, LANES), (48, LANES)]
    return pl.pallas_call(
        sums_kernel,
        in_specs=[SMEM] * 4 + [HBM, HBM],
        out_specs=[VMEM] * 5 + [SMEM],
        out_shape=[jax.ShapeDtypeStruct(x, F32) for x in shapes] + [jax.ShapeDtypeStruct((2 * REGION,), jnp.int32)],
        scratch_shapes=[
            pltpu.VMEM((slots, IMAGE, LANES), F32),
            pltpu.VMEM((2, STEP_SLOTS * ROWS, LANES), F32),
            pltpu.VMEM((2, TILE, surface.shape[1]), F32),
            pltpu.SemaphoreType.DMA((slots // STEP_SLOTS,)),
            pltpu.SemaphoreType.DMA,
            pltpu.SemaphoreType.DMA,
        ],
        compiler_params=pltpu.CompilerParams(vmem_limit_bytes=53 << 20),
        name="depth_sums",
    )(meta, code, weight, diffusion, view.reshape(slots, IMAGE, LANES), surface)


def field_kernel(meta, inv, s_ref, q_ref, a_ref, b_ref, far_ref, surf_ref, after_ref, f_ref, ca_ref, cb_ref):
    del after_ref
    slots = s_ref.shape[0] // TILE
    even = meta[1] % 2 == 0
    group = lane_id((TILE, LANES)) // BLOCK

    def below(start, size):
        return jnp.where(even, b_ref[pl.ds(start, size), :], a_ref[pl.ds(start, size), :])

    def above(start, size):
        return jnp.where(even, a_ref[pl.ds(start, size), :], b_ref[pl.ds(start, size), :])

    f_ref[...] = jnp.zeros(f_ref.shape, F32)
    for by in range(REG_Y):
        for b in range(FIELD_TILES):
            held = [g for g in range(4) if 4 * b + g < REG_X]
            mask = jnp.zeros((TILE, LANES), F32)
            tiles = {}
            for g in held:
                src = inv[by * REG_X + 4 * b + g]
                own_at = pl.multiple_of(jnp.clip(src, 0, slots - 1) * TILE, TILE)
                came_at = pl.multiple_of(jnp.clip(src - slots, 0, MOVED - 1) * TILE, TILE)
                for kind, ref in ((0, s_ref), (1, q_ref)):
                    own = ref[pl.ds(own_at, TILE), :]
                    other = below(pl.multiple_of(kind * MOVED * TILE + came_at, TILE), TILE)
                    tiles[kind, g] = jnp.where(src >= slots, other, jnp.where(src >= 0, own, 0.0))
                mask = jnp.where(group == g, jnp.where(src >= 0, 1.0, 0.0), mask)
            for kind in range(2):
                for q in range(4):
                    value = jnp.zeros((TILE, LANES), F32)
                    for g in held:
                        value = jnp.where(group == g, turn(tiles[kind, g], BLOCK * (g - q), 1), value)
                    f_ref[kind, b, pl.ds(TILE + BLOCK * by + q, TILE, stride=4), :] = value
            for q in range(4):
                f_ref[2, b, pl.ds(TILE + BLOCK * by + TILE * q, TILE), :] = mask

    row16 = lax.broadcasted_iota(jnp.int32, (16, LANES), 0)
    group16 = lane_id((16, LANES)) // BLOCK

    def rim_rows(kind, rim, first):
        rolled = [turn(rim, BLOCK * d, 1) for d in range(4)]
        for q in range(4):
            value = jnp.zeros((16, LANES), F32)
            for g in range(4):
                value = jnp.where((row16 % 4 == g) & (group16 == g), rolled[(g - q) % 4], value)
            value = value + turn(value, -1, 0)
            value = value + turn(value, -2, 0)
            for b in range(FIELD_TILES):
                f_ref[kind, b, pl.ds(first + q, 1), :] = value[4 * b : 4 * b + 1, :]

    @pl.when(meta[1] > 0)
    def _():
        for kind, base in ((0, RIM_S), (1, RIM_Q), (2, RIM_M)):
            rim_rows(kind, below(base, 16) + far_ref[pl.ds(base - RIM_S, 16), :], 4)

    @pl.when(meta[1] < meta[2] - 1)
    def _():
        def own_rim(ref):
            rows = []
            for k in range(16):
                if k < REG_X:
                    src = inv[REGION + k]
                    at = jnp.maximum(src, 0) * TILE
                    line = jnp.ones((1, LANES), F32) if ref is None else ref[pl.ds(at, 1), :]
                    rows.append(jnp.where(src >= 0, line, 0.0))
                else:
                    rows.append(jnp.zeros((1, LANES), F32))
            return jnp.concatenate(rows, axis=0)

        for kind, base, ref in ((0, RIM_S, s_ref), (1, RIM_Q, q_ref), (2, RIM_M, None)):
            rim_rows(kind, above(base, 16) + own_rim(ref), FIELD_ROWS - TILE)

    height, width = surf_ref.shape
    for b in range(FIELD_TILES):
        lanes = min(LANES, width - b * LANES)
        f_ref[3, b, pl.ds(TILE, height), pl.ds(0, lanes)] = surf_ref[:, pl.ds(b * LANES, lanes)]
        f_ref[3, b, pl.ds(4, 4), :] = below(SURF + b * TILE, TILE)[4:]
        f_ref[3, b, pl.ds(FIELD_ROWS - TILE, 4), :] = above(SURF + b * TILE, TILE)[:4]

    lane = lane_id((TILE, LANES))
    last = width - (FIELD_TILES - 1) * LANES - 4
    east_even = meta[0] % 2 == 0
    for h in range(3):
        west_out = jnp.zeros((TILE, LANES), F32)
        east_out = jnp.zeros((TILE, LANES), F32)
        for g in range(8):
            v = 3 * g + h
            if v * TILE >= FIELD_ROWS:
                continue
            for kind in range(4):
                at = 16 * g + 4 * kind
                inside = (lane >= at) & (lane < at + 4)
                west = f_ref[kind, 0, pl.ds(v * TILE, TILE), :]
                east = f_ref[kind, FIELD_TILES - 1, pl.ds(v * TILE, TILE), :]
                west_out = jnp.where(inside, turn(west, at, 1), west_out)
                east_out = jnp.where(inside, turn(east, at - last, 1), east_out)
        ca_ref[pl.ds(h * TILE, TILE), :] = jnp.where(east_even, east_out, west_out)
        cb_ref[pl.ds(h * TILE, TILE), :] = jnp.where(east_even, west_out, east_out)


def region_fields(meta, places, s, q, a, b, far, surface, after):
    return pl.pallas_call(
        field_kernel,
        in_specs=[SMEM, SMEM] + [VMEM] * 6 + [ANY],
        out_specs=[VMEM] * 3,
        out_shape=[
            jax.ShapeDtypeStruct((4, FIELD_TILES, FIELD_ROWS, LANES), F32),
            jax.ShapeDtypeStruct((24, LANES), F32),
            jax.ShapeDtypeStruct((24, LANES), F32),
        ],
        compiler_params=pltpu.CompilerParams(vmem_limit_bytes=12 << 20),
        name="region_fields",
    )(meta, places, s, q, a, b, far, surface, after)


def basis_kernel(meta, moved, f_ref, ca_ref, cb_ref, g_ref, blocks_ref, back_ref, u_ref):
    even = meta[0] % 2 == 0
    lane = lane_id((TILE, LANES))
    tiles = range(FIELD_TILES)
    fields = []
    for kind in range(4):
        parts = [f_ref[kind, b] for b in tiles]
        strip = []
        for v in range(FIELD_ROWS // TILE):
            g, h = v // 3, v % 3
            ca = ca_ref[pl.ds(h * TILE, TILE), :]
            cb = cb_ref[pl.ds(h * TILE, TILE), :]
            at = 16 * g + 4 * kind
            west = turn(jnp.where(even, cb, ca), 124 - at, 1)
            east = turn(jnp.where(even, ca, cb), 64 - at, 1)
            tile = f_ref[kind, FIELD_TILES - 1, pl.ds(v * TILE, TILE), :]
            tile = jnp.where((lane >= 64) & (lane < 68), east, tile)
            strip.append(jnp.where(lane >= 124, west, tile))
        parts[-1] = jnp.concatenate(strip, axis=0)
        fields.append(parts)
    depth, inner, mask, surf = fields
    wide = lane_id((FIELD_ROWS, LANES))

    def sides(v):
        fwd = [turn(x, 1, 1) for x in v]
        bwd = [turn(x, -1, 1) for x in v]
        out = []
        for b in tiles:
            left = jnp.where(wide == 0, fwd[b - 1], fwd[b])
            right = jnp.where(wide == LANES - 1, bwd[(b + 1) % FIELD_TILES], bwd[b])
            out.append(left + right)
        return out

    def rows(v):
        return [turn(x, 1, 0) + turn(x, -1, 0) for x in v]

    def spread(v):
        side = sides(v)
        both = rows([v[b] + 0.5 * side[b] for b in tiles])
        return [mask[b] * (side[b] + both[b]) for b in tiles]

    def edges(v):
        side, both = sides(v), rows(v)
        return [side[b] + both[b] for b in tiles]

    near, count = edges(inner), edges(mask)
    rhs = [mask[b] * (depth[b] + near[b] - count[b] * inner[b]) for b in tiles]
    scale = [1.0 / (6.0 + surf[b]) for b in tiles]
    u0 = [rhs[b] * scale[b] for b in tiles]
    z1 = spread(u0)
    u1 = [z1[b] * scale[b] for b in tiles]
    z2 = spread(u1)
    u2 = [z2[b] * scale[b] for b in tiles]
    z3 = spread(u2)
    rows_in = slice(TILE, FIELD_ROWS - TILE)

    def dot(x, y):
        total = jnp.zeros((TILE, LANES), F32)
        for b in tiles:
            p = x[b][rows_in] * y[b][rows_in]
            p = jnp.sum(p.reshape(-1, TILE, LANES), axis=0)
            if b == FIELD_TILES - 1:
                p = jnp.where(lane < 64, p, 0.0)
            total = total + p
        return jnp.sum(jnp.sum(total, axis=1, keepdims=True), axis=0, keepdims=True)

    row = jnp.zeros((1, LANES), F32)
    pairs = ((u0, rhs), (u0, z1), (u1, z1), (u1, z2), (u2, z2), (u2, z3))
    for k, (x, y) in enumerate(pairs):
        row = jnp.where(lane[:1] == k, dot(x, y), row)
    row = jnp.where(lane[:1] == 6, meta[3].astype(F32), row)
    g_ref[...] = jnp.broadcast_to(row, g_ref.shape)
    for k, u in enumerate((u0, u1, u2)):
        for b in tiles:
            u_ref[k, b] = u[b][rows_in]
    group = lane // BLOCK
    for k in range(3):
        for by in range(REG_Y):
            for b in tiles:
                value = [u_ref[k, b, pl.ds(BLOCK * by + q, TILE, stride=4), :] for q in range(4)]
                for g in range(4):
                    if 4 * b + g >= REG_X:
                        continue
                    tile = value[0]
                    for q in range(4):
                        part = turn(value[q], BLOCK * (q - g), 1)
                        tile = part if q == 0 else jnp.where(group == q, part, tile)
                    blocks_ref[pl.ds((k * REGION + by * REG_X + 4 * b + g) * TILE, TILE), :] = tile
    for m in range(MOVED):
        at = pl.multiple_of(jnp.maximum(moved[m], 0) * TILE, TILE)
        for k in range(3):
            tile = blocks_ref[pl.ds(k * REGION * TILE + at, TILE), :]
            back_ref[pl.ds((k * MOVED + m) * TILE, TILE), :] = tile


def solve_basis(meta, moved, fields, ca, cb, devices):
    return pl.pallas_call(
        basis_kernel,
        in_specs=[SMEM, SMEM, VMEM, VMEM, VMEM],
        out_specs=[VMEM] * 3,
        out_shape=[
            jax.ShapeDtypeStruct((devices, LANES), F32),
            jax.ShapeDtypeStruct((3 * REGION * TILE, LANES), F32),
            jax.ShapeDtypeStruct((3 * MOVED * TILE, LANES), F32),
        ],
        scratch_shapes=[pltpu.VMEM((3, FIELD_TILES, FIELD_ROWS - 2 * TILE, LANES), F32)],
        compiler_params=pltpu.CompilerParams(vmem_limit_bytes=24 << 20),
        name="solve_basis",
    )(meta, moved, fields, ca, cb)


def pressure_kernel(code, g_ref, blocks_ref, back_ref, held_ref, out_ref, same_ref, work):
    del held_ref, same_ref
    slots = out_ref.shape[0]
    total = jnp.sum(g_ref[...].reshape(-1, TILE, LANES), axis=0)
    total = jnp.broadcast_to(jnp.sum(total, axis=0, keepdims=True), (TILE, LANES))
    lane = lane_id((TILE, LANES))
    pick = lambda k: jnp.sum(jnp.where(lane == k, total, 0.0), axis=1, keepdims=True)
    g = [pick(k) for k in range(6)]
    g = [x / g[0] for x in g]
    a = [g[k] - g[k + 1] for k in range(5)]
    zero = jnp.zeros_like(g[0])
    one = zero + 1.0

    def form(v, m):
        out = zero
        for i in range(3):
            for k in range(3):
                out = out + v[i] * v[k] * m[i + k]
        return out

    coef = [zero, zero, zero]
    rho = [one, zero, zero]
    way = [one, zero, zero]
    norm = g[0]
    for iteration in range(ITERS):
        length = norm / form(way, a)
        coef = [coef[k] + length * way[k] for k in range(3)]
        if iteration + 1 < ITERS:
            moved = [way[0], way[1] - way[0], way[2] - way[1]]
            rho = [rho[k] - length * moved[k] for k in range(3)]
            norm_next = form(rho, g)
            way = [rho[k] + (norm_next / norm) * way[k] for k in range(3)]
            norm = norm_next
    coef = [jnp.broadcast_to(c, (TILE, LANES)) for c in coef]
    for s in range(slots):
        c = code[s]
        at = pl.multiple_of(jnp.where(c < REGION, c, 0) * TILE, TILE)
        tiles = [blocks_ref[pl.ds(k * REGION * TILE + at, TILE), :] for k in range(3)]
        m = s - (slots - MOVED)
        if m >= 0:
            for k in range(3):
                other = back_ref[pl.ds((k * MOVED + m) * TILE, TILE), :]
                tiles[k] = jnp.where(c < REGION, tiles[k], other)
        work[pl.ds(s * TILE, TILE), :] = coef[0] * tiles[0] + coef[1] * tiles[1] + coef[2] * tiles[2]
    for first in range(0, slots, TILE):
        size = min(TILE, slots - first)
        for c in range(TILE):
            lines = work[pl.ds(first * TILE + c, size, stride=TILE), :]
            out_ref[pl.ds(first, size), pl.ds(c * LANES, LANES)] = lines


def slot_pressure(code, sums, blocks, back, held):
    slots = code.shape[0]
    return pl.pallas_call(
        pressure_kernel,
        in_specs=[SMEM, VMEM, VMEM, VMEM, ANY],
        out_specs=[VMEM, ANY],
        out_shape=[
            jax.ShapeDtypeStruct((slots, TILE * LANES), F32),
            jax.ShapeDtypeStruct(held.shape, F32),
        ],
        scratch_shapes=[pltpu.VMEM((slots * TILE, LANES), F32)],
        input_output_aliases={4: 1},
        compiler_params=pltpu.CompilerParams(vmem_limit_bytes=12 << 20),
        name="slot_pressure",
    )(code, sums, blocks, back, held)


def columns_kernel(meta, inv, t_ref, after_ref, a_ref, b_ref, west, east, sems):
    del after_ref
    even = meta[0] % 2 == 0
    count = 2 * REG_Y

    def copies(k):
        w, e = inv[REG_X * k], inv[REG_X * k + REG_X - 1]
        cw = pltpu.make_async_copy(t_ref.at[jnp.maximum(w, 0)], west.at[k], sems.at[0, k])
        ce = pltpu.make_async_copy(t_ref.at[jnp.maximum(e, 0)], east.at[k], sems.at[1, k])
        return cw, ce

    for k in range(count):
        for c in copies(k):
            c.start()
    column = lane_id((ROWS, LANES)) % BLOCK
    for first in (0, REG_Y):
        for k in range(first, first + REG_Y):
            for c in copies(k):
                c.wait()
        for level in range(HALF):
            at = pl.ds(level * ROWS, ROWS)
            if first:
                out_a, out_b = a_ref[at, :], b_ref[at, :]
                out_w, out_e = jnp.where(even, out_b, out_a), jnp.where(even, out_a, out_b)
            else:
                out_w = out_e = jnp.zeros((ROWS, LANES), F32)
            for k in range(first, first + REG_Y):
                has_w, has_e = inv[REG_X * k] >= 0, inv[REG_X * k + REG_X - 1] >= 0
                for part in range(2):
                    lane = k + 16 * part
                    here = column == lane
                    x = pl.ds((level + HALF * part) * ROWS, ROWS)
                    out_w = jnp.where(here & has_w, turn(west[k, x, :], lane, 1), out_w)
                    out_e = jnp.where(here & has_e, turn(east[k, x, :], lane - (BLOCK - 1), 1), out_e)
            a_ref[at, :] = jnp.where(even, out_e, out_w)
            b_ref[at, :] = jnp.where(even, out_w, out_e)


def column_strips(meta, places, view, after):
    count = 2 * REG_Y
    return pl.pallas_call(
        columns_kernel,
        in_specs=[SMEM, SMEM, HBM, ANY],
        out_specs=[VMEM] * 2,
        out_shape=[jax.ShapeDtypeStruct((HALF * ROWS, LANES), F32)] * 2,
        scratch_shapes=[
            pltpu.VMEM((count, IMAGE, LANES), F32),
            pltpu.VMEM((count, IMAGE, LANES), F32),
            pltpu.SemaphoreType.DMA((2, count)),
        ],
        compiler_params=pltpu.CompilerParams(vmem_limit_bytes=52 << 20),
        cost_estimate=pl.CostEstimate(flops=1, bytes_accessed=1, transcendentals=0),
        name="column_strips",
    )(meta, places, view.reshape(view.shape[0], IMAGE, LANES), after)


def lines_kernel(meta, table, t_ref, after_ref, a_ref, b_ref, half, sems):
    del after_ref
    even = meta[1] % 2 == 0
    links = [[jnp.maximum(table[way * (CAP_WE + CAP_NS) + CAP_WE + k], 2) for k in range(CAP_NS)] for way in range(2)]

    def copy(way, k):
        link = links[way][k]
        rows = pl.ds(pl.multiple_of((link % 4 - 2) * TILE, TILE), TILE)
        dest = half.at[way, k, :, pl.ds(TILE, TILE), :]
        return pltpu.make_async_copy(t_ref.at[link // 4, :, rows, :], dest, sems.at[way, k])

    for way in range(2):
        for k in range(CAP_NS):
            copy(way, k).start()
    place = lax.broadcasted_iota(jnp.int32, (TILE, LANES), 0) // 2 * 4 + lane_id((TILE, LANES)) // BLOCK
    values = []
    for way in range(2):
        first = [TILE + 6 * (links[way][k] % 4 - 2) - 2 * (k // 4) for k in range(CAP_NS)]
        by = [(BLOCK * (k % 4) + BLOCK * (links[way][k] % 4 - 2)) % LANES for k in range(CAP_NS)]
        for k in range(CAP_NS):
            copy(way, k).wait()
        for level in range(LEVELS):
            value = jnp.zeros((TILE, LANES), F32)
            for k in range(CAP_NS):
                x = pltpu.roll(half[way, k, level, pl.ds(first[k], TILE), :], by[k], 1)
                value = jnp.where(place == k, x, value)
            at = pl.ds(level * TILE, TILE)
            if way == 0:
                a_ref[at, :] = value
            else:
                other = a_ref[at, :]
                a_ref[at, :] = jnp.where(even, other, value)
                b_ref[at, :] = jnp.where(even, value, other)


def line_strips(meta, table, view, after):
    return pl.pallas_call(
        lines_kernel,
        in_specs=[SMEM, SMEM, HBM, ANY],
        out_specs=[VMEM] * 2,
        out_shape=[jax.ShapeDtypeStruct((LEVELS * TILE, LANES), F32)] * 2,
        scratch_shapes=[
            pltpu.VMEM((2, CAP_NS, LEVELS, 3 * TILE, LANES), F32),
            pltpu.SemaphoreType.DMA((2, CAP_NS)),
        ],
        compiler_params=pltpu.CompilerParams(vmem_limit_bytes=52 << 20),
        name="line_strips",
    )(meta, table, view, after)


def links_kernel(meta, table, t_ref, ga_ref, gb_ref, na_ref, nb_ref, a_ref, b_ref, whole, sems):
    even_x = meta[0] % 2 == 0
    even_y = meta[1] % 2 == 0

    def copy(way, k):
        link = jnp.maximum(table[way * (CAP_WE + CAP_NS) + k], 0)
        return pltpu.make_async_copy(t_ref.at[link // 4], whole.at[way, k], sems.at[way, k])

    for way in range(2):
        for k in range(CAP_WE):
            @pl.when(table[way * (CAP_WE + CAP_NS) + k] >= 0)
            def _():
                copy(way, k).start()

    column = lane_id((HALF * ROWS, LANES)) % 16
    from_west = jnp.where(even_x, gb_ref[...], ga_ref[...])
    from_east = jnp.where(even_x, ga_ref[...], gb_ref[...])
    ways = ((turn(from_west, -5, 1), from_east), (from_west, turn(from_east, 5, 1)))
    relays = [jnp.where(column < 5, w, jnp.where(column < RELAY, e, 0.0)) for w, e in ways]
    for out, lines in ((a_ref, na_ref), (b_ref, nb_ref)):
        out[pl.ds(HALF * ROWS, LEVELS * TILE), :] = lines[...]
        out[pl.ds(HALF * ROWS + LEVELS * TILE, TILE), :] = jnp.zeros((TILE, LANES), F32)

    def message(way, out):
        out[pl.ds(0, HALF * ROWS), :] = relays[way]
        lane32 = lane_id((ROWS, LANES)) % BLOCK
        for k in range(CAP_WE):
            link = table[way * (CAP_WE + CAP_NS) + k]

            @pl.when(link >= 0)
            def _():
                copy(way, k).wait()
                start = (link % 4) * (BLOCK - 1)
                for level in range(HALF):
                    at = pl.ds(level * ROWS, ROWS)
                    value = out[at, :]
                    for part in range(2):
                        lane = RELAY + k + 16 * part
                        x = turn(whole[way, k, level + HALF * part], lane, 1)
                        x = jnp.where(start > 0, turn(x, 1 - BLOCK, 1), x)
                        value = jnp.where(lane32 == lane, x, value)
                    out[at, :] = value

    @pl.when(even_y)
    def _():
        message(0, a_ref)
        message(1, b_ref)

    @pl.when(jnp.logical_not(even_y))
    def _():
        message(0, b_ref)
        message(1, a_ref)


def link_strips(meta, table, view, ga, gb, na, nb):
    return pl.pallas_call(
        links_kernel,
        in_specs=[SMEM, SMEM, HBM] + [VMEM] * 4,
        out_specs=[VMEM] * 2,
        out_shape=[jax.ShapeDtypeStruct((LINK_ROWS, LANES), F32)] * 2,
        scratch_shapes=[
            pltpu.VMEM((2, CAP_WE, LEVELS, ROWS, LANES), F32),
            pltpu.SemaphoreType.DMA((2, CAP_WE)),
        ],
        compiler_params=pltpu.CompilerParams(vmem_limit_bytes=52 << 20),
        name="link_strips",
    )(meta, table, view, ga, gb, na, nb)


BOX_LOW = 2 * HALF * ROWS
BOX_HIGH = BOX_LOW + LINK_ROWS
BOX = BOX_HIGH + LINK_ROWS


def tracer_kernel(meta, table, need, diffusion, t_ref, ga_ref, gb_ref, ha_ref, hb_ref, out_ref, own, inner, across, beside, box, perm, sems, out_sems):
    slots = own.shape[0]
    chunks = slots // STEP_SLOTS

    def fetch(c):
        part = pl.ds(c * STEP_SLOTS, STEP_SLOTS)
        return pltpu.make_async_copy(t_ref.at[part], own.at[part], sems.at[c])

    def keep(c):
        part = pl.ds(c * STEP_SLOTS, STEP_SLOTS)
        return pltpu.make_async_copy(own.at[part], out_ref.at[part], out_sems.at[c])

    for c in range(chunks):
        fetch(c).start()
    even_x = meta[0] % 2 == 0
    even_y = meta[1] % 2 == 0
    src = lax.broadcasted_iota(jnp.int32, perm.shape, 0) % LANES
    dst = lax.broadcasted_iota(jnp.int32, perm.shape, 1)
    to = dst % LANES
    gap = jnp.abs(src - to)
    linked = ((gap == 1) & (src // BLOCK == to // BLOCK)) | (gap == BLOCK)
    crossed = gap == LANES - BLOCK
    swapped = (gap == BLOCK - 1) & (src // BLOCK == to // BLOCK)
    hit = ((dst < LANES) & linked) | ((dst >= LANES) & (dst < 2 * LANES) & crossed) | ((dst >= 2 * LANES) & swapped)
    perm[...] = jnp.where(hit, 1.0, 0.0).astype(jnp.bfloat16)
    across[slots] = jnp.zeros(across.shape[1:], F32)
    beside[slots] = jnp.zeros(beside.shape[1:], F32)
    for first, second, size, low, high in (
        (ga_ref, gb_ref, HALF * ROWS, 0, HALF * ROWS),
        (ha_ref, hb_ref, LINK_ROWS, BOX_LOW, BOX_HIGH),
    ):
        even = even_x if low == 0 else even_y
        box[pl.ds(low, size), :] = jnp.where(even, second[...], first[...])
        box[pl.ds(high, size), :] = jnp.where(even, first[...], second[...])

    cells = (ROWS, LANES)
    lane = lane_id(cells)
    column = lane % BLOCK
    row = lax.broadcasted_iota(jnp.int32, cells, 0)
    row8, lane8 = row[:TILE], lane[:TILE]
    outer = (lane8 < BLOCK) | (lane8 >= LANES - BLOCK)
    for way, low in enumerate((BOX_LOW, BOX_HIGH)):
        for level in range(LEVELS):
            x = box[pl.ds(low + HALF * ROWS + level * TILE, TILE), :]
            for d in range(4):
                y = jnp.where(outer, turn(x, BLOCK * d, 1), 0.0)
                across[slots + 1 + 4 * way + d, pl.ds(TILE + level * ROWS, TILE), :] = y
    for level in range(LEVELS):
        part = level // HALF
        w = box[pl.ds((level % HALF) * ROWS, ROWS), :]
        e = box[pl.ds((HALF + level % HALF) * ROWS, ROWS), :]
        for k in range(2 * REG_Y):
            y = jnp.where(column == BLOCK - 1, turn(e, BLOCK - 1 - k - 16 * part, 1), 0.0)
            y = jnp.where(column == 0, turn(w, -k - 16 * part, 1), y)
            beside[slots + 1 + k, pl.ds(level * ROWS, ROWS), :] = y

    def arrive(c, carry):
        fetch(c).wait()
        for n in range(STEP_SLOTS):
            s = c * STEP_SLOTS + n
            x = own[s]
            high = x.astype(jnp.bfloat16)
            low = (x - high.astype(F32)).astype(jnp.bfloat16)
            pair = jnp.concatenate([high, low], axis=1)
            moved = jnp.dot(pair, perm[...], preferred_element_type=F32)
            inner[s] = moved[:, :LANES]
            across[s, pl.ds(TILE, IMAGE), :] = moved[:, LANES : 2 * LANES]
            beside[s] = moved[:, 2 * LANES :]
        return carry

    edge = (
        jnp.where(column == 0, 1.0, 0.0),
        jnp.where(column == BLOCK - 1, 1.0, 0.0),
        jnp.where((row < 2) & (lane < BLOCK), 1.0, 0.0),
        jnp.where((row >= ROWS - 2) & (lane >= LANES - BLOCK), 1.0, 0.0),
    )

    def unpack(n, s):
        for t in range(2):
            at = s * 4 + t

            @pl.when(table[1, at] == 1)
            def _():
                first, by = pl.multiple_of(table[2, at], TILE), table[3, at]
                for level in range(LEVELS):
                    part = level // HALF
                    x = box[pl.ds(first + (level % HALF) * ROWS, ROWS), :]
                    x = pltpu.roll(x, (by + LANES - 16 * part) % LANES, 1)
                    x = jnp.where(column == t * (BLOCK - 1), x, 0.0)
                    beside[slots + 11 + 2 * n + t, pl.ds(level * ROWS, ROWS), :] = x

    def step(n, s):
        count = jnp.full(cells, 4.0, F32)
        for t in range(4):
            count = count - edge[t] * table[4, s * 4 + t].astype(F32)
        west, east, south, north = [table[0, s * 4 + t] for t in range(4)]
        south_at, north_at = TILE + table[2, s * 4 + 2], TILE + table[2, s * 4 + 3]
        for level in range(LEVELS):
            for h in range(2):
                at = level * ROWS + h * TILE
                x = own[s, pl.ds(at, TILE), :]
                under = across[s, pl.ds(TILE + at - 2, TILE), :]
                over = across[s, pl.ds(TILE + at + 2, TILE), :]
                if h == 0:
                    under = jnp.where(row8 < 2, across[south, pl.ds(south_at + level * ROWS, TILE), :], under)
                else:
                    over = jnp.where(row8 >= TILE - 2, across[north, pl.ds(north_at + level * ROWS, TILE), :], over)
                total = inner[s, pl.ds(at, TILE), :] + jnp.where(lane8 < LANES // 2, under, over)
                w, e = beside[west, pl.ds(at, TILE), :], beside[east, pl.ds(at, TILE), :]
                total = total + jnp.where(lane8 % BLOCK == 0, w, jnp.where(lane8 % BLOCK == BLOCK - 1, e, 0.0))
                part = count[h * TILE : (h + 1) * TILE]
                own[s, pl.ds(at, TILE), :] = x + diffusion[level] * (total - part * x)

    def work(c, seen):
        upto = jnp.maximum(seen, need[c] + 1)
        lax.fori_loop(seen, upto, arrive, 0)
        for n in range(STEP_SLOTS):
            unpack(n, c * STEP_SLOTS + n)
        for n in range(STEP_SLOTS):
            step(n, c * STEP_SLOTS + n)
        keep(c).start()
        return upto

    lax.fori_loop(0, chunks, work, 0)
    for c in range(chunks):
        keep(c).wait()


def step_tracers(meta, table, need, diffusion, view, ga, gb, ha, hb):
    slots = view.shape[0]
    chunks = slots // STEP_SLOTS
    size = slots * IMAGE * LANES
    out = pl.pallas_call(
        tracer_kernel,
        in_specs=[SMEM] * 4 + [HBM] + [VMEM] * 4,
        out_specs=HBM,
        out_shape=jax.ShapeDtypeStruct((slots, IMAGE, LANES), F32),
        scratch_shapes=[
            pltpu.VMEM((slots, IMAGE, LANES), F32),
            pltpu.VMEM((slots, IMAGE, LANES), F32),
            pltpu.VMEM((slots + 9, IMAGE + 2 * TILE, LANES), F32),
            pltpu.VMEM((slots + 11 + 2 * STEP_SLOTS, IMAGE, LANES), F32),
            pltpu.VMEM((BOX, LANES), F32),
            pltpu.VMEM((2 * LANES, 3 * LANES), jnp.bfloat16),
            pltpu.SemaphoreType.DMA((chunks,)),
            pltpu.SemaphoreType.DMA((chunks,)),
        ],
        compiler_params=pltpu.CompilerParams(vmem_limit_bytes=52 << 20),
        cost_estimate=pl.CostEstimate(flops=14 * size, bytes_accessed=8 * size, transcendentals=0),
        name="step_tracers",
    )(meta, table, need, diffusion, view.reshape(slots, IMAGE, LANES), ga, gb, ha, hb)
    return out.reshape(view.shape)


def with_halo(block, sides, width):
    for axis, dim in sides:
        low = shifted(lax.slice_in_dim(block, block.shape[dim] - width, None, axis=dim), axis, 1)
        high = shifted(lax.slice_in_dim(block, 0, width, axis=dim), axis, -1)
        block = jnp.concatenate([low, block, high], axis=dim)
    return block


def edge_strips(grid):
    sides = [grid[..., :, 0], grid[..., :, -1], grid[..., 0, :], grid[..., -1, :]]
    return jnp.stack(sides, axis=1).reshape(grid.shape[0] * 4, -1)


def general_step(tracers, diffusion, halo_source):
    slots = tracers.shape[0]
    grid = tracers.reshape(slots, TRACER, LEVELS, BLOCK, BLOCK)
    strips = edge_strips(grid)
    width = strips.shape[1]
    count_gx, count_gy = lax.axis_size("gx"), lax.axis_size("gy")
    source = halo_source.reshape(-1)
    missing = source >= 4 * slots * count_gx * count_gy
    slot = jnp.where(missing, 0, source) // 4
    owner = slot // slots
    step_gx = (owner // count_gy - lax.axis_index("gx") + count_gx + 1) % count_gx
    step_gy = (owner % count_gy - lax.axis_index("gy") + count_gy + 1) % count_gy
    every = slots * 4
    table = with_halo(strips.reshape(1, 1, every, width), (("gx", 0), ("gy", 1)), 1).reshape(9 * every, width)
    index = (step_gx * 3 + step_gy) * every + slot % slots * 4 + source % 4
    halo = jnp.take(table, jnp.where(missing, 0, index), axis=0, mode="clip")
    halo = halo.reshape(slots, 4, TRACER, LEVELS, BLOCK)
    gate = jnp.where(missing, 0.0, 1.0).astype(F32).reshape(slots, 4, 1, 1, 1)
    inner_x = grid[..., :, :-1] - grid[..., :, 1:]
    inner_y = grid[..., :-1, :] - grid[..., 1:, :]
    west = (halo[:, 0] - grid[..., :, 0]) * gate[:, 0]
    east = (halo[:, 1] - grid[..., :, -1]) * gate[:, 1]
    south = (halo[:, 2] - grid[..., 0, :]) * gate[:, 2]
    north = (halo[:, 3] - grid[..., -1, :]) * gate[:, 3]
    laplace = (
        jnp.concatenate([west[..., None], inner_x], axis=-1)
        + jnp.concatenate([-inner_x, east[..., None]], axis=-1)
        + jnp.concatenate([south[..., None, :], inner_y], axis=-2)
        + jnp.concatenate([-inner_y, north[..., None, :]], axis=-2)
    )
    updated = grid + diffusion[None, None, :, None, None] * laplace
    return plain(seen_by_rows(updated.reshape(tracers.shape)))


def strip_tables(halo_source, code, at_x, at_y, count_x, count_y):
    slots = halo_source.shape[0]
    source = halo_source.reshape(-1)
    missing = source >= 4 * slots * count_x * count_y
    source = jnp.where(missing, 0, source)
    owner = source // (4 * slots)
    local_slot = source // 4 - owner * slots
    same_x = owner // count_y == at_x
    owner_y = owner % count_y
    up = owner_y == (at_y + 1) % count_y
    here = owner_y == at_y
    index = jnp.arange(4 * slots, dtype=jnp.int32)
    side = index % 4
    kind = jnp.where(side >= 2, 1, 0)
    linked = ~missing & same_x & ~here
    group = jnp.where(linked, jnp.where(up, kind, 2 + kind), -1)

    def rank(key):
        before = (key[None, :] < key[:, None]) & (group[None, :] == group[:, None])
        return jnp.sum(before.astype(jnp.int32), axis=1)

    take = rank(index)
    give = rank(source)
    entry = jnp.arange(2 * (CAP_WE + CAP_NS), dtype=jnp.int32)
    rest = entry % (CAP_WE + CAP_NS)
    of_kind = jnp.where(rest >= CAP_WE, 1, 0)
    want = (2 * (entry // (CAP_WE + CAP_NS)) + of_kind) * 1024 + rest - CAP_WE * of_kind
    has = jnp.where(group >= 0, group * 1024 + give, -1)
    send = jnp.sum(jnp.where(want[:, None] == has[None, :], index[None, :] + 1, 0), axis=1) - 1
    over = jnp.any(linked & (take >= jnp.where(kind == 1, CAP_NS, CAP_WE)))
    row = jnp.broadcast_to((code // REG_X)[:, None], (slots, 4)).reshape(-1)
    local = same_x & here
    north = kind == 1
    lane = jnp.where(same_x, RELAY + take, row % REG_Y + jnp.where(side == 0, 0, REG_Y))
    box = jnp.where(up, BOX_HIGH, BOX_LOW)
    by = (jnp.where(side == 0, 0, BLOCK - 1) - lane) % LANES
    unpacked = slots + 11 + 2 * (index // 4 % STEP_SLOTS) + side
    image_we = jnp.where(local, local_slot, jnp.where(here, slots + 1 + row, unpacked))
    take = jnp.minimum(take, CAP_NS - 1)
    turns = jnp.where(side == 2, -take, 3 - take) % 4
    image_ns = jnp.where(local, local_slot, slots + 1 + jnp.where(up, 4, 0) + turns)
    row_ns = jnp.where(local | missing, jnp.where(side == 2, ROWS - 2, 0), 2 * (take // 4))
    row_ns = row_ns - jnp.where(side == 3, TILE - 2, 0)
    image = jnp.where(missing, slots, jnp.where(north, image_ns, image_we))
    unpack = jnp.where(missing | here | north, 0, 1)
    table = jnp.stack([image, unpack, jnp.where(north, row_ns, box), by, jnp.where(missing, 1, 0)])
    last = jnp.where(local & ~missing, local_slot, 0).reshape(-1, 4 * STEP_SLOTS)
    need = jnp.maximum(jnp.max(last, axis=1) // STEP_SLOTS, jnp.arange(slots // STEP_SLOTS))
    return table, need, send, over.astype(jnp.int32)


def on_device(tracers, diffusion, layer_weight, surface_term, clinic_blocks, halo_source):
    slots = tracers.shape[0]
    count_x, count_y = lax.axis_size("gx"), lax.axis_size("gy")
    at_x, at_y = lax.axis_index("gx"), lax.axis_index("gy")
    grid_columns = REG_X * count_x
    grid_rows = REG_Y * count_y
    own_row = (clinic_blocks // grid_columns - REG_Y * at_y) % grid_rows
    code = own_row * REG_X + clinic_blocks % grid_columns % REG_X
    zero = jnp.zeros((), jnp.int32)
    meta = jnp.stack([at_x, at_y, zero + count_y, zero]).astype(jnp.int32)

    view = seen_by_rows(tracers)
    s, q, a, b, far, places = depth_sums(view, meta, code, layer_weight, diffusion, surface_term)
    ra, rb = swap(a, b, "gy", count_y)
    rfar = shifted(far, "gy", 2)

    source, places = lax.optimization_barrier((halo_source, places))
    table, need, send, over = strip_tables(source, code, at_x, at_y, count_x, count_y)
    columns = column_strips(meta, places, view, rfar)
    ga, gb = swap(*columns, "gx", count_x)
    na, nb = line_strips(meta, send, view, columns[0])

    moved = jnp.where(at_y % 2 == 0, rb[IDS, :MOVED], ra[IDS, :MOVED]).astype(jnp.int32)
    spot = jnp.arange(2 * REGION, dtype=jnp.int32)[:, None]
    index = jnp.arange(MOVED, dtype=jnp.int32)[None, :]
    both = places + jnp.sum(jnp.where(moved[None, :] == spot, index + 1 + slots, 0), axis=1)
    fields, ca, cb = region_fields(meta, both, s, q, ra, rb, rfar, surface_term, na)
    ca, cb = swap(ca, cb, "gx", count_x)
    ha, hb = swap(*link_strips(meta, send, view, ga, gb, na, nb), "gy", count_y)

    meta_over = jnp.stack([at_x, at_y, zero + count_y, over]).astype(jnp.int32)
    sums, blocks, back = solve_basis(meta_over, moved, fields, ca, cb, count_x * count_y)
    back = shifted(back, "gy", -1)
    sums = lax.all_to_all(sums[:, None], ("gx", "gy"), 0, 0, tiled=True)
    updated = step_tracers(meta, table, need, diffusion, view, ga, gb, ha, hb)
    sums, updated = lax.optimization_barrier((sums, updated))
    updated = lax.cond(
        jnp.max(sums[:, 0, 6]) > 0.0,
        lambda fast: general_step(tracers, diffusion, halo_source),
        lambda fast: fast,
        updated,
    )
    pressure, updated = slot_pressure(code, sums.reshape(-1, LANES), blocks, back, updated)
    updated = updated.reshape(slots, LEVELS, TILE, TRACER, LANES).transpose(0, 3, 1, 2, 4)
    return (updated.reshape(tracers.shape), pressure)


def solution(mesh):
    placed = (
        P(("gx", "gy"), None, None, None),
        P(),
        P(),
        P("gy", "gx"),
        P(("gx", "gy")),
        P(("gx", "gy"), None),
    )
    return jax.shard_map(
        on_device,
        mesh=mesh,
        in_specs=placed,
        out_specs=(P(("gx", "gy"), None, None, None), P(("gx", "gy"), None)),
        check_vma=False,
    )
```
